128 devices in a mesh: dp: 4 (over z_lo, core), tm: 32 (over y, x, z_hi).
Axes of the slice: x: 4, y: 4, z: 4 (z_hi: 2, z_lo: 2; z = z_hi * 2 + z_lo), core: 2. Of those that a mesh axis runs over, the one named last changes fastest.
Arguments:
- noisy: bfloat16 [4, 32, 2, 128, 2048], P('dp', 'tm'), may hold values from -6 to 6
- clean: bfloat16 [4, 32, 128, 2048], P('dp', 'tm'), may hold values from -6 to 6
- actions: int32 [4, 32], P('dp', 'tm'), may hold values from 0 to 17
- levels: int32 [4, 32, 2], P('dp', 'tm'), may hold values from 1 to 63
- starts: int32 [4, 32], P('dp', 'tm'), may hold values from 0 to 31, as said below
- w_qkv: bfloat16 [2048, 3, 1024], replicated, may hold values from -1 to 1
- w_out: bfloat16 [1024, 2048], replicated, may hold values from -0.1875 to 0.1875
- noise_table: float32 [64, 3, 2048], replicated, may hold values from -3 to 3
- action_table: float32 [18, 3, 2048], replicated, may hold values from -3 to 3
- temps: float32 [8], replicated, may hold values from 0.5 to 16
- out_grad: bfloat16 [4, 32, 2, 128, 2048], P('dp', 'tm'), may hold values from -6 to 6
Outputs:
- grad_noisy: bfloat16 [4, 32, 2, 128, 2048], P('dp', 'tm')
- grad_qkv: bfloat16 [2048, 3, 1024], P('tm', None, 'dp')
- grad_out: bfloat16 [1024, 2048], P('tm', 'dp')
The draws below stay inside these ranges and needn't reach their ends.
Inputs may be any that keep to these rules, and one draw needn't show every extreme that they name: starts of frame g is at most g; the last frame of rollout 0 has no clean context.
All inputs are finite; a program needn't handle non-finite values.
Results may differ from the reference program's by a relative error of at most 0.035.
Values may be sent and summed in bfloat16 or wider, within the bound.
A program may use at most 192 MiB of HBM per device.

```python
import math
import jax
import jax.numpy as jnp
from jax import lax

D = 2048
HEADS = 8
HD = 128
HH = 1024
TOKF = 128
F_DEV = 1
LEVELS = 64
ACTIONS = 18
FRAMES = 32
ROLLS = 4
N_DP = 4
N_TM = 32


def draw_starts(key, part):
    key = jax.random.fold_in(key, 11)
    upper = jnp.broadcast_to(jnp.arange(FRAMES, dtype=jnp.int32) + 1, (ROLLS, FRAMES))
    picks = jax.random.randint(key, (ROLLS, FRAMES), 0, upper)
    return picks.at[0, FRAMES - 1].set(FRAMES - 1).astype(jnp.int32)


def draw_temps(key, part):
    key = jax.random.fold_in(key, 23)
    spread = jax.random.uniform(key, (HEADS,), jnp.float32, jnp.log(0.5), jnp.log(4.0))
    values = jnp.exp(spread)
    return values.astype(jnp.float32)


def draw_noisy(key, part):
    key = jax.random.fold_in(key, 5)
    values = jnp.clip(jax.random.normal(key, (ROLLS, FRAMES, 2, TOKF, D), jnp.float32), -6.0, 6.0)
    return values.astype(jnp.bfloat16)


def draw_noise_table(key, part):
    key = jax.random.fold_in(key, 7)
    values = jnp.clip(0.5 * jax.random.normal(key, (LEVELS, 3, D), jnp.float32), -3.0, 3.0)
    return values.astype(jnp.float32)


def draw_w_qkv(key, part):
    key = jax.random.fold_in(key, 17)
    width = HEADS * HD
    values = jnp.clip(jax.random.normal(key, (D, 3, width), jnp.float32), -3.0, 3.0)
    return (values * D ** (-0.5)).astype(jnp.bfloat16)


def with_ends(values, key, least, largest):
    longest = values.shape.index(max(values.shape))
    spots = []
    for shift in (0, 1):
        where = [jax.random.randint(jax.random.fold_in(key, axis), (), 0, length) for axis, length in enumerate(values.shape)]
        where[longest] = (where[longest] + shift) % values.shape[longest]
        spots.append(tuple(where))
    return values.at[spots[0]].set(least).at[spots[1]].set(largest)


def steps_of(own_key, shape, cuts, smallest, top_value):
    def one(position, blocks):
        steps = jax.random.uniform(jax.random.fold_in(jax.random.fold_in(own_key, 6), position), (blocks,), jnp.float32, smallest / len(cuts), top_value / len(cuts))
        return jnp.repeat(jnp.exp(steps), shape[position] // blocks).reshape((-1,) + (1,) * (len(shape) - position - 1))

    loudness = one(*cuts[0])
    for cut in cuts[1:]:
        loudness = loudness * one(*cut)
    return loudness


def normal_values(stream_key, shape, scale, reach, shards=(), kind=jnp.bfloat16):
    drawn = scale * jax.random.normal(stream_key, shape, jnp.float32)
    if shards:
        drawn = drawn * steps_of(stream_key, shape, shards, -0.22, 0.18)
    return jnp.clip(drawn, -reach, reach).astype(kind)


def setup_inputs(seed: int = 0) -> dict:
    seeds = jax.random.split(jax.random.key(seed), 12)
    noisy = draw_noisy(jax.random.fold_in(seeds[11], 71), 0)
    clean = normal_values(seeds[1], (ROLLS, FRAMES, TOKF, D), 1.0, 6.0, ((0, 4), (1, 32)))
    actions = with_ends(jax.random.randint(seeds[2], (ROLLS, FRAMES), 0, ACTIONS), jax.random.fold_in(seeds[2], 1), 0, ACTIONS - 1).astype(jnp.int32)
    levels = with_ends(jax.random.randint(seeds[3], (ROLLS, FRAMES, 2), 1, LEVELS), jax.random.fold_in(seeds[3], 1), 1, LEVELS - 1).astype(jnp.int32)
    starts = draw_starts(jax.random.fold_in(seeds[11], 71), 0)
    w_qkv = draw_w_qkv(jax.random.fold_in(seeds[11], 71), 0)
    w_out = normal_values(seeds[6], (HH, D), HH ** -0.5, 0.1875)
    noise_table = draw_noise_table(jax.random.fold_in(seeds[11], 71), 0)
    action_table = normal_values(seeds[8], (ACTIONS, 3, D), 0.5, 3.0, (), jnp.float32)
    temps = draw_temps(jax.random.fold_in(seeds[11], 71), 0)
    out_grad = normal_values(seeds[10], (ROLLS, FRAMES, 2, TOKF, D), 1.0, 6.0, ((0, 4), (1, 32)))
    return dict(noisy=noisy, clean=clean, actions=actions, levels=levels, starts=starts, w_qkv=w_qkv, w_out=w_out, noise_table=noise_table, action_table=action_table, temps=temps, out_grad=out_grad)


EPS = 1e-06
NEG = -1e+30

def layer_norm(values):
    center = values - lax.optimization_barrier(jnp.mean(values, axis=-1, keepdims=True))
    return center * lax.rsqrt(lax.optimization_barrier(jnp.mean(center * center, axis=-1, keepdims=True)) + EPS)

def head_norm(values, heads):
    count = values.shape[0]
    split = values.reshape(count, heads, -1)
    factor = lax.rsqrt(lax.optimization_barrier(jnp.mean(split * split, axis=-1, keepdims=True)) + EPS)
    return (split * factor).reshape(count, -1)

def contract(left, right, left_dim, right_dim):
    return lax.dot_general(left, right, (((left_dim,), (right_dim,)), ((), ())), preferred_element_type=jnp.float32)

def modulate(values, shift, scale):
    return (layer_norm(values) * (1.0 + scale) + shift).astype(jnp.bfloat16)

def attend(query, key_own, value_own, ctx_keys, ctx_vals, own_mask, ctx_mask, temps, heads):
    count = query.shape[0]
    size = query.shape[1] // heads
    q_norm = head_norm(query, heads).astype(jnp.bfloat16)
    k_norm = head_norm(key_own, heads).astype(jnp.bfloat16)
    keys = jnp.concatenate([k_norm, ctx_keys], 0)
    vals = jnp.concatenate([value_own.astype(jnp.bfloat16), ctx_vals], 0)
    allowed = jnp.concatenate([own_mask, ctx_mask], 1)
    q_heads = q_norm.reshape(count, heads, size).transpose(1, 0, 2)
    k_heads = keys.reshape(-1, heads, size).transpose(1, 0, 2)
    v_heads = vals.reshape(-1, heads, size).transpose(1, 0, 2)

    def one_head(pieces):
        q_one, k_one, v_one, temp = pieces
        scores = contract(q_one, k_one, 1, 1) * (temp / math.sqrt(size))
        scores = jnp.where(allowed, scores, NEG)
        top = lax.stop_gradient(lax.optimization_barrier(jnp.max(scores, axis=1, keepdims=True)))
        weights = jnp.exp(scores - top)
        probs = (weights / lax.optimization_barrier(jnp.sum(weights, axis=1, keepdims=True))).astype(jnp.bfloat16)
        return jnp.dot(probs, v_one, preferred_element_type=jnp.float32).astype(jnp.bfloat16)
    mixed = lax.map(jax.checkpoint(one_head), (q_heads, k_heads, v_heads, temps))
    return mixed.transpose(1, 0, 2).reshape(count, -1)

def build_masks(starts_local, first, frames, tokens, total):
    rows = frames * 2 * tokens
    row_ids = jnp.arange(rows, dtype=jnp.int32)
    group = row_ids // tokens
    own_mask = group[:, None] == group[None, :]
    row_frame = row_ids // (2 * tokens)
    lower = jnp.repeat(starts_local, 2 * tokens, total_repeat_length=rows)
    upper = first + row_frame
    ctx_frame = jnp.arange(total, dtype=jnp.int32) // tokens
    ctx_mask = (ctx_frame[None, :] >= lower[:, None]) & (ctx_frame[None, :] < upper[:, None])
    return (own_mask, ctx_mask)

def block_terms(noisy_rows, grad_rows, w_flat, w_out, mods, ctx_keys, ctx_vals, own_mask, ctx_mask, temps, heads):
    width = w_out.shape[0]
    model = w_out.shape[1]
    shift = mods[:, :model]
    scale = mods[:, model:2 * model]
    gate = mods[:, 2 * model:]

    def front(values):
        return modulate(values, shift, scale)
    hidden, front_back = jax.vjp(front, noisy_rows.astype(jnp.float32))
    qkv = jnp.dot(hidden, w_flat, preferred_element_type=jnp.float32)

    def mixer(query, key_own, value_own):
        return attend(query, key_own, value_own, ctx_keys, ctx_vals, own_mask, ctx_mask, temps, heads)
    mixed, mixer_back = jax.vjp(mixer, qkv[:, :width], qkv[:, width:2 * width], qkv[:, 2 * width:])
    grad_z = (gate * grad_rows.astype(jnp.float32)).astype(jnp.bfloat16)
    grad_mixed = contract(grad_z, w_out, 1, 1).astype(jnp.bfloat16)
    parts = mixer_back(grad_mixed)
    grad_proj = jnp.concatenate(parts, 1).astype(jnp.bfloat16)
    grad_hidden = contract(grad_proj, w_flat, 1, 1).astype(jnp.bfloat16)
    grad_input = front_back(grad_hidden)[0]
    grad_noisy = (grad_input + grad_rows.astype(jnp.float32)).astype(jnp.bfloat16)
    return (grad_noisy, hidden, grad_proj, mixed, grad_z)

def rounded(values):
    return lax.optimization_barrier(values.astype(jnp.bfloat16)).astype(jnp.float32)

def reference(noisy, clean, actions, levels, starts, w_qkv, w_out, noise_table, action_table, temps, out_grad):
    width = HEADS * HD
    w_flat = w_qkv.reshape(D, 3 * width)
    table = noise_table.reshape(LEVELS, 3 * D)
    acts = action_table.reshape(ACTIONS, 3 * D)
    rows = 2 * F_DEV * TOKF
    total_qkv = jnp.zeros((D, 3 * width), jnp.float32)
    total_out = jnp.zeros((width, D), jnp.float32)
    grads_all = []
    for replica in range(N_DP):
        act_rows = acts[actions[replica]]
        noisy_mods = table[levels[replica]] + act_rows[:, None, :]
        clean_mods = table[0][None, :] + act_rows
        clean_exp = jnp.repeat(clean_mods, TOKF, axis=0)
        clean_rows = clean[replica].reshape(FRAMES * TOKF, D).astype(jnp.float32)
        clean_hidden = modulate(clean_rows, clean_exp[:, :D], clean_exp[:, D:2 * D])
        clean_proj = jnp.dot(clean_hidden, w_flat[:, width:], preferred_element_type=jnp.float32)
        ctx_keys = head_norm(clean_proj[:, :width], HEADS).astype(jnp.bfloat16)
        ctx_vals = clean_proj[:, width:].astype(jnp.bfloat16)
        noisy_r = noisy[replica]
        grad_r = out_grad[replica]
        starts_r = starts[replica]

        def step(carry, block):
            acc_qkv, acc_out = carry
            first = (block * F_DEV).astype(jnp.int32)
            part_noisy = lax.dynamic_slice_in_dim(noisy_r, first, F_DEV, 0).reshape(rows, D)
            part_grad = lax.dynamic_slice_in_dim(grad_r, first, F_DEV, 0).reshape(rows, D)
            part_mods = lax.dynamic_slice_in_dim(noisy_mods, first, F_DEV, 0)
            mods = jnp.broadcast_to(part_mods[:, :, None, :], (F_DEV, 2, TOKF, 3 * D)).reshape(rows, 3 * D)
            part_starts = lax.dynamic_slice_in_dim(starts_r, first, F_DEV, 0)
            own_mask, ctx_mask = build_masks(part_starts, first, F_DEV, TOKF, FRAMES * TOKF)
            grad_noisy, hidden, grad_proj, mixed, grad_z = block_terms(part_noisy, part_grad, w_flat, w_out, mods, ctx_keys, ctx_vals, own_mask, ctx_mask, temps, HEADS)
            acc_qkv = acc_qkv + rounded(contract(hidden, grad_proj, 0, 0))
            acc_out = acc_out + rounded(contract(mixed, grad_z, 0, 0))
            return ((acc_qkv, acc_out), grad_noisy.reshape(F_DEV, 2, TOKF, D))
        init = (jnp.zeros((D, 3 * width), jnp.float32), jnp.zeros((width, D), jnp.float32))
        (acc_qkv, acc_out), grads = lax.scan(step, init, jnp.arange(N_TM, dtype=jnp.int32))
        total_qkv = total_qkv + rounded(acc_qkv)
        total_out = total_out + rounded(acc_out)
        grads_all.append(grads.reshape(FRAMES, 2, TOKF, D))
    grad_noisy = jnp.stack(grads_all, 0)
    return (grad_noisy, total_qkv.reshape(D, 3, width).astype(jnp.bfloat16), total_out.astype(jnp.bfloat16))
```

```python
import functools
import math

import jax
import jax.numpy as jnp
from jax import lax
from jax.experimental import pallas as pl
from jax.experimental.pallas import tpu as pltpu
from jax.sharding import PartitionSpec as P

EPS = 1e-06
NEG = -1e30
MESH = pl.DeviceIdType.MESH
HEADS = 8
HD = 128
BF = jnp.bfloat16
F32 = jnp.float32
ANY = pl.BlockSpec(memory_space=pl.ANY)
LOG2E = 1.4426950408889634


def dot(left, right, left_dim, right_dim):
    return lax.dot_general(
        left, right, (((left_dim,), (right_dim,)), ((), ())), preferred_element_type=F32
    )


def layer_norm(values):
    center = values - jnp.mean(values, axis=-1, keepdims=True)
    return center * lax.rsqrt(jnp.mean(center * center, axis=-1, keepdims=True) + EPS)


def head_norm(values):
    count = values.shape[0]
    split = values.reshape(count, HEADS, HD)
    factor = lax.rsqrt(jnp.mean(split * split, axis=-1, keepdims=True) + EPS)
    return (split * factor).reshape(count, -1)


def lanes(start, size):
    return pl.ds(pl.multiple_of(start, 128), size)


def rows_of(start, size):
    return pl.ds(pl.multiple_of(start, size), size)


def wait_bytes(ref, sem):
    pltpu.make_async_copy(ref, ref, sem).wait()


def place(t):
    return t // 8, (t // 2) % 4, t % 2


def head_home(h, x):
    return ((h // 2) * 4 + x) * 2 + h % 2


def shifted(t, s):
    y, x, z = place(t)
    dy, dx, dz = place(s)
    return (((y + dy) % 4) * 4 + (x + dx) % 4) * 2 + (z + dz) % 2


def spread_kernel(ck, cv, qn, kn, v, do, kv_ref, own_ref, sems):
    me = lax.axis_index("tm")
    y, x, z = place(me)
    slot = y * 2 + z
    barrier = pltpu.get_barrier_semaphore()

    def greet(s, carry):
        pl.semaphore_signal(
            barrier, inc=1, device_id={"tm": shifted(me, s)}, device_id_type=MESH
        )
        return carry

    lax.fori_loop(1, 32, greet, 0)
    pl.semaphore_wait(barrier, 31)

    def send_kv(s, carry):
        t = shifted(me, s)
        ty, _, tz = place(t)
        cut = lanes((ty * 2 + tz) * HD, HD)
        for part, ref in enumerate((ck, cv)):
            pltpu.make_async_remote_copy(
                src_ref=ref.at[:, cut],
                dst_ref=kv_ref.at[me, part],
                send_sem=sems.at[0],
                recv_sem=sems.at[1],
                device_id={"tm": t},
                device_id_type=MESH,
            ).start()
        return carry

    def send_own(s, carry):
        h = (slot + s) % 8
        cut = lanes(h * HD, HD)
        for part, ref in enumerate((qn, kn, v, do)):
            pltpu.make_async_remote_copy(
                src_ref=ref.at[:, cut],
                dst_ref=own_ref.at[slot, part],
                send_sem=sems.at[2],
                recv_sem=sems.at[3],
                device_id={"tm": head_home(h, x)},
                device_id_type=MESH,
            ).start()
        return carry

    lax.fori_loop(1, 32, send_kv, 0)
    lax.fori_loop(1, 8, send_own, 0)
    cut = lanes(slot * HD, HD)
    for part, ref in enumerate((ck, cv)):
        pltpu.make_async_copy(ref.at[:, cut], kv_ref.at[me, part], sems.at[4]).start()
    for part, ref in enumerate((qn, kn, v, do)):
        pltpu.make_async_copy(ref.at[:, cut], own_ref.at[slot, part], sems.at[5]).start()
    wait_bytes(kv_ref.at[0], sems.at[4])
    wait_bytes(own_ref.at[0], sems.at[5])
    wait_bytes(kv_ref.at[pl.ds(0, 31)], sems.at[0])
    wait_bytes(own_ref.at[pl.ds(0, 7)], sems.at[2])
    wait_bytes(kv_ref.at[pl.ds(0, 31)], sems.at[1])
    wait_bytes(own_ref.at[pl.ds(0, 7)], sems.at[3])


def spread(ck, cv, qn, kn, v, do):
    frames = 32
    tokens = ck.shape[0]
    rows = qn.shape[0]
    return pl.pallas_call(
        spread_kernel,
        out_shape=(
            jax.ShapeDtypeStruct((frames, 2, tokens, HD), BF),
            jax.ShapeDtypeStruct((8, 4, rows, HD), BF),
        ),
        in_specs=[ANY] * 6,
        out_specs=(ANY, ANY),
        scratch_shapes=[pltpu.SemaphoreType.DMA((6,))],
        compiler_params=pltpu.CompilerParams(collective_id=0, has_side_effects=True),
        name="spread",
    )(ck, cv, qn, kn, v, do)


def attend_kernel(frames, starts, temp, kv, own, out, s_scr):
    i = pl.program_id(0)
    g = frames[i]
    st = starts[i]
    n = g - st
    odd = n % 2
    pairs = n // 2
    first = st + odd
    scale = temp[0]
    c2 = scale * LOG2E
    q = own[0, 0]
    ko = own[0, 1]
    vo = own[0, 2]
    do = own[0, 3]
    k_odd = kv[st, 0]
    v_odd = kv[st, 1]
    h = HD

    s_own = jnp.concatenate([dot(q[:h], ko[:h], 1, 1), dot(q[h:], ko[h:], 1, 1)], 0)
    s_odd = jnp.where(odd == 1, dot(q, k_odd, 1, 1), NEG)
    s_scr[0, :, :h] = s_own
    s_scr[0, :, h:] = s_odd

    def scores(c, top):
        k = kv[pl.ds(first + 2 * c, 2), 0].reshape(2 * h, h)
        s = dot(q, k, 1, 1)
        s_scr[c + 1] = s
        return jnp.maximum(top, jnp.maximum(s[:, :h], s[:, h:]))

    top = lax.fori_loop(0, pairs, scores, jnp.maximum(s_own, s_odd))
    m2 = jnp.max(top, axis=1, keepdims=True) * c2

    p_own = jnp.exp2(s_own * c2 - m2)
    p_odd = jnp.exp2(s_odd * c2 - m2)
    pb_own = p_own.astype(BF)
    acc = jnp.concatenate([dot(pb_own[:h], vo[:h], 1, 0), dot(pb_own[h:], vo[h:], 1, 0)], 0)
    acc = acc + dot(p_odd.astype(BF), v_odd, 1, 0)

    def weigh(c, carry):
        acc, total = carry
        p = jnp.exp2(s_scr[c + 1] * c2 - m2)
        s_scr[c + 1] = p
        v = kv[pl.ds(first + 2 * c, 2), 1].reshape(2 * h, h)
        return acc + dot(p.astype(BF), v, 1, 0), total + p[:, :h] + p[:, h:]

    acc, total = lax.fori_loop(0, pairs, weigh, (acc, p_own + p_odd))
    inv = 1.0 / jnp.sum(total, axis=1, keepdims=True)
    mixed = acc * inv
    delta = jnp.sum(mixed * do.astype(F32), axis=1, keepdims=True)
    out[0, 0] = mixed.astype(BF)

    dp_own = jnp.concatenate([dot(do[:h], vo[:h], 1, 1), dot(do[h:], vo[h:], 1, 1)], 0)
    ds_own = (p_own * (dp_own - delta)).astype(BF)
    ds_odd = (p_odd * (dot(do, v_odd, 1, 1) - delta)).astype(BF)
    dq = jnp.concatenate([dot(ds_own[:h], ko[:h], 1, 0), dot(ds_own[h:], ko[h:], 1, 0)], 0)
    dq = dq + dot(ds_odd, k_odd, 1, 0)

    def pull(c, dq):
        k = kv[pl.ds(first + 2 * c, 2), 0].reshape(2 * h, h)
        v = kv[pl.ds(first + 2 * c, 2), 1].reshape(2 * h, h)
        ds = s_scr[c + 1] * (dot(do, v, 1, 1) - delta)
        return dq + dot(ds.astype(BF), k, 1, 0)

    dq = lax.fori_loop(0, pairs, pull, dq)
    out[0, 1] = (dq * (inv * scale)).astype(BF)
    dsn = (p_own * (dp_own - delta) * (inv * scale)).astype(BF)
    pn = (p_own * inv).astype(BF)
    for j in range(2):
        cut = slice(j * h, (j + 1) * h)
        out[0, 2, cut] = dot(dsn[cut], q[cut], 0, 0).astype(BF)
        out[0, 3, cut] = dot(pn[cut], do[cut], 0, 0).astype(BF)


def attend(frames, starts, temp, kv, own):
    rows = own.shape[2]
    smem = pl.BlockSpec(memory_space=pltpu.SMEM)
    return pl.pallas_call(
        attend_kernel,
        grid=(8,),
        out_shape=jax.ShapeDtypeStruct(own.shape, BF),
        in_specs=[
            smem,
            smem,
            smem,
            pl.BlockSpec(kv.shape, lambda i: (0, 0, 0, 0)),
            pl.BlockSpec((1, 4, rows, HD), lambda i: (i, 0, 0, 0)),
        ],
        out_specs=pl.BlockSpec((1, 4, rows, HD), lambda i: (i, 0, 0, 0)),
        scratch_shapes=[pltpu.VMEM((17, rows, 2 * HD), F32)],
        compiler_params=pltpu.CompilerParams(vmem_limit_bytes=40 * 1024 * 1024),
        name="attend",
    )(frames, starts, temp, kv, own)


def bring_kernel(res, mixed, dqkv, sems):
    me = lax.axis_index("tm")
    y, x, z = place(me)
    slot = y * 2 + z
    barrier = pltpu.get_barrier_semaphore()

    def greet(s, carry):
        pl.semaphore_signal(
            barrier,
            inc=1,
            device_id={"tm": head_home((slot + s) % 8, x)},
            device_id_type=MESH,
        )
        return carry

    lax.fori_loop(1, 8, greet, 0)
    pl.semaphore_wait(barrier, 7)

    def send(s, carry):
        i = (slot + s) % 8
        for part in range(4):
            if part == 0:
                dst = mixed.at[:, lanes(slot * HD, HD)]
            else:
                dst = dqkv.at[:, lanes((part - 1) * 1024 + slot * HD, HD)]
            pltpu.make_async_remote_copy(
                src_ref=res.at[i, part],
                dst_ref=dst,
                send_sem=sems.at[0],
                recv_sem=sems.at[1 if part == 0 else 2],
                device_id={"tm": head_home(i, x)},
                device_id_type=MESH,
            ).start()
        return carry

    lax.fori_loop(1, 8, send, 0)
    cut = lanes(slot * HD, HD)
    pltpu.make_async_copy(res.at[slot, 0], mixed.at[:, cut], sems.at[3]).start()
    for part in range(1, 4):
        dst = dqkv.at[:, lanes((part - 1) * 1024 + slot * HD, HD)]
        pltpu.make_async_copy(res.at[slot, part], dst, sems.at[3]).start()
    wait_bytes(res.at[0], sems.at[3])
    wait_bytes(res.at[pl.ds(0, 7)], sems.at[0])
    wait_bytes(mixed.at[:, pl.ds(0, 7 * HD)], sems.at[1])
    wait_bytes(dqkv.at[:, pl.ds(0, 21 * HD)], sems.at[2])


def bring(res):
    rows = res.shape[2]
    return pl.pallas_call(
        bring_kernel,
        out_shape=(
            jax.ShapeDtypeStruct((rows, HEADS * HD), BF),
            jax.ShapeDtypeStruct((rows, 3 * HEADS * HD), BF),
        ),
        in_specs=[ANY],
        out_specs=(ANY, ANY),
        scratch_shapes=[pltpu.SemaphoreType.DMA((4,))],
        compiler_params=pltpu.CompilerParams(collective_id=1, has_side_effects=True),
        name="bring",
    )(res)


def swap_kernel(hidden, mixed, proj, gz, h2, m2, p2, z2, sems):
    rows = hidden.shape[0]
    d = lax.axis_index("dp")
    core = d % 2
    partner = d + 1 - 2 * core
    barrier = pltpu.get_barrier_semaphore()
    pl.semaphore_signal(barrier, inc=1, device_id={"dp": partner}, device_id_type=MESH)
    pl.semaphore_wait(barrier, 1)
    here = rows_of(core * rows, rows)
    whole = [(hidden, h2.at[here], 0), (mixed, m2.at[here], 1)]

    def halves(c):
        cuts = []
        for zl in range(2):
            for j in range(3):
                cuts.append(
                    (
                        proj.at[:, lanes(j * 1024 + zl * 512 + c * 256, 256)],
                        p2.at[here, pl.ds(zl * 768 + j * 256, 256)],
                        2,
                    )
                )
            cuts.append(
                (gz.at[:, lanes(zl * 1024 + c * 512, 512)], z2.at[here, pl.ds(zl * 512, 512)], 3)
            )
        return cuts

    for src, dst, part in whole + halves(1 - core):
        pltpu.make_async_remote_copy(
            src_ref=src,
            dst_ref=dst,
            send_sem=sems.at[0, part],
            recv_sem=sems.at[1, part],
            device_id={"dp": partner},
            device_id_type=MESH,
        ).start()
    for src, dst, part in whole + halves(core):
        pltpu.make_async_copy(src, dst, sems.at[2, part]).start()
    for way in (2, 0, 1):
        for part, ref in enumerate((h2, m2, p2, z2)):
            wait_bytes(ref.at[pl.ds(0, rows)], sems.at[way, part])


def swap(hidden, mixed, proj, gz):
    rows = hidden.shape[0]
    shapes = ((2 * rows, 2048), (2 * rows, 1024), (2 * rows, 1536), (2 * rows, 1024))
    return pl.pallas_call(
        swap_kernel,
        out_shape=tuple(jax.ShapeDtypeStruct(shape, BF) for shape in shapes),
        in_specs=[ANY] * 4,
        out_specs=(ANY,) * 4,
        scratch_shapes=[pltpu.SemaphoreType.DMA((3, 4))],
        compiler_params=pltpu.CompilerParams(collective_id=2, has_side_effects=True),
        name="swap",
    )(hidden, mixed, proj, gz)


def total_kernel(tg, to, out_g, out_o, got_g, got_o, sems):
    t = lax.axis_index("tm")
    d = lax.axis_index("dp")
    zl = d // 2
    core = d % 2
    me = zl * 32 + t
    barrier = pltpu.get_barrier_semaphore()

    def target(s):
        return shifted(t, s % 32), (zl + s // 32) % 2

    def greet(s, carry):
        tt, tz = target(s)
        pl.semaphore_signal(
            barrier, inc=1, device_id={"tm": tt, "dp": tz * 2 + core}, device_id_type=MESH
        )
        return carry

    lax.fori_loop(1, 64, greet, 0)
    pl.semaphore_wait(barrier, 63)

    def send(s, carry):
        tt, tz = target(s)
        for src, dst, sem in (
            (tg.at[rows_of(tt * 64, 64), lanes(tz * 768, 768)], got_g.at[me], 0),
            (to.at[rows_of(tt * 32, 32), lanes(tz * 512, 512)], got_o.at[me], 1),
        ):
            pltpu.make_async_remote_copy(
                src_ref=src,
                dst_ref=dst,
                send_sem=sems.at[sem],
                recv_sem=sems.at[2 + sem],
                device_id={"tm": tt, "dp": tz * 2 + core},
                device_id_type=MESH,
            ).start()
        return carry

    lax.fori_loop(1, 64, send, 0)
    own_g = tg.at[rows_of(t * 64, 64), lanes(zl * 768, 768)]
    own_o = to.at[rows_of(t * 32, 32), lanes(zl * 512, 512)]
    copies = [
        pltpu.make_async_copy(own_g, got_g.at[me], sems.at[4]),
        pltpu.make_async_copy(own_o, got_o.at[me], sems.at[5]),
    ]
    for copy in copies:
        copy.start()
    for copy in copies:
        copy.wait()
    for sem in (0, 2):
        wait_bytes(got_g.at[pl.ds(0, 63)], sems.at[sem])
        wait_bytes(got_o.at[pl.ds(0, 63)], sems.at[sem + 1])

    for j in range(3):
        cut = slice(j * 256, (j + 1) * 256)

        def add(n, acc):
            return acc + got_g[n, :, cut].astype(F32)

        out_g[j] = lax.fori_loop(0, 64, add, jnp.zeros((64, 256), F32)).astype(BF)

    def add_out(n, acc):
        return acc + got_o[n].astype(F32)

    out_o[...] = lax.fori_loop(0, 64, add_out, jnp.zeros((32, 512), F32)).astype(BF)


def total(tg, to):
    vmem = pl.BlockSpec(memory_space=pltpu.VMEM)
    return pl.pallas_call(
        total_kernel,
        out_shape=(
            jax.ShapeDtypeStruct((3, 64, 256), BF),
            jax.ShapeDtypeStruct((32, 512), BF),
        ),
        in_specs=[ANY] * 2,
        out_specs=(vmem, vmem),
        scratch_shapes=[
            pltpu.VMEM((64, 64, 768), BF),
            pltpu.VMEM((64, 32, 512), BF),
            pltpu.SemaphoreType.DMA((6,)),
        ],
        compiler_params=pltpu.CompilerParams(
            collective_id=3, has_side_effects=True, vmem_limit_bytes=40 * 1024 * 1024
        ),
        name="total",
    )(tg, to)


def on_device(
    noisy, clean, actions, levels, starts, w_qkv, w_out, noise_table, action_table, temps, out_grad
):
    tokens, model = noisy.shape[3:]
    rows = 2 * tokens
    width = w_out.shape[0]
    t = lax.axis_index("tm")
    y, x, z = place(t)
    starts_all = lax.all_gather(starts.reshape(1), "tm", axis=0, tiled=True)
    w3 = w_qkv.transpose(1, 0, 2)

    def pick(table, index):
        return lax.dynamic_index_in_dim(table, index, 0, keepdims=False)

    action_mod = pick(action_table, actions[0, 0])
    clean_mod = noise_table[0] + action_mod
    mods = jnp.stack([pick(noise_table, levels[0, 0, j]) + action_mod for j in range(2)])

    def spread_rows(part):
        return jnp.broadcast_to(mods[:, None, part, :], (2, tokens, model)).reshape(rows, model)

    shift, scale, gate = spread_rows(0), spread_rows(1), spread_rows(2)

    clean_rows = clean.reshape(tokens, model).astype(F32)
    clean_hidden = (layer_norm(clean_rows) * (1.0 + clean_mod[1]) + clean_mod[0]).astype(BF)
    ckn = head_norm(dot(clean_hidden, w3[1], 1, 0)).astype(BF)
    cv = dot(clean_hidden, w3[2], 1, 0).astype(BF)

    noisy_rows = noisy.reshape(rows, model).astype(F32)
    grad_rows = out_grad.reshape(rows, model).astype(F32)

    def front(values):
        return (layer_norm(values) * (1.0 + scale) + shift).astype(BF)

    hidden, front_back = jax.vjp(front, noisy_rows)
    q = dot(hidden, w3[0], 1, 0)
    k = dot(hidden, w3[1], 1, 0)
    v = dot(hidden, w3[2], 1, 0).astype(BF)
    qn, q_back = jax.vjp(lambda u: head_norm(u).astype(BF), q)
    kn, k_back = jax.vjp(lambda u: head_norm(u).astype(BF), k)
    grad_z = (gate * grad_rows).astype(BF)
    grad_mixed = dot(grad_z, w_out, 1, 1).astype(BF)

    kv, own = spread(ckn, cv, qn, kn, v, grad_mixed)
    slots = jnp.arange(8, dtype=jnp.int32)
    my_frames = (slots // 2) * 8 + x * 2 + slots % 2
    my_starts = starts_all.reshape(4, 4, 2)[:, x].reshape(8)
    temp = (pick(temps, y * 2 + z) / math.sqrt(HD)).reshape(1)
    res = attend(my_frames, my_starts, temp, kv, own)
    mixed, dqkv = bring(res)

    grad_proj = jnp.concatenate(
        [
            q_back(dqkv[:, :width])[0].astype(BF),
            k_back(dqkv[:, width : 2 * width])[0].astype(BF),
            dqkv[:, 2 * width :],
        ],
        1,
    )
    grad_hidden = sum(
        dot(grad_proj[:, j * width : (j + 1) * width], w3[j], 1, 1) for j in range(3)
    ).astype(BF)
    grad_noisy = (front_back(grad_hidden)[0] + grad_rows).astype(BF)

    h2, m2, p2, z2 = swap(hidden, mixed, grad_proj, grad_z)
    term_g = dot(h2, p2, 0, 0).astype(BF)
    term_o = dot(m2, z2, 0, 0).astype(BF)
    total_g, total_o = total(term_g, term_o)
    return (grad_noisy.reshape(noisy.shape), total_g.transpose(1, 0, 2), total_o)


def solution(mesh):
    in_specs = (
        P("dp", "tm", None, None, None),
        P("dp", "tm", None, None),
        P("dp", "tm"),
        P("dp", "tm", None),
        P("dp", "tm"),
        P(),
        P(),
        P(),
        P(),
        P(),
        P("dp", "tm", None, None, None),
    )
    out_specs = (P("dp", "tm", None, None, None), P("tm", None, "dp"), P("tm", "dp"))
    return jax.shard_map(
        on_device, mesh=mesh, in_specs=in_specs, out_specs=out_specs, check_vma=False
    )
```

```python
import functools
import math

import jax
import jax.numpy as jnp
from jax import lax
from jax.experimental import pallas as pl
from jax.experimental.pallas import tpu as pltpu
from jax.sharding import PartitionSpec as P

EPS = 1e-06
NEG = -1e30
MESH = pl.DeviceIdType.MESH
HEADS = 8
HD = 128
BF = jnp.bfloat16
F32 = jnp.float32
ANY = pl.BlockSpec(memory_space=pl.ANY)
LOG2E = 1.4426950408889634


def dot(left, right, left_dim, right_dim):
    return lax.dot_general(
        left, right, (((left_dim,), (right_dim,)), ((), ())), preferred_element_type=F32
    )


def layer_norm(values):
    center = values - jnp.mean(values, axis=-1, keepdims=True)
    return center * lax.rsqrt(jnp.mean(center * center, axis=-1, keepdims=True) + EPS)


def head_norm(values):
    count = values.shape[0]
    split = values.reshape(count, HEADS, HD)
    factor = lax.rsqrt(jnp.mean(split * split, axis=-1, keepdims=True) + EPS)
    return (split * factor).reshape(count, -1)


def lanes(start, size):
    return pl.ds(pl.multiple_of(start, 128), size)


def rows_of(start, size):
    return pl.ds(pl.multiple_of(start, size), size)


def wait_bytes(ref, sem):
    pltpu.make_async_copy(ref, ref, sem).wait()


def place(t):
    return t // 8, (t // 2) % 4, t % 2


def head_home(h, x):
    return ((h // 2) * 4 + x) * 2 + h % 2


def shifted(t, s):
    y, x, z = place(t)
    dy, dx, dz = place(s)
    return (((y + dy) % 4) * 4 + (x + dx) % 4) * 2 + (z + dz) % 2


def spread_kernel(ck, cv, qn, kn, v, do, kv_ref, own_ref, sems):
    me = lax.axis_index("tm")
    y, x, z = place(me)
    slot = y * 2 + z
    barrier = pltpu.get_barrier_semaphore()

    def greet(s, carry):
        pl.semaphore_signal(
            barrier, inc=1, device_id={"tm": shifted(me, s)}, device_id_type=MESH
        )
        return carry

    lax.fori_loop(1, 32, greet, 0)
    pl.semaphore_wait(barrier, 31)

    def send_kv(s, carry):
        t = shifted(me, s)
        ty, _, tz = place(t)
        cut = lanes((ty * 2 + tz) * HD, HD)
        for part, ref in enumerate((ck, cv)):
            pltpu.make_async_remote_copy(
                src_ref=ref.at[:, cut],
                dst_ref=kv_ref.at[me, part],
                send_sem=sems.at[0],
                recv_sem=sems.at[1],
                device_id={"tm": t},
                device_id_type=MESH,
            ).start()
        return carry

    def send_own(s, carry):
        h = (slot + s) % 8
        cut = lanes(h * HD, HD)
        for part, ref in enumerate((qn, kn, v, do)):
            pltpu.make_async_remote_copy(
                src_ref=ref.at[:, cut],
                dst_ref=own_ref.at[slot, part],
                send_sem=sems.at[2],
                recv_sem=sems.at[3],
                device_id={"tm": head_home(h, x)},
                device_id_type=MESH,
            ).start()
        return carry

    lax.fori_loop(1, 32, send_kv, 0)
    lax.fori_loop(1, 8, send_own, 0)
    cut = lanes(slot * HD, HD)
    for part, ref in enumerate((ck, cv)):
        pltpu.make_async_copy(ref.at[:, cut], kv_ref.at[me, part], sems.at[4]).start()
    for part, ref in enumerate((qn, kn, v, do)):
        pltpu.make_async_copy(ref.at[:, cut], own_ref.at[slot, part], sems.at[5]).start()
    wait_bytes(kv_ref.at[0], sems.at[4])
    wait_bytes(own_ref.at[0], sems.at[5])
    wait_bytes(kv_ref.at[pl.ds(0, 31)], sems.at[0])
    wait_bytes(own_ref.at[pl.ds(0, 7)], sems.at[2])
    wait_bytes(kv_ref.at[pl.ds(0, 31)], sems.at[1])
    wait_bytes(own_ref.at[pl.ds(0, 7)], sems.at[3])


def spread(ck, cv, qn, kn, v, do):
    frames = 32
    tokens = ck.shape[0]
    rows = qn.shape[0]
    return pl.pallas_call(
        spread_kernel,
        out_shape=(
            jax.ShapeDtypeStruct((frames, 2, tokens, HD), BF),
            jax.ShapeDtypeStruct((8, 4, rows, HD), BF),
        ),
        in_specs=[ANY] * 6,
        out_specs=(ANY, ANY),
        scratch_shapes=[pltpu.SemaphoreType.DMA((6,))],
        compiler_params=pltpu.CompilerParams(collective_id=0, has_side_effects=True),
        name="spread",
    )(ck, cv, qn, kn, v, do)


def attend_kernel(frames, starts, temp, kv, own, out, s_scr):
    i = pl.program_id(0)
    g = frames[i]
    st = starts[i]
    n = g - st
    odd = n % 2
    pairs = n // 2
    first = st + odd
    scale = temp[0]
    c2 = scale * LOG2E
    q = own[0, 0]
    ko = own[0, 1]
    vo = own[0, 2]
    do = own[0, 3]
    k_odd = kv[st, 0]
    v_odd = kv[st, 1]
    h = HD

    s_own = jnp.concatenate([dot(q[:h], ko[:h], 1, 1), dot(q[h:], ko[h:], 1, 1)], 0)
    s_odd = jnp.where(odd == 1, dot(q, k_odd, 1, 1), NEG)
    s_scr[0, :, :h] = s_own
    s_scr[0, :, h:] = s_odd

    def scores(c, top):
        k = kv[pl.ds(first + 2 * c, 2), 0].reshape(2 * h, h)
        s = dot(q, k, 1, 1)
        s_scr[c + 1] = s
        return jnp.maximum(top, jnp.maximum(s[:, :h], s[:, h:]))

    top = lax.fori_loop(0, pairs, scores, jnp.maximum(s_own, s_odd))
    m2 = jnp.max(top, axis=1, keepdims=True) * c2

    p_own = jnp.exp2(s_own * c2 - m2)
    p_odd = jnp.exp2(s_odd * c2 - m2)
    pb_own = p_own.astype(BF)
    acc = jnp.concatenate([dot(pb_own[:h], vo[:h], 1, 0), dot(pb_own[h:], vo[h:], 1, 0)], 0)
    acc = acc + dot(p_odd.astype(BF), v_odd, 1, 0)

    def weigh(c, carry):
        acc, total = carry
        p = jnp.exp2(s_scr[c + 1] * c2 - m2)
        s_scr[c + 1] = p
        v = kv[pl.ds(first + 2 * c, 2), 1].reshape(2 * h, h)
        return acc + dot(p.astype(BF), v, 1, 0), total + p[:, :h] + p[:, h:]

    acc, total = lax.fori_loop(0, pairs, weigh, (acc, p_own + p_odd))
    inv = 1.0 / jnp.sum(total, axis=1, keepdims=True)
    mixed = acc * inv
    delta = jnp.sum(mixed * do.astype(F32), axis=1, keepdims=True)
    out[0, 0] = mixed.astype(BF)

    dp_own = jnp.concatenate([dot(do[:h], vo[:h], 1, 1), dot(do[h:], vo[h:], 1, 1)], 0)
    ds_own = (p_own * (dp_own - delta)).astype(BF)
    ds_odd = (p_odd * (dot(do, v_odd, 1, 1) - delta)).astype(BF)
    dq = jnp.concatenate([dot(ds_own[:h], ko[:h], 1, 0), dot(ds_own[h:], ko[h:], 1, 0)], 0)
    dq = dq + dot(ds_odd, k_odd, 1, 0)

    def pull(c, dq):
        k = kv[pl.ds(first + 2 * c, 2), 0].reshape(2 * h, h)
        v = kv[pl.ds(first + 2 * c, 2), 1].reshape(2 * h, h)
        ds = s_scr[c + 1] * (dot(do, v, 1, 1) - delta)
        return dq + dot(ds.astype(BF), k, 1, 0)

    dq = lax.fori_loop(0, pairs, pull, dq)
    out[0, 1] = (dq * (inv * scale)).astype(BF)
    dsn = (p_own * (dp_own - delta) * (inv * scale)).astype(BF)
    pn = (p_own * inv).astype(BF)
    for j in range(2):
        cut = slice(j * h, (j + 1) * h)
        out[0, 2, cut] = dot(dsn[cut], q[cut], 0, 0).astype(BF)
        out[0, 3, cut] = dot(pn[cut], do[cut], 0, 0).astype(BF)


def attend(frames, starts, temp, kv, own):
    rows = own.shape[2]
    smem = pl.BlockSpec(memory_space=pltpu.SMEM)
    return pl.pallas_call(
        attend_kernel,
        grid=(8,),
        out_shape=jax.ShapeDtypeStruct(own.shape, BF),
        in_specs=[
            smem,
            smem,
            smem,
            pl.BlockSpec(kv.shape, lambda i: (0, 0, 0, 0)),
            pl.BlockSpec((1, 4, rows, HD), lambda i: (i, 0, 0, 0)),
        ],
        out_specs=pl.BlockSpec((1, 4, rows, HD), lambda i: (i, 0, 0, 0)),
        scratch_shapes=[pltpu.VMEM((17, rows, 2 * HD), F32)],
        compiler_params=pltpu.CompilerParams(vmem_limit_bytes=40 * 1024 * 1024),
        name="attend",
    )(frames, starts, temp, kv, own)


ORDERS = (("x", "y", "z"), ("y", "z", "x"), ("z", "x", "y"))
UNITS = (5, 5, 6)
FIRST_UNIT = (0, 5, 10)


def stream_of(unit):
    k = 0 if unit < 5 else 1 if unit < 10 else 2
    return k, unit - FIRST_UNIT[k]


def close_kernel(
    res, hidden, gz, q, k, noisy, grad, scale1, w3,
    out_n, out_g, out_o,
    got, proj, ph, pm, pp, pz, w, gh,
    t0a, t0b, t0c, t1a, t1b, t1c, t2a, t2b, t2c, b0a, b0b, b0c, b1a, b1b, b1c, b2a, b2b, b2c,
    back_sems, swap_sems, w_sem, ring_sems, last_sems,
):
    t = lax.axis_index("tm")
    d = lax.axis_index("dp")
    y, x, zh = place(t)
    zl, core = d // 2, d % 2
    z = zh * 2 + zl
    slot = y * 2 + zh
    partner = {"dp": d + 1 - 2 * core, "tm": t}
    at = {"x": x, "y": y, "z": z}
    rows = hidden.shape[0]
    terms = ((t0a, t0b, t0c), (t1a, t1b, t1c), (t2a, t2b, t2c))
    boxes = ((b0a, b0b, b0c), (b1a, b1b, b1c), (b2a, b2b, b2c))

    def along(axis, step):
        c = dict(at)
        c[axis] = (c[axis] + step) % 4
        return {
            "dp": (c["z"] % 2) * 2 + core,
            "tm": (c["y"] * 4 + c["x"]) * 2 + c["z"] // 2,
        }

    load_w = pltpu.make_async_copy(w3, w, w_sem)
    load_w.start()
    barrier = pltpu.get_barrier_semaphore()

    def greet(s, carry):
        pl.semaphore_signal(
            barrier,
            inc=1,
            device_id={"dp": d, "tm": head_home((slot + s) % 8, x)},
            device_id_type=MESH,
        )
        return carry

    lax.fori_loop(1, 8, greet, 0)
    for axis in "xyz":
        for step in (1, 2, 3):
            pl.semaphore_signal(
                barrier, inc=1, device_id=along(axis, step), device_id_type=MESH
            )
    pl.semaphore_signal(barrier, inc=1, device_id=partner, device_id_type=MESH)
    pl.semaphore_wait(barrier, 17)

    def remote(src, dst, send_sem, recv_sem, device):
        return pltpu.make_async_remote_copy(
            src_ref=src,
            dst_ref=dst,
            send_sem=send_sem,
            recv_sem=recv_sem,
            device_id=device,
            device_id_type=MESH,
        )

    def send_back(s, carry):
        i = (slot + s) % 8
        remote(
            res.at[i], got.at[slot], back_sems.at[0], back_sems.at[1],
            {"dp": d, "tm": head_home(i, x)},
        ).start()
        return carry

    lax.fori_loop(1, 8, send_back, 0)
    own = pltpu.make_async_copy(res.at[slot], got.at[slot], back_sems.at[2])
    own.start()

    def swap(src, dst, part):
        copy = remote(src, dst, swap_sems.at[0, part], swap_sems.at[1, part], partner)
        copy.start()
        return copy

    other = 1 - core
    swaps = [swap(hidden, ph, 0)]
    for l in range(2):
        cut = lanes(l * 1024 + other * 512, 512)
        swaps.append(swap(gz.at[:, cut], pz.at[:, pl.ds(l * 512, 512)], 1 + l))

    own.wait()
    wait_bytes(got.at[pl.ds(0, 7)], back_sems.at[1])
    swaps.append(swap(got.at[:, 0], pm, 3))

    def norm_back(h, carry):
        for part, u_ref in ((0, q), (1, k)):
            u = u_ref[:, lanes(h * HD, HD)]
            factor = lax.rsqrt(jnp.mean(u * u, axis=1, keepdims=True) + EPS)
            hat = u * factor
            g = got[h, 1 + part].astype(F32)
            du = factor * (g - hat * jnp.mean(hat * g, axis=1, keepdims=True))
            proj[:, lanes(part * 1024 + h * HD, HD)] = du.astype(BF)
        proj[:, lanes(2048 + h * HD, HD)] = got[h, 3]
        return carry

    lax.fori_loop(0, 8, norm_back, 0)
    for l in range(2):
        for j in range(3):
            swaps.append(
                swap(
                    proj.at[:, lanes(j * 1024 + l * 512 + other * 256, 256)],
                    pp.at[:, pl.ds(l * 768 + j * 256, 256)],
                    4 + l * 3 + j,
                )
            )
    for copy in swaps:
        copy.wait_recv()

    def put(yb, xb, zb, unit, value):
        s, u = stream_of(unit)
        spot = {"x": xb, "y": yb, "z": zb}
        terms[0][s][spot[ORDERS[s][0]], spot[ORDERS[s][1]], spot[ORDERS[s][2]], u] = value

    def terms_of(yb, carry):
        cut = lanes(yb * 512, 512)
        left = jnp.concatenate([hidden[:, cut], ph[:, cut]], 0).T
        for l in range(2):
            for j in range(3):
                mine = proj[:, lanes(j * 1024 + l * 512 + core * 256, 256)]
                theirs = pp[:, l * 768 + j * 256 : l * 768 + (j + 1) * 256]
                right = jnp.concatenate([mine, theirs], 0)
                term = dot(left, right, 1, 0).astype(BF)
                for xb in range(4):
                    for hb in range(2):
                        for rg in range(4):
                            r = (xb * 2 + hb) * 64 + rg * 16
                            put(yb, xb, hb * 2 + l, j * 4 + rg, term[r : r + 16])
        left = jnp.concatenate(
            [
                jnp.concatenate([got[2 * yb, 0], got[2 * yb + 1, 0]], 1),
                jnp.concatenate([pm[2 * yb], pm[2 * yb + 1]], 1),
            ],
            0,
        ).T
        for l in range(2):
            mine = gz[:, lanes(l * 1024 + core * 512, 512)]
            right = jnp.concatenate([mine, pz[:, l * 512 : (l + 1) * 512]], 0)
            term = dot(left, right, 1, 0).astype(BF)
            for xb in range(4):
                for hb in range(2):
                    for rg in range(2):
                        for ch in range(2):
                            r = (xb * 2 + hb) * 32 + rg * 16
                            put(
                                yb, xb, hb * 2 + l, 12 + rg * 2 + ch,
                                term[r : r + 16, ch * 256 : (ch + 1) * 256],
                            )
        return carry

    lax.fori_loop(0, 4, terms_of, 0)

    travel = (pl.ds(0, 2), pl.ds(2, 2))

    def ring(s, level, way, part):
        axis = ORDERS[s][level]
        step = 1 if way == 0 else 3
        near, far = (at[axis] + step) % 4, (at[axis] + 2) % 4
        src = (
            terms[level][s].at[far, travel[way]],
            terms[level][s].at[near, travel[1 - way]],
            terms[level][s].at[near, travel[way]],
        )[part]
        sems = ring_sems.at[s, level, way, part]
        return remote(
            src, boxes[level][s].at[way, part], sems.at[0], sems.at[1], along(axis, step)
        )

    def ring_open(level, s):
        for part in range(2):
            for way in range(2):
                ring(s, level, way, part).start()

    def ring_middle(level, s):
        axis = ORDERS[s][level]
        for way in range(2):
            ring(s, level, way, 0).wait_recv()
            near = (at[axis] + (1 if way == 0 else 3)) % 4
            spot = terms[level][s].at[near, travel[way]]
            spot[...] = (
                spot[...].astype(F32) + boxes[level][s][way, 0].astype(F32)
            ).astype(BF)
            ring(s, level, way, 2).start()

    def ring_close(level, s):
        for way in range(2):
            ring(s, level, way, 1).wait_recv()
            ring(s, level, way, 2).wait_recv()
        mine = at[ORDERS[s][level]]
        box = boxes[level][s]
        for way in range(2):
            terms[level + 1][s][travel[way]] = (
                terms[level][s][mine, travel[way]].astype(F32)
                + box[way, 2].astype(F32)
                + box[1 - way, 1].astype(F32)
            ).astype(BF)

    for s in range(3):
        ring_open(0, s)

    load_w.wait()

    def pull_hidden(n, carry):
        cut = lanes(n * 512, 512)
        total = dot(proj[:, :1024], w[0, cut, :], 1, 1)
        total = total + dot(proj[:, 1024:2048], w[1, cut, :], 1, 1)
        total = total + dot(proj[:, 2048:], w[2, cut, :], 1, 1)
        gh[:, cut] = total.astype(BF)
        return carry

    lax.fori_loop(0, 4, pull_hidden, 0)
    for s in range(3):
        ring_middle(0, s)

    def norm_rows(n, carry):
        cut = rows_of(n * 16, 16)
        level = n // 8
        v = noisy[cut, :].astype(F32)
        center = v - jnp.mean(v, axis=1, keepdims=True)
        factor = lax.rsqrt(jnp.mean(center * center, axis=1, keepdims=True) + EPS)
        hat = center * factor
        g = gh[cut, :].astype(F32) * scale1[pl.ds(level, 1), :]
        dv = factor * (
            g
            - jnp.mean(g, axis=1, keepdims=True)
            - hat * jnp.mean(g * hat, axis=1, keepdims=True)
        )
        out_n[cut, :] = (dv + grad[cut, :].astype(F32)).astype(BF)
        return carry

    lax.fori_loop(0, rows // 16, norm_rows, 0)

    for s in range(3):
        ring_close(0, s)
        ring_open(1, s)
    for s in range(3):
        ring_middle(1, s)

    def last(s, step):
        axis = ORDERS[s][2]
        there = (at[axis] + step) % 4
        sems = last_sems.at[s, step - 1]
        return remote(
            terms[2][s].at[there], boxes[2][s].at[step - 1], sems.at[0], sems.at[1],
            along(axis, step),
        )

    for s in range(3):
        ring_close(1, s)
        for step in (1, 2, 3):
            last(s, step).start()
    for s in range(3):
        for step in (1, 2, 3):
            last(s, step).wait_recv()
        mine = at[ORDERS[s][2]]
        sums = terms[2][s][mine].astype(F32)
        for step in (1, 2, 3):
            sums = sums + boxes[2][s][step - 1].astype(F32)
        sums = sums.astype(BF)
        for u in range(UNITS[s]):
            unit = FIRST_UNIT[s] + u
            if unit < 12:
                j, rg = unit // 4, unit % 4
                out_g[j, rg * 16 : (rg + 1) * 16, :] = sums[u]
            else:
                rg, ch = (unit - 12) // 2, (unit - 12) % 2
                out_o[rg * 16 : (rg + 1) * 16, ch * 256 : (ch + 1) * 256] = sums[u]

    wait_bytes(got.at[pl.ds(0, 7)], back_sems.at[0])
    for copy in swaps:
        copy.wait_send()
    for s in range(3):
        for level in range(2):
            for way in range(2):
                for part in range(3):
                    ring(s, level, way, part).wait_send()
        for step in (1, 2, 3):
            last(s, step).wait_send()


def close(res, hidden, gz, q, k, noisy, grad, scale1, w3):
    rows, model = hidden.shape
    vmem = pl.BlockSpec(memory_space=pltpu.VMEM)

    def box(*shape):
        return [pltpu.VMEM(shape + (u, 16, 256), BF) for u in UNITS]

    return pl.pallas_call(
        close_kernel,
        out_shape=(
            jax.ShapeDtypeStruct((rows, model), BF),
            jax.ShapeDtypeStruct((3, 64, 256), BF),
            jax.ShapeDtypeStruct((32, 512), BF),
        ),
        in_specs=[ANY] + [vmem] * 7 + [ANY],
        out_specs=(vmem,) * 3,
        scratch_shapes=[
            pltpu.VMEM((8, 4, rows, HD), BF),
            pltpu.VMEM((rows, 3072), BF),
            pltpu.VMEM((rows, model), BF),
            pltpu.VMEM((8, rows, HD), BF),
            pltpu.VMEM((rows, 1536), BF),
            pltpu.VMEM((rows, 1024), BF),
            pltpu.VMEM(w3.shape, BF),
            pltpu.VMEM((rows, model), BF),
            *box(4, 4, 4),
            *box(4, 4),
            *box(4),
            *box(2, 3, 2, 4),
            *box(2, 3, 2),
            *box(3),
            pltpu.SemaphoreType.DMA((3,)),
            pltpu.SemaphoreType.DMA((2, 10)),
            pltpu.SemaphoreType.DMA,
            pltpu.SemaphoreType.DMA((3, 2, 2, 3, 2)),
            pltpu.SemaphoreType.DMA((3, 3, 2)),
        ],
        compiler_params=pltpu.CompilerParams(
            collective_id=1, has_side_effects=True, vmem_limit_bytes=62 * 1024 * 1024
        ),
        name="close",
    )(res, hidden, gz, q, k, noisy, grad, scale1, w3)


def on_device(
    noisy, clean, actions, levels, starts, w_qkv, w_out, noise_table, action_table, temps, out_grad
):
    tokens, model = noisy.shape[3:]
    rows = 2 * tokens
    t = lax.axis_index("tm")
    y, x, z = place(t)
    starts_all = lax.all_gather(starts.reshape(1), "tm", axis=0, tiled=True)
    w3 = w_qkv.transpose(1, 0, 2)

    def pick(table, index):
        return lax.dynamic_index_in_dim(table, index, 0, keepdims=False)

    action_mod = pick(action_table, actions[0, 0])
    clean_mod = noise_table[0] + action_mod
    mods = jnp.stack([pick(noise_table, levels[0, 0, j]) + action_mod for j in range(2)])

    def spread_rows(part):
        return jnp.broadcast_to(mods[:, None, part, :], (2, tokens, model)).reshape(rows, model)

    shift, scale, gate = spread_rows(0), spread_rows(1), spread_rows(2)

    clean_rows = clean.reshape(tokens, model).astype(F32)
    clean_hidden = (layer_norm(clean_rows) * (1.0 + clean_mod[1]) + clean_mod[0]).astype(BF)
    ckn = head_norm(dot(clean_hidden, w3[1], 1, 0)).astype(BF)
    cv = dot(clean_hidden, w3[2], 1, 0).astype(BF)

    noisy_rows = noisy.reshape(rows, model).astype(F32)
    grad_rows = out_grad.reshape(rows, model).astype(F32)

    def front(values):
        return (layer_norm(values) * (1.0 + scale) + shift).astype(BF)

    hidden = front(noisy_rows)
    q = dot(hidden, w3[0], 1, 0)
    k = dot(hidden, w3[1], 1, 0)
    v = dot(hidden, w3[2], 1, 0).astype(BF)
    qn = head_norm(q).astype(BF)
    kn = head_norm(k).astype(BF)
    grad_z = (gate * grad_rows).astype(BF)
    grad_mixed = dot(grad_z, w_out, 1, 1).astype(BF)

    kv, own = spread(ckn, cv, qn, kn, v, grad_mixed)
    slots = jnp.arange(8, dtype=jnp.int32)
    my_frames = (slots // 2) * 8 + x * 2 + slots % 2
    my_starts = starts_all.reshape(4, 4, 2)[:, x].reshape(8)
    temp = (pick(temps, y * 2 + z) / math.sqrt(HD)).reshape(1)
    res = attend(my_frames, my_starts, temp, kv, own)
    grad_noisy, total_g, total_o = close(
        res,
        hidden,
        grad_z,
        q,
        k,
        noisy.reshape(rows, model),
        out_grad.reshape(rows, model),
        1.0 + mods[:, 1, :],
        w3,
    )
    return (grad_noisy.reshape(noisy.shape), total_g.transpose(1, 0, 2), total_o)


def solution(mesh):
    in_specs = (
        P("dp", "tm", None, None, None),
        P("dp", "tm", None, None),
        P("dp", "tm"),
        P("dp", "tm", None),
        P("dp", "tm"),
        P(),
        P(),
        P(),
        P(),
        P(),
        P("dp", "tm", None, None, None),
    )
    out_specs = (P("dp", "tm", None, None, None), P("tm", None, "dp"), P("tm", "dp"))
    return jax.shard_map(
        on_device, mesh=mesh, in_specs=in_specs, out_specs=out_specs, check_vma=False
    )
```

```python
import functools
import math

import jax
import jax.numpy as jnp
from jax import lax
from jax.experimental import pallas as pl
from jax.experimental.pallas import tpu as pltpu
from jax.sharding import PartitionSpec as P

EPS = 1e-06
NEG = -1e30
MESH = pl.DeviceIdType.MESH
HEADS = 8
HD = 128
BF = jnp.bfloat16
F32 = jnp.float32
ANY = pl.BlockSpec(memory_space=pl.ANY)
LOG2E = 1.4426950408889634


def dot(left, right, left_dim, right_dim):
    return lax.dot_general(
        left, right, (((left_dim,), (right_dim,)), ((), ())), preferred_element_type=F32
    )


def lanes(start, size):
    return pl.ds(pl.multiple_of(start, 128), size)


def rows_of(start, size):
    return pl.ds(pl.multiple_of(start, size), size)


def wait_bytes(ref, sem):
    pltpu.make_async_copy(ref, ref, sem).wait()


def place(t):
    return t // 8, (t // 2) % 4, t % 2


def head_home(h, x):
    return ((h // 2) * 4 + x) * 2 + h % 2


def open_kernel(
    level, action, start, noisy, clean, grad, noise, acts, w3, w_out,
    kv, own, stretch, hidden, gz, q, k, scale1,
    clean_hidden, ckv, out, tile, w, wo,
    w_sems, kv_sems, x_sems, own_sems, start_sems, local_sems,
):
    t = lax.axis_index("tm")
    d = lax.axis_index("dp")
    y, x, zh = place(t)
    slot = y * 2 + zh
    loads = [
        pltpu.make_async_copy(w3.at[1], w.at[1], w_sems.at[1]),
        pltpu.make_async_copy(w3.at[2], w.at[2], w_sems.at[2]),
        pltpu.make_async_copy(w3.at[0], w.at[0], w_sems.at[0]),
        pltpu.make_async_copy(w_out, wo, w_sems.at[3]),
    ]
    for load in loads:
        load.start()

    def peer(h):
        return {"dp": d, "tm": head_home(h, x)}

    def beside(step):
        return {"dp": d, "tm": (y * 4 + (x + step) % 4) * 2 + zh}

    barrier = pltpu.get_barrier_semaphore()

    def greet(s, carry):
        pl.semaphore_signal(
            barrier, inc=1, device_id=peer((slot + s) % 8), device_id_type=MESH
        )
        return carry

    lax.fori_loop(1, 8, greet, 0)
    for step in (1, 2, 3):
        pl.semaphore_signal(barrier, inc=1, device_id=beside(step), device_id_type=MESH)

    def remote(src, dst, sems, device):
        return pltpu.make_async_remote_copy(
            src_ref=src,
            dst_ref=dst,
            send_sem=sems.at[0],
            recv_sem=sems.at[1],
            device_id=device,
            device_id_type=MESH,
        )

    def modulated(values, shift, scale):
        center = values - jnp.mean(values, axis=1, keepdims=True)
        factor = lax.rsqrt(jnp.mean(center * center, axis=1, keepdims=True) + EPS)
        return (center * factor * scale + shift).astype(BF)

    act = acts[action[0]]
    clean_shift = noise[0, 0:1, :] + act[0:1]
    clean_scale = 1.0 + (noise[1, 0:1, :] + act[1:2])

    def clean_rows(n, carry):
        cut = rows_of(n * 16, 16)
        clean_hidden[cut, :] = modulated(clean[cut, :].astype(F32), clean_shift, clean_scale)
        return carry

    lax.fori_loop(0, 8, clean_rows, 0, unroll=2)

    def normed(u):
        factor = lax.rsqrt(jnp.mean(u * u, axis=1, keepdims=True) + EPS)
        return (u * factor).astype(BF)

    def clean_keys(m, carry):
        u = dot(clean_hidden[...], w[1, :, lanes(m * 256, 256)], 1, 0)
        for i in range(2):
            ckv[2 * m + i, 0] = normed(u[:, i * HD : (i + 1) * HD])
        return carry

    def clean_vals(m, carry):
        u = dot(clean_hidden[...], w[2, :, lanes(m * 256, 256)], 1, 0).astype(BF)
        for i in range(2):
            ckv[2 * m + i, 1] = u[:, i * HD : (i + 1) * HD]
        return carry

    tile[...] = jnp.full((8, 128), start[0], jnp.int32)
    loads[0].wait()
    lax.fori_loop(0, 4, clean_keys, 0)
    loads[1].wait()
    lax.fori_loop(0, 4, clean_vals, 0)

    pl.semaphore_wait(barrier, 10)

    def send_kv(s, carry):
        h = (slot + s) % 8
        remote(ckv.at[h], kv.at[y, x, zh], kv_sems, peer(h)).start()
        remote(tile, stretch.at[slot], start_sems, peer(h)).start()
        return carry

    lax.fori_loop(1, 8, send_kv, 0)
    mine = [
        pltpu.make_async_copy(ckv.at[slot], kv.at[y, x, zh], local_sems.at[0]),
        pltpu.make_async_copy(tile, stretch.at[slot], local_sems.at[1]),
    ]
    for copy in mine:
        copy.start()

    for j in range(2):
        row = pl.ds(level[j], 1)
        shift = noise[0, row, :] + act[0:1]
        scale = 1.0 + (noise[1, row, :] + act[1:2])
        gate = noise[2, row, :] + act[2:3]
        scale1[j : j + 1, :] = scale

        def noisy_rows(n, carry):
            cut = rows_of((j * 8 + n) * 16, 16)
            hidden[cut, :] = modulated(noisy[cut, :].astype(F32), shift, scale)
            gz[cut, :] = (gate * grad[cut, :].astype(F32)).astype(BF)
            return carry

        lax.fori_loop(0, 8, noisy_rows, 0, unroll=2)

    loads[2].wait()
    loads[3].wait()

    def project(i, carry):
        m = (slot // 2 + 1 + i) % 4
        cut = lanes(m * 256, 256)
        uk = dot(hidden[...], w[1, :, cut], 1, 0)
        uv = dot(hidden[...], w[2, :, cut], 1, 0).astype(BF)
        uq = dot(hidden[...], w[0, :, cut], 1, 0)
        um = dot(gz[...], wo[rows_of(m * 256, 256), :], 1, 1).astype(BF)
        k[:, cut] = uk
        q[:, cut] = uq
        for a in range(2):
            part = slice(a * HD, (a + 1) * HD)
            out[2 * m + a, 0] = normed(uq[:, part])
            out[2 * m + a, 1] = normed(uk[:, part])
            out[2 * m + a, 2] = uv[:, part]
            out[2 * m + a, 3] = um[:, part]
        return carry

    def send_own(h):
        remote(out.at[h], own.at[slot], own_sems, peer(h)).start()

    def send_pair(i):
        m = (slot // 2 + 1 + i) % 4
        send_own(2 * m)
        send_own(2 * m + 1)

    project(0, 0)
    send_pair(0)
    for copy in mine:
        copy.wait()
    wait_bytes(ckv.at[pl.ds(0, 7)], kv_sems.at[1])
    for step in (1, 3, 2):
        remote(kv.at[:, x], kv.at[:, x], x_sems, beside(step)).start()

    def project_send(i, carry):
        project(i, carry)
        send_pair(i)
        return carry

    lax.fori_loop(1, 3, project_send, 0)
    project(3, 0)
    send_own(slot + 1 - 2 * (slot % 2))
    last = pltpu.make_async_copy(out.at[slot], own.at[slot], local_sems.at[2])
    last.start()
    last.wait()
    for way in (0, 1):
        wait_bytes(stretch.at[pl.ds(0, 7)], start_sems.at[way])
        wait_bytes(kv.at[:, pl.ds(0, 3)], x_sems.at[way])
        wait_bytes(own.at[pl.ds(0, 7)], own_sems.at[way])
    wait_bytes(ckv.at[pl.ds(0, 7)], kv_sems.at[0])


def open_up(level, action, start, noisy, clean, grad, noise, acts, w3, w_out):
    rows, model = noisy.shape
    tokens = clean.shape[0]
    width = w_out.shape[0]
    vmem = pl.BlockSpec(memory_space=pltpu.VMEM)
    smem = pl.BlockSpec(memory_space=pltpu.SMEM)
    return pl.pallas_call(
        open_kernel,
        out_shape=(
            jax.ShapeDtypeStruct((4, 4, 2, 2, tokens, HD), BF),
            jax.ShapeDtypeStruct((8, 4, rows, HD), BF),
            jax.ShapeDtypeStruct((8, 8, 128), jnp.int32),
            jax.ShapeDtypeStruct((rows, model), BF),
            jax.ShapeDtypeStruct((rows, model), BF),
            jax.ShapeDtypeStruct((rows, width), F32),
            jax.ShapeDtypeStruct((rows, width), F32),
            jax.ShapeDtypeStruct((2, model), F32),
        ),
        in_specs=[smem] * 3 + [vmem] * 5 + [ANY] * 2,
        out_specs=(ANY, ANY, ANY) + (vmem,) * 5,
        scratch_shapes=[
            pltpu.VMEM((tokens, model), BF),
            pltpu.VMEM((8, 2, tokens, HD), BF),
            pltpu.VMEM((8, 4, rows, HD), BF),
            pltpu.VMEM((8, 128), jnp.int32),
            pltpu.VMEM(w3.shape, BF),
            pltpu.VMEM(w_out.shape, BF),
            pltpu.SemaphoreType.DMA((4,)),
            pltpu.SemaphoreType.DMA((2,)),
            pltpu.SemaphoreType.DMA((2,)),
            pltpu.SemaphoreType.DMA((2,)),
            pltpu.SemaphoreType.DMA((2,)),
            pltpu.SemaphoreType.DMA((3,)),
        ],
        compiler_params=pltpu.CompilerParams(
            collective_id=0, has_side_effects=True, vmem_limit_bytes=60 * 1024 * 1024
        ),
        name="open",
    )(level, action, start, noisy, clean, grad, noise, acts, w3, w_out)


def attend_kernel(starts, temps, kv, own, out, s_scr):
    i = pl.program_id(0)
    y, x, zh = place(lax.axis_index("tm"))
    g = (i // 2) * 8 + x * 2 + i % 2
    st = starts[i]
    n = g - st
    rest = n % 4
    steps = n // 4
    first = st + rest
    scale = temps[y * 2 + zh] * (1.0 / math.sqrt(HD))
    c2 = scale * LOG2E
    q = own[0, 0]
    ko = own[0, 1]
    vo = own[0, 2]
    do = own[0, 3]
    h = HD
    near = jnp.minimum(st, 29)
    k_near = kv[pl.ds(near, 3), 0].reshape(3 * h, h)
    v_near = kv[pl.ds(near, 3), 1].reshape(3 * h, h)

    def keys(c, part):
        return kv[pl.ds(first + 4 * c, 4), part].reshape(4 * h, h)

    def widest(s):
        top = s[:, :h]
        for b in range(1, s.shape[1] // h):
            top = jnp.maximum(top, s[:, b * h : (b + 1) * h])
        return top

    def folded(p):
        total = p[:, :h]
        for b in range(1, p.shape[1] // h):
            total = total + p[:, b * h : (b + 1) * h]
        return total

    s_own = jnp.concatenate([dot(q[:h], ko[:h], 1, 1), dot(q[h:], ko[h:], 1, 1)], 0)
    s_near = dot(q, k_near, 1, 1)
    s_near = jnp.concatenate(
        [
            jnp.where(
                (near + b >= st) & (near + b < first), s_near[:, b * h : (b + 1) * h], NEG
            )
            for b in range(3)
        ],
        1,
    )

    def scores(c, top):
        s = dot(q, keys(c, 0), 1, 1)
        s_scr[c] = s
        return jnp.maximum(top, widest(s))

    top = lax.fori_loop(0, steps, scores, jnp.maximum(s_own, widest(s_near)))
    m2 = jnp.max(top, axis=1, keepdims=True) * c2

    p_own = jnp.exp2(s_own * c2 - m2)
    p_near = jnp.exp2(s_near * c2 - m2)
    pb_own = p_own.astype(BF)
    acc = jnp.concatenate([dot(pb_own[:h], vo[:h], 1, 0), dot(pb_own[h:], vo[h:], 1, 0)], 0)
    acc = acc + dot(p_near.astype(BF), v_near, 1, 0)

    def weigh(c, carry):
        acc, total = carry
        p = jnp.exp2(s_scr[c] * c2 - m2)
        s_scr[c] = p
        return acc + dot(p.astype(BF), keys(c, 1), 1, 0), total + folded(p)

    acc, total = lax.fori_loop(0, steps, weigh, (acc, p_own + folded(p_near)))
    inv = 1.0 / jnp.sum(total, axis=1, keepdims=True)
    mixed = acc * inv
    delta = jnp.sum(mixed * do.astype(F32), axis=1, keepdims=True)
    out[0, 0] = mixed.astype(BF)

    dp_own = jnp.concatenate([dot(do[:h], vo[:h], 1, 1), dot(do[h:], vo[h:], 1, 1)], 0)
    ds_own = p_own * (dp_own - delta)
    ds_near = (p_near * (dot(do, v_near, 1, 1) - delta)).astype(BF)
    db_own = ds_own.astype(BF)
    dq = jnp.concatenate([dot(db_own[:h], ko[:h], 1, 0), dot(db_own[h:], ko[h:], 1, 0)], 0)
    dq = dq + dot(ds_near, k_near, 1, 0)

    def pull(c, dq):
        ds = s_scr[c] * (dot(do, keys(c, 1), 1, 1) - delta)
        return dq + dot(ds.astype(BF), keys(c, 0), 1, 0)

    dq = lax.fori_loop(0, steps, pull, dq)
    out[0, 1] = (dq * (inv * scale)).astype(BF)
    dsn = (ds_own * (inv * scale)).astype(BF)
    pn = (p_own * inv).astype(BF)
    for j in range(2):
        cut = slice(j * h, (j + 1) * h)
        out[0, 2, cut] = dot(dsn[cut], q[cut], 0, 0).astype(BF)
        out[0, 3, cut] = dot(pn[cut], do[cut], 0, 0).astype(BF)


def attend(starts, temps, kv, own):
    rows = own.shape[2]
    smem = pl.BlockSpec(memory_space=pltpu.SMEM)
    return pl.pallas_call(
        attend_kernel,
        grid=(8,),
        out_shape=jax.ShapeDtypeStruct(own.shape, BF),
        in_specs=[
            smem,
            smem,
            pl.BlockSpec(kv.shape, lambda i: (0, 0, 0, 0)),
            pl.BlockSpec((1, 4, rows, HD), lambda i: (i, 0, 0, 0)),
        ],
        out_specs=pl.BlockSpec((1, 4, rows, HD), lambda i: (i, 0, 0, 0)),
        scratch_shapes=[pltpu.VMEM((8, rows, 4 * HD), F32)],
        compiler_params=pltpu.CompilerParams(vmem_limit_bytes=40 * 1024 * 1024),
        name="attend",
    )(starts, temps, kv, own)


ORDERS = (("x", "y", "z"), ("y", "z", "x"), ("z", "x", "y"))
UNITS = (5, 5, 6)
FIRST_UNIT = (0, 5, 10)


def stream_of(unit):
    k = 0 if unit < 5 else 1 if unit < 10 else 2
    return k, unit - FIRST_UNIT[k]


def close_kernel(
    res, hidden, gz, q, k, noisy, grad, scale1, w3,
    out_n, out_g, out_o,
    got, proj, ph, pm, pp, pz, w, gh,
    t0a, t0b, t0c, t1a, t1b, t1c, t2a, t2b, t2c, b0a, b0b, b0c, b1a, b1b, b1c, b2a, b2b, b2c,
    back_sems, swap_sems, w_sem, ring_sems, last_sems,
):
    t = lax.axis_index("tm")
    d = lax.axis_index("dp")
    y, x, zh = place(t)
    zl, core = d // 2, d % 2
    z = zh * 2 + zl
    slot = y * 2 + zh
    partner = {"dp": d + 1 - 2 * core, "tm": t}
    at = {"x": x, "y": y, "z": z}
    rows = hidden.shape[0]
    terms = ((t0a, t0b, t0c), (t1a, t1b, t1c), (t2a, t2b, t2c))
    boxes = ((b0a, b0b, b0c), (b1a, b1b, b1c), (b2a, b2b, b2c))

    def along(axis, step):
        c = dict(at)
        c[axis] = (c[axis] + step) % 4
        return {
            "dp": (c["z"] % 2) * 2 + core,
            "tm": (c["y"] * 4 + c["x"]) * 2 + c["z"] // 2,
        }

    load_w = pltpu.make_async_copy(w3, w, w_sem)
    load_w.start()
    barrier = pltpu.get_barrier_semaphore()

    def greet(s, carry):
        pl.semaphore_signal(
            barrier,
            inc=1,
            device_id={"dp": d, "tm": head_home((slot + s) % 8, x)},
            device_id_type=MESH,
        )
        return carry

    lax.fori_loop(1, 8, greet, 0)
    for axis in "xyz":
        for step in (1, 2, 3):
            pl.semaphore_signal(
                barrier, inc=1, device_id=along(axis, step), device_id_type=MESH
            )
    pl.semaphore_signal(barrier, inc=1, device_id=partner, device_id_type=MESH)
    pl.semaphore_wait(barrier, 17)

    def remote(src, dst, send_sem, recv_sem, device):
        return pltpu.make_async_remote_copy(
            src_ref=src,
            dst_ref=dst,
            send_sem=send_sem,
            recv_sem=recv_sem,
            device_id=device,
            device_id_type=MESH,
        )

    def send_back(s, carry):
        i = (slot + s) % 8
        remote(
            res.at[i], got.at[slot], back_sems.at[0], back_sems.at[1],
            {"dp": d, "tm": head_home(i, x)},
        ).start()
        return carry

    lax.fori_loop(1, 8, send_back, 0)
    own = pltpu.make_async_copy(res.at[slot], got.at[slot], back_sems.at[2])
    own.start()

    def swap(src, dst, part):
        copy = remote(src, dst, swap_sems.at[0, part], swap_sems.at[1, part], partner)
        copy.start()
        return copy

    other = 1 - core
    swaps = [swap(hidden, ph, 0)]
    for l in range(2):
        cut = lanes(l * 1024 + other * 512, 512)
        swaps.append(swap(gz.at[:, cut], pz.at[:, pl.ds(l * 512, 512)], 1 + l))

    own.wait()
    wait_bytes(got.at[pl.ds(0, 7)], back_sems.at[1])
    swaps.append(swap(got.at[:, 0], pm, 3))

    def norm_back(h, carry):
        for part, u_ref in ((0, q), (1, k)):
            u = u_ref[:, lanes(h * HD, HD)]
            factor = lax.rsqrt(jnp.mean(u * u, axis=1, keepdims=True) + EPS)
            hat = u * factor
            g = got[h, 1 + part].astype(F32)
            du = factor * (g - hat * jnp.mean(hat * g, axis=1, keepdims=True))
            proj[:, lanes(part * 1024 + h * HD, HD)] = du.astype(BF)
        proj[:, lanes(2048 + h * HD, HD)] = got[h, 3]
        return carry

    lax.fori_loop(0, 8, norm_back, 0)
    for l in range(2):
        for j in range(3):
            swaps.append(
                swap(
                    proj.at[:, lanes(j * 1024 + l * 512 + other * 256, 256)],
                    pp.at[:, pl.ds(l * 768 + j * 256, 256)],
                    4 + l * 3 + j,
                )
            )
    for copy in swaps:
        copy.wait_recv()

    def put(yb, xb, zb, unit, value):
        s, u = stream_of(unit)
        spot = {"x": xb, "y": yb, "z": zb}
        terms[0][s][spot[ORDERS[s][0]], spot[ORDERS[s][1]], spot[ORDERS[s][2]], u] = value

    def terms_of(yb, carry):
        cut = lanes(yb * 512, 512)
        left = jnp.concatenate([hidden[:, cut], ph[:, cut]], 0).T
        for l in range(2):
            for j in range(3):
                mine = proj[:, lanes(j * 1024 + l * 512 + core * 256, 256)]
                theirs = pp[:, l * 768 + j * 256 : l * 768 + (j + 1) * 256]
                right = jnp.concatenate([mine, theirs], 0)
                term = dot(left, right, 1, 0).astype(BF)
                for xb in range(4):
                    for hb in range(2):
                        for rg in range(4):
                            r = (xb * 2 + hb) * 64 + rg * 16
                            put(yb, xb, hb * 2 + l, j * 4 + rg, term[r : r + 16])
        left = jnp.concatenate(
            [
                jnp.concatenate([got[2 * yb, 0], got[2 * yb + 1, 0]], 1),
                jnp.concatenate([pm[2 * yb], pm[2 * yb + 1]], 1),
            ],
            0,
        ).T
        for l in range(2):
            mine = gz[:, lanes(l * 1024 + core * 512, 512)]
            right = jnp.concatenate([mine, pz[:, l * 512 : (l + 1) * 512]], 0)
            term = dot(left, right, 1, 0).astype(BF)
            for xb in range(4):
                for hb in range(2):
                    for rg in range(2):
                        for ch in range(2):
                            r = (xb * 2 + hb) * 32 + rg * 16
                            put(
                                yb, xb, hb * 2 + l, 12 + rg * 2 + ch,
                                term[r : r + 16, ch * 256 : (ch + 1) * 256],
                            )
        return carry

    lax.fori_loop(0, 4, terms_of, 0)

    travel = (pl.ds(0, 2), pl.ds(2, 2))

    def ring(s, level, way, part):
        axis = ORDERS[s][level]
        step = 1 if way == 0 else 3
        near, far = (at[axis] + step) % 4, (at[axis] + 2) % 4
        src = (
            terms[level][s].at[far, travel[way]],
            terms[level][s].at[near, travel[1 - way]],
            terms[level][s].at[near, travel[way]],
        )[part]
        sems = ring_sems.at[s, level, way, part]
        return remote(
            src, boxes[level][s].at[way, part], sems.at[0], sems.at[1], along(axis, step)
        )

    def ring_open(level, s):
        for part in range(2):
            for way in range(2):
                ring(s, level, way, part).start()

    def ring_middle(level, s):
        axis = ORDERS[s][level]
        for way in range(2):
            ring(s, level, way, 0).wait_recv()
            near = (at[axis] + (1 if way == 0 else 3)) % 4
            spot = terms[level][s].at[near, travel[way]]
            spot[...] = (
                spot[...].astype(F32) + boxes[level][s][way, 0].astype(F32)
            ).astype(BF)
            ring(s, level, way, 2).start()

    def ring_close(level, s):
        for way in range(2):
            ring(s, level, way, 1).wait_recv()
            ring(s, level, way, 2).wait_recv()
        mine = at[ORDERS[s][level]]
        box = boxes[level][s]
        for way in range(2):
            terms[level + 1][s][travel[way]] = (
                terms[level][s][mine, travel[way]].astype(F32)
                + box[way, 2].astype(F32)
                + box[1 - way, 1].astype(F32)
            ).astype(BF)

    for s in range(3):
        ring_open(0, s)

    load_w.wait()

    def pull_hidden(n, carry):
        cut = lanes(n * 512, 512)
        total = dot(proj[:, :1024], w[0, cut, :], 1, 1)
        total = total + dot(proj[:, 1024:2048], w[1, cut, :], 1, 1)
        total = total + dot(proj[:, 2048:], w[2, cut, :], 1, 1)
        gh[:, cut] = total.astype(BF)
        return carry

    lax.fori_loop(0, 4, pull_hidden, 0)
    for s in range(3):
        ring_middle(0, s)

    def norm_rows(n, carry):
        cut = rows_of(n * 16, 16)
        level = n // 8
        v = noisy[cut, :].astype(F32)
        center = v - jnp.mean(v, axis=1, keepdims=True)
        factor = lax.rsqrt(jnp.mean(center * center, axis=1, keepdims=True) + EPS)
        hat = center * factor
        g = gh[cut, :].astype(F32) * scale1[pl.ds(level, 1), :]
        dv = factor * (
            g
            - jnp.mean(g, axis=1, keepdims=True)
            - hat * jnp.mean(g * hat, axis=1, keepdims=True)
        )
        out_n[cut, :] = (dv + grad[cut, :].astype(F32)).astype(BF)
        return carry

    lax.fori_loop(0, rows // 16, norm_rows, 0)

    for s in range(3):
        ring_close(0, s)
        ring_open(1, s)
    for s in range(3):
        ring_middle(1, s)

    def last(s, step):
        axis = ORDERS[s][2]
        there = (at[axis] + step) % 4
        sems = last_sems.at[s, step - 1]
        return remote(
            terms[2][s].at[there], boxes[2][s].at[step - 1], sems.at[0], sems.at[1],
            along(axis, step),
        )

    for s in range(3):
        ring_close(1, s)
        for step in (1, 2, 3):
            last(s, step).start()
    for s in range(3):
        for step in (1, 2, 3):
            last(s, step).wait_recv()
        mine = at[ORDERS[s][2]]
        sums = terms[2][s][mine].astype(F32)
        for step in (1, 2, 3):
            sums = sums + boxes[2][s][step - 1].astype(F32)
        sums = sums.astype(BF)
        for u in range(UNITS[s]):
            unit = FIRST_UNIT[s] + u
            if unit < 12:
                j, rg = unit // 4, unit % 4
                out_g[j, rg * 16 : (rg + 1) * 16, :] = sums[u]
            else:
                rg, ch = (unit - 12) // 2, (unit - 12) % 2
                out_o[rg * 16 : (rg + 1) * 16, ch * 256 : (ch + 1) * 256] = sums[u]

    wait_bytes(got.at[pl.ds(0, 7)], back_sems.at[0])
    for copy in swaps:
        copy.wait_send()
    for s in range(3):
        for level in range(2):
            for way in range(2):
                for part in range(3):
                    ring(s, level, way, part).wait_send()
        for step in (1, 2, 3):
            last(s, step).wait_send()


def close(res, hidden, gz, q, k, noisy, grad, scale1, w3):
    rows, model = hidden.shape
    vmem = pl.BlockSpec(memory_space=pltpu.VMEM)

    def box(*shape):
        return [pltpu.VMEM(shape + (u, 16, 256), BF) for u in UNITS]

    return pl.pallas_call(
        close_kernel,
        out_shape=(
            jax.ShapeDtypeStruct((rows, model), BF),
            jax.ShapeDtypeStruct((3, 64, 256), BF),
            jax.ShapeDtypeStruct((32, 512), BF),
        ),
        in_specs=[ANY] + [vmem] * 7 + [ANY],
        out_specs=(vmem,) * 3,
        scratch_shapes=[
            pltpu.VMEM((8, 4, rows, HD), BF),
            pltpu.VMEM((rows, 3072), BF),
            pltpu.VMEM((rows, model), BF),
            pltpu.VMEM((8, rows, HD), BF),
            pltpu.VMEM((rows, 1536), BF),
            pltpu.VMEM((rows, 1024), BF),
            pltpu.VMEM(w3.shape, BF),
            pltpu.VMEM((rows, model), BF),
            *box(4, 4, 4),
            *box(4, 4),
            *box(4),
            *box(2, 3, 2, 4),
            *box(2, 3, 2),
            *box(3),
            pltpu.SemaphoreType.DMA((3,)),
            pltpu.SemaphoreType.DMA((2, 10)),
            pltpu.SemaphoreType.DMA,
            pltpu.SemaphoreType.DMA((3, 2, 2, 3, 2)),
            pltpu.SemaphoreType.DMA((3, 3, 2)),
        ],
        compiler_params=pltpu.CompilerParams(
            collective_id=1, has_side_effects=True, vmem_limit_bytes=62 * 1024 * 1024
        ),
        name="close",
    )(res, hidden, gz, q, k, noisy, grad, scale1, w3)


def on_device(
    noisy, clean, actions, levels, starts, w_qkv, w_out, noise_table, action_table, temps, out_grad
):
    tokens, model = noisy.shape[3:]
    rows = 2 * tokens
    w3 = w_qkv.transpose(1, 0, 2)
    noisy_rows = noisy.reshape(rows, model)
    grad_rows = out_grad.reshape(rows, model)
    kv, own, stretch, hidden, grad_z, q, k, scale1 = open_up(
        levels.reshape(2),
        actions.reshape(1),
        starts.reshape(1),
        noisy_rows,
        clean.reshape(tokens, model),
        grad_rows,
        noise_table.transpose(1, 0, 2),
        action_table,
        w3,
        w_out,
    )
    res = attend(stretch[:, 0, 0], temps, kv.reshape(32, 2, tokens, HD), own)
    grad_noisy, total_g, total_o = close(
        res, hidden, grad_z, q, k, noisy_rows, grad_rows, scale1, w3
    )
    return (grad_noisy.reshape(noisy.shape), total_g.transpose(1, 0, 2), total_o)


def solution(mesh):
    in_specs = (
        P("dp", "tm", None, None, None),
        P("dp", "tm", None, None),
        P("dp", "tm"),
        P("dp", "tm", None),
        P("dp", "tm"),
        P(),
        P(),
        P(),
        P(),
        P(),
        P("dp", "tm", None, None, None),
    )
    out_specs = (P("dp", "tm", None, None, None), P("tm", None, "dp"), P("tm", "dp"))
    return jax.shard_map(
        on_device, mesh=mesh, in_specs=in_specs, out_specs=out_specs, check_vma=False
    )
```

```python
import functools
import math

import jax
import jax.numpy as jnp
from jax import lax
from jax.experimental import pallas as pl
from jax.experimental.pallas import tpu as pltpu
from jax.sharding import PartitionSpec as P

EPS = 1e-06
NEG = -1e30
MESH = pl.DeviceIdType.MESH
HEADS = 8
HD = 128
BF = jnp.bfloat16
F32 = jnp.float32
ANY = pl.BlockSpec(memory_space=pl.ANY)
LOG2E = 1.4426950408889634


def dot(left, right, left_dim, right_dim):
    return lax.dot_general(
        left, right, (((left_dim,), (right_dim,)), ((), ())), preferred_element_type=F32
    )


def lanes(start, size):
    return pl.ds(pl.multiple_of(start, 128), size)


def rows_of(start, size):
    return pl.ds(pl.multiple_of(start, size), size)


def wait_bytes(ref, sem):
    pltpu.make_async_copy(ref, ref, sem).wait()


def place(t):
    return t // 8, (t // 2) % 4, t % 2


def head_home(h, x):
    return ((h // 2) * 4 + x) * 2 + h % 2


def open_kernel(
    level, action, start, noisy, clean, grad, noise, acts, w3, w_out,
    temps, got, hidden, gz, q, k, scale1,
    kv, own, stretch, clean_hidden, ckv, out, tile, w, wo, s_scr, res,
    w_sems, kv_sems, x_sems, own_sems, start_sems, local_sems, back_sems,
):
    t = lax.axis_index("tm")
    d = lax.axis_index("dp")
    y, x, zh = place(t)
    slot = y * 2 + zh
    loads = [
        pltpu.make_async_copy(w3.at[1], w.at[1], w_sems.at[1]),
        pltpu.make_async_copy(w3.at[2], w.at[2], w_sems.at[2]),
        pltpu.make_async_copy(w3.at[0], w.at[0], w_sems.at[0]),
        pltpu.make_async_copy(w_out, wo, w_sems.at[3]),
    ]
    for load in loads:
        load.start()

    def peer(h):
        return {"dp": d, "tm": head_home(h, x)}

    def beside(step):
        return {"dp": d, "tm": (y * 4 + (x + step) % 4) * 2 + zh}

    barrier = pltpu.get_barrier_semaphore()

    def greet(s, carry):
        pl.semaphore_signal(
            barrier, inc=1, device_id=peer((slot + s) % 8), device_id_type=MESH
        )
        return carry

    lax.fori_loop(1, 8, greet, 0)
    for step in (1, 2, 3):
        pl.semaphore_signal(barrier, inc=1, device_id=beside(step), device_id_type=MESH)

    def remote(src, dst, sems, device, arrived=1):
        return pltpu.make_async_remote_copy(
            src_ref=src,
            dst_ref=dst,
            send_sem=sems.at[0],
            recv_sem=sems.at[arrived],
            device_id=device,
            device_id_type=MESH,
        )

    def modulated(values, shift, scale):
        center = values - jnp.mean(values, axis=1, keepdims=True)
        factor = lax.rsqrt(jnp.mean(center * center, axis=1, keepdims=True) + EPS)
        return (center * factor * scale + shift).astype(BF)

    act = acts[action[0]]
    clean_shift = noise[0, 0:1, :] + act[0:1]
    clean_scale = 1.0 + (noise[1, 0:1, :] + act[1:2])

    def clean_rows(n, carry):
        cut = rows_of(n * 16, 16)
        clean_hidden[cut, :] = modulated(clean[cut, :].astype(F32), clean_shift, clean_scale)
        return carry

    lax.fori_loop(0, 8, clean_rows, 0, unroll=2)

    def normed(u):
        factor = lax.rsqrt(jnp.mean(u * u, axis=1, keepdims=True) + EPS)
        return (u * factor).astype(BF)

    def clean_keys(m, carry):
        u = dot(clean_hidden[...], w[1, :, lanes(m * 256, 256)], 1, 0)
        for i in range(2):
            ckv[2 * m + i, 0] = normed(u[:, i * HD : (i + 1) * HD])
        return carry

    def clean_vals(m, carry):
        u = dot(clean_hidden[...], w[2, :, lanes(m * 256, 256)], 1, 0).astype(BF)
        for i in range(2):
            ckv[2 * m + i, 1] = u[:, i * HD : (i + 1) * HD]
        return carry

    tile[...] = jnp.full((8, 128), start[0], jnp.int32)
    loads[0].wait()
    lax.fori_loop(0, 4, clean_keys, 0)
    loads[1].wait()
    lax.fori_loop(0, 4, clean_vals, 0)

    pl.semaphore_wait(barrier, 10)

    def send_kv(s, carry):
        h = (slot + s) % 8
        remote(ckv.at[h], kv.at[y, x, zh], kv_sems, peer(h)).start()
        remote(tile, stretch.at[slot], start_sems, peer(h)).start()
        return carry

    lax.fori_loop(1, 8, send_kv, 0)
    mine = [
        pltpu.make_async_copy(ckv.at[slot], kv.at[y, x, zh], local_sems.at[0]),
        pltpu.make_async_copy(tile, stretch.at[slot], local_sems.at[1]),
    ]
    for copy in mine:
        copy.start()

    for j in range(2):
        row = pl.ds(level[j], 1)
        shift = noise[0, row, :] + act[0:1]
        scale = 1.0 + (noise[1, row, :] + act[1:2])
        gate = noise[2, row, :] + act[2:3]
        scale1[j : j + 1, :] = scale

        def noisy_rows(n, carry):
            cut = rows_of((j * 8 + n) * 16, 16)
            hidden[cut, :] = modulated(noisy[cut, :].astype(F32), shift, scale)
            gz[cut, :] = (gate * grad[cut, :].astype(F32)).astype(BF)
            return carry

        lax.fori_loop(0, 8, noisy_rows, 0, unroll=2)

    loads[2].wait()
    loads[3].wait()

    def project(i, carry):
        m = (slot // 2 + 1 + i) % 4
        cut = lanes(m * 256, 256)
        uk = dot(hidden[...], w[1, :, cut], 1, 0)
        uv = dot(hidden[...], w[2, :, cut], 1, 0).astype(BF)
        uq = dot(hidden[...], w[0, :, cut], 1, 0)
        um = dot(gz[...], wo[rows_of(m * 256, 256), :], 1, 1).astype(BF)
        k[:, cut] = uk
        q[:, cut] = uq
        for a in range(2):
            part = slice(a * HD, (a + 1) * HD)
            out[2 * m + a, 0] = normed(uq[:, part])
            out[2 * m + a, 1] = normed(uk[:, part])
            out[2 * m + a, 2] = uv[:, part]
            out[2 * m + a, 3] = um[:, part]
        return carry

    def send_own(h, i):
        remote(out.at[h], own.at[slot], own_sems, peer(h), 1 + i).start()

    def send_pair(i):
        m = (slot // 2 + 1 + i) % 4
        send_own(2 * m, i)
        send_own(2 * m + 1, i)

    project(0, 0)
    send_pair(0)
    for copy in mine:
        copy.wait()
    wait_bytes(ckv.at[pl.ds(0, 7)], kv_sems.at[1])
    for step in (1, 3, 2):
        remote(kv.at[:, x], kv.at[:, x], x_sems, beside(step)).start()

    def project_send(i, carry):
        project(i, carry)
        send_pair(i)
        return carry

    lax.fori_loop(1, 3, project_send, 0)
    project(3, 0)
    sibling = slot + 1 - 2 * zh
    send_own(sibling, 3)
    last = pltpu.make_async_copy(out.at[slot], own.at[slot], local_sems.at[2])
    last.start()
    last.wait()
    wait_bytes(stretch.at[pl.ds(0, 7)], start_sems.at[1])
    wait_bytes(kv.at[:, pl.ds(0, 3)], x_sems.at[1])

    scale = temps[slot] * (1.0 / math.sqrt(HD))
    c2 = scale * LOG2E
    h = HD
    pair = (0, 1)

    def keys(c, part):
        return kv[c, :, :, part].reshape(8 * h, h)

    def both(left, right, left_dim, right_dim):
        return jnp.concatenate(
            [
                dot(left[:h], right[:h], left_dim, right_dim),
                dot(left[h:], right[h:], left_dim, right_dim),
            ],
            0,
        )

    def attend(row):
        at = [row * 2 + n for n in pair]
        g = [row * 8 + x * 2 + n for n in pair]
        st = [stretch[i, 0:1, :] for i in at]
        qs = [own[i, 0] for i in at]
        ks = [own[i, 1] for i in at]
        vs = [own[i, 2] for i in at]
        ds = [own[i, 3] for i in at]
        s_own = [both(qs[n], ks[n], 1, 1) for n in pair]
        top = list(s_own)
        for c in range(row + 1):
            for n in pair:
                s = dot(qs[n], keys(c, 0), 1, 1)
                for b in range(8):
                    f = c * 8 + b
                    seen = (st[n] <= f) & (f < g[n])
                    sb = s[:, b * h : (b + 1) * h] + jnp.where(seen, 0.0, NEG)
                    s_scr[n, c, :, b * h : (b + 1) * h] = sb
                    top[n] = jnp.maximum(top[n], sb)
        m2 = [jnp.max(top[n], axis=1, keepdims=True) * c2 for n in pair]
        p_own = [jnp.exp2(s_own[n] * c2 - m2[n]) for n in pair]
        acc = [both(p_own[n].astype(BF), vs[n], 1, 0) for n in pair]
        total = list(p_own)
        for c in range(row + 1):
            for n in pair:
                p = jnp.exp2(s_scr[n, c] * c2 - m2[n])
                s_scr[n, c] = p
                for b in range(8):
                    total[n] = total[n] + p[:, b * h : (b + 1) * h]
                acc[n] = acc[n] + dot(p.astype(BF), keys(c, 1), 1, 0)
        inv = [1.0 / jnp.sum(total[n], axis=1, keepdims=True) for n in pair]
        mixed = [acc[n] * inv[n] for n in pair]
        delta = [jnp.sum(mixed[n] * ds[n].astype(F32), axis=1, keepdims=True) for n in pair]
        ds_own = [p_own[n] * (both(ds[n], vs[n], 1, 1) - delta[n]) for n in pair]
        dq = [both(ds_own[n].astype(BF), ks[n], 1, 0) for n in pair]
        for c in range(row + 1):
            for n in pair:
                pull = s_scr[n, c] * (dot(ds[n], keys(c, 1), 1, 1) - delta[n])
                dq[n] = dq[n] + dot(pull.astype(BF), keys(c, 0), 1, 0)
        for n in pair:
            i = at[n]
            res[i, 0] = mixed[n].astype(BF)
            res[i, 1] = (dq[n] * (inv[n] * scale)).astype(BF)
            dsn = (ds_own[n] * (inv[n] * scale)).astype(BF)
            pn = (p_own[n] * inv[n]).astype(BF)
            for j in range(2):
                cut = slice(j * h, (j + 1) * h)
                res[i, 2, cut] = dot(dsn[cut], qs[n][cut], 0, 0).astype(BF)
                res[i, 3, cut] = dot(pn[cut], ds[n][cut], 0, 0).astype(BF)

    def send_back(i):
        remote(res.at[i], got.at[slot], back_sems, peer(i)).start()

    def attend_row(s, carry):
        row = (y + 3 - s) % 4

        @pl.when(s < 3)
        def _():
            wait_bytes(own.at[pl.ds(0, 2)], own_sems.at[1 + s])

        @pl.when(s == 3)
        def _():
            wait_bytes(own.at[0], own_sems.at[4])

        for r in range(4):

            @pl.when(row == r)
            def _():
                attend(r)

        @pl.when(s < 3)
        def _():
            send_back(2 * row)
            send_back(2 * row + 1)

        return carry

    lax.fori_loop(0, 4, attend_row, 0)
    send_back(sibling)
    keep = pltpu.make_async_copy(res.at[slot], got.at[slot], local_sems.at[2])
    keep.start()
    keep.wait()
    wait_bytes(stretch.at[pl.ds(0, 7)], start_sems.at[0])
    wait_bytes(kv.at[:, pl.ds(0, 3)], x_sems.at[0])
    wait_bytes(own.at[pl.ds(0, 7)], own_sems.at[0])
    wait_bytes(ckv.at[pl.ds(0, 7)], kv_sems.at[0])
    for way in (0, 1):
        wait_bytes(res.at[pl.ds(0, 7)], back_sems.at[way])


def open_up(level, action, start, noisy, clean, grad, noise, acts, w3, w_out, temps):
    rows, model = noisy.shape
    tokens = clean.shape[0]
    width = w_out.shape[0]
    vmem = pl.BlockSpec(memory_space=pltpu.VMEM)
    smem = pl.BlockSpec(memory_space=pltpu.SMEM)
    return pl.pallas_call(
        open_kernel,
        out_shape=(
            jax.ShapeDtypeStruct((8, 4, rows, HD), BF),
            jax.ShapeDtypeStruct((rows, model), BF),
            jax.ShapeDtypeStruct((rows, model), BF),
            jax.ShapeDtypeStruct((rows, width), F32),
            jax.ShapeDtypeStruct((rows, width), F32),
            jax.ShapeDtypeStruct((2, model), F32),
        ),
        in_specs=[smem] * 3 + [vmem] * 5 + [ANY] * 2 + [smem],
        out_specs=(ANY,) + (vmem,) * 5,
        scratch_shapes=[
            pltpu.VMEM((4, 4, 2, 2, tokens, HD), BF),
            pltpu.VMEM((8, 4, rows, HD), BF),
            pltpu.VMEM((8, 8, 128), jnp.int32),
            pltpu.VMEM((tokens, model), BF),
            pltpu.VMEM((8, 2, tokens, HD), BF),
            pltpu.VMEM((8, 4, rows, HD), BF),
            pltpu.VMEM((8, 128), jnp.int32),
            pltpu.VMEM(w3.shape, BF),
            pltpu.VMEM(w_out.shape, BF),
            pltpu.VMEM((2, 4, rows, 8 * HD), F32),
            pltpu.VMEM((8, 4, rows, HD), BF),
            pltpu.SemaphoreType.DMA((4,)),
            pltpu.SemaphoreType.DMA((2,)),
            pltpu.SemaphoreType.DMA((2,)),
            pltpu.SemaphoreType.DMA((5,)),
            pltpu.SemaphoreType.DMA((2,)),
            pltpu.SemaphoreType.DMA((3,)),
            pltpu.SemaphoreType.DMA((2,)),
        ],
        compiler_params=pltpu.CompilerParams(
            collective_id=0, has_side_effects=True, vmem_limit_bytes=60 * 1024 * 1024
        ),
        name="open",
    )(level, action, start, noisy, clean, grad, noise, acts, w3, w_out, temps)


ORDERS = (("x", "y", "z"), ("y", "z", "x"), ("z", "x", "y"))
UNITS = (5, 5, 6)
FIRST_UNIT = (0, 5, 10)


def stream_of(unit):
    k = 0 if unit < 5 else 1 if unit < 10 else 2
    return k, unit - FIRST_UNIT[k]


def close_kernel(
    got, hidden, gz, q, k, noisy, grad, scale1, w3,
    out_n, out_g, out_o,
    proj, ph, pm, pp, pz, w, gh,
    t0a, t0b, t0c, t1a, t1b, t1c, t2a, t2b, t2c, b0a, b0b, b0c, b1a, b1b, b1c, b2a, b2b, b2c,
    swap_sems, w_sem, ring_sems, last_sems,
):
    t = lax.axis_index("tm")
    d = lax.axis_index("dp")
    y, x, zh = place(t)
    zl, core = d // 2, d % 2
    z = zh * 2 + zl
    partner = {"dp": d + 1 - 2 * core, "tm": t}
    at = {"x": x, "y": y, "z": z}
    rows = hidden.shape[0]
    terms = ((t0a, t0b, t0c), (t1a, t1b, t1c), (t2a, t2b, t2c))
    boxes = ((b0a, b0b, b0c), (b1a, b1b, b1c), (b2a, b2b, b2c))

    def along(axis, step):
        c = dict(at)
        c[axis] = (c[axis] + step) % 4
        return {
            "dp": (c["z"] % 2) * 2 + core,
            "tm": (c["y"] * 4 + c["x"]) * 2 + c["z"] // 2,
        }

    load_w = pltpu.make_async_copy(w3, w, w_sem)
    load_w.start()
    barrier = pltpu.get_barrier_semaphore()

    for axis in "xyz":
        for step in (1, 2, 3):
            pl.semaphore_signal(
                barrier, inc=1, device_id=along(axis, step), device_id_type=MESH
            )
    pl.semaphore_signal(barrier, inc=1, device_id=partner, device_id_type=MESH)
    def remote(src, dst, send_sem, recv_sem, device):
        return pltpu.make_async_remote_copy(
            src_ref=src,
            dst_ref=dst,
            send_sem=send_sem,
            recv_sem=recv_sem,
            device_id=device,
            device_id_type=MESH,
        )

    def swap(src, dst, part):
        copy = remote(src, dst, swap_sems.at[0, part], swap_sems.at[1, part], partner)
        copy.start()
        return copy

    def norm_back(h, carry):
        for part, u_ref in ((0, q), (1, k)):
            u = u_ref[:, lanes(h * HD, HD)]
            factor = lax.rsqrt(jnp.mean(u * u, axis=1, keepdims=True) + EPS)
            hat = u * factor
            g = got[h, 1 + part].astype(F32)
            du = factor * (g - hat * jnp.mean(hat * g, axis=1, keepdims=True))
            proj[:, lanes(part * 1024 + h * HD, HD)] = du.astype(BF)
        proj[:, lanes(2048 + h * HD, HD)] = got[h, 3]
        return carry

    lax.fori_loop(0, 8, norm_back, 0)
    pl.semaphore_wait(barrier, 10)
    other = 1 - core
    swaps = [swap(hidden, ph, 0)]
    for l in range(2):
        cut = lanes(l * 1024 + other * 512, 512)
        swaps.append(swap(gz.at[:, cut], pz.at[:, pl.ds(l * 512, 512)], 1 + l))
    swaps.append(swap(got.at[:, 0], pm, 3))
    for l in range(2):
        for j in range(3):
            swaps.append(
                swap(
                    proj.at[:, lanes(j * 1024 + l * 512 + other * 256, 256)],
                    pp.at[:, pl.ds(l * 768 + j * 256, 256)],
                    4 + l * 3 + j,
                )
            )
    for copy in swaps:
        copy.wait_recv()

    def put(yb, xb, zb, unit, value):
        s, u = stream_of(unit)
        spot = {"x": xb, "y": yb, "z": zb}
        terms[0][s][spot[ORDERS[s][0]], spot[ORDERS[s][1]], spot[ORDERS[s][2]], u] = value

    def terms_of(yb, carry):
        cut = lanes(yb * 512, 512)
        left = jnp.concatenate([hidden[:, cut], ph[:, cut]], 0).T
        for l in range(2):
            for j in range(3):
                mine = proj[:, lanes(j * 1024 + l * 512 + core * 256, 256)]
                theirs = pp[:, l * 768 + j * 256 : l * 768 + (j + 1) * 256]
                right = jnp.concatenate([mine, theirs], 0)
                term = dot(left, right, 1, 0).astype(BF)
                for xb in range(4):
                    for hb in range(2):
                        for rg in range(4):
                            r = (xb * 2 + hb) * 64 + rg * 16
                            put(yb, xb, hb * 2 + l, j * 4 + rg, term[r : r + 16])
        left = jnp.concatenate(
            [
                jnp.concatenate([got[2 * yb, 0], got[2 * yb + 1, 0]], 1),
                jnp.concatenate([pm[2 * yb], pm[2 * yb + 1]], 1),
            ],
            0,
        ).T
        for l in range(2):
            mine = gz[:, lanes(l * 1024 + core * 512, 512)]
            right = jnp.concatenate([mine, pz[:, l * 512 : (l + 1) * 512]], 0)
            term = dot(left, right, 1, 0).astype(BF)
            for xb in range(4):
                for hb in range(2):
                    for rg in range(2):
                        for ch in range(2):
                            r = (xb * 2 + hb) * 32 + rg * 16
                            put(
                                yb, xb, hb * 2 + l, 12 + rg * 2 + ch,
                                term[r : r + 16, ch * 256 : (ch + 1) * 256],
                            )
        return carry

    lax.fori_loop(0, 4, terms_of, 0)

    travel = (pl.ds(0, 2), pl.ds(2, 2))

    def ring(s, level, way, part):
        axis = ORDERS[s][level]
        step = 1 if way == 0 else 3
        near, far = (at[axis] + step) % 4, (at[axis] + 2) % 4
        src = (
            terms[level][s].at[far, travel[way]],
            terms[level][s].at[near, travel[1 - way]],
            terms[level][s].at[near, travel[way]],
        )[part]
        sems = ring_sems.at[s, level, way, part]
        return remote(
            src, boxes[level][s].at[way, part], sems.at[0], sems.at[1], along(axis, step)
        )

    def ring_open(level, s):
        for part in range(2):
            for way in range(2):
                ring(s, level, way, part).start()

    def ring_middle(level, s):
        axis = ORDERS[s][level]
        for way in range(2):
            ring(s, level, way, 0).wait_recv()
            near = (at[axis] + (1 if way == 0 else 3)) % 4
            spot = terms[level][s].at[near, travel[way]]
            spot[...] = (
                spot[...].astype(F32) + boxes[level][s][way, 0].astype(F32)
            ).astype(BF)
            ring(s, level, way, 2).start()

    def ring_close(level, s):
        for way in range(2):
            ring(s, level, way, 1).wait_recv()
            ring(s, level, way, 2).wait_recv()
        mine = at[ORDERS[s][level]]
        box = boxes[level][s]
        for way in range(2):
            terms[level + 1][s][travel[way]] = (
                terms[level][s][mine, travel[way]].astype(F32)
                + box[way, 2].astype(F32)
                + box[1 - way, 1].astype(F32)
            ).astype(BF)

    for s in range(3):
        ring_open(0, s)

    load_w.wait()

    def pull_hidden(n, carry):
        cut = lanes(n * 512, 512)
        total = dot(proj[:, :1024], w[0, cut, :], 1, 1)
        total = total + dot(proj[:, 1024:2048], w[1, cut, :], 1, 1)
        total = total + dot(proj[:, 2048:], w[2, cut, :], 1, 1)
        gh[:, cut] = total.astype(BF)
        return carry

    lax.fori_loop(0, 4, pull_hidden, 0)
    for s in range(3):
        ring_middle(0, s)

    def norm_rows(n, carry):
        cut = rows_of(n * 16, 16)
        level = n // 8
        v = noisy[cut, :].astype(F32)
        center = v - jnp.mean(v, axis=1, keepdims=True)
        factor = lax.rsqrt(jnp.mean(center * center, axis=1, keepdims=True) + EPS)
        hat = center * factor
        g = gh[cut, :].astype(F32) * scale1[pl.ds(level, 1), :]
        dv = factor * (
            g
            - jnp.mean(g, axis=1, keepdims=True)
            - hat * jnp.mean(g * hat, axis=1, keepdims=True)
        )
        out_n[cut, :] = (dv + grad[cut, :].astype(F32)).astype(BF)
        return carry

    lax.fori_loop(0, rows // 16, norm_rows, 0)

    for s in range(3):
        ring_close(0, s)
        ring_open(1, s)
    for s in range(3):
        ring_middle(1, s)

    def last(s, step):
        axis = ORDERS[s][2]
        there = (at[axis] + step) % 4
        sems = last_sems.at[s, step - 1]
        return remote(
            terms[2][s].at[there], boxes[2][s].at[step - 1], sems.at[0], sems.at[1],
            along(axis, step),
        )

    for s in range(3):
        ring_close(1, s)
        for step in (1, 2, 3):
            last(s, step).start()
    for s in range(3):
        for step in (1, 2, 3):
            last(s, step).wait_recv()
        mine = at[ORDERS[s][2]]
        sums = terms[2][s][mine].astype(F32)
        for step in (1, 2, 3):
            sums = sums + boxes[2][s][step - 1].astype(F32)
        sums = sums.astype(BF)
        for u in range(UNITS[s]):
            unit = FIRST_UNIT[s] + u
            if unit < 12:
                j, rg = unit // 4, unit % 4
                out_g[j, rg * 16 : (rg + 1) * 16, :] = sums[u]
            else:
                rg, ch = (unit - 12) // 2, (unit - 12) % 2
                out_o[rg * 16 : (rg + 1) * 16, ch * 256 : (ch + 1) * 256] = sums[u]

    for copy in swaps:
        copy.wait_send()
    for s in range(3):
        for level in range(2):
            for way in range(2):
                for part in range(3):
                    ring(s, level, way, part).wait_send()
        for step in (1, 2, 3):
            last(s, step).wait_send()


def close(got, hidden, gz, q, k, noisy, grad, scale1, w3):
    rows, model = hidden.shape
    vmem = pl.BlockSpec(memory_space=pltpu.VMEM)

    def box(*shape):
        return [pltpu.VMEM(shape + (u, 16, 256), BF) for u in UNITS]

    return pl.pallas_call(
        close_kernel,
        out_shape=(
            jax.ShapeDtypeStruct((rows, model), BF),
            jax.ShapeDtypeStruct((3, 64, 256), BF),
            jax.ShapeDtypeStruct((32, 512), BF),
        ),
        in_specs=[vmem] * 8 + [ANY],
        out_specs=(vmem,) * 3,
        scratch_shapes=[
            pltpu.VMEM((rows, 3072), BF),
            pltpu.VMEM((rows, model), BF),
            pltpu.VMEM((8, rows, HD), BF),
            pltpu.VMEM((rows, 1536), BF),
            pltpu.VMEM((rows, 1024), BF),
            pltpu.VMEM(w3.shape, BF),
            pltpu.VMEM((rows, model), BF),
            *box(4, 4, 4),
            *box(4, 4),
            *box(4),
            *box(2, 3, 2, 4),
            *box(2, 3, 2),
            *box(3),
            pltpu.SemaphoreType.DMA((2, 10)),
            pltpu.SemaphoreType.DMA,
            pltpu.SemaphoreType.DMA((3, 2, 2, 3, 2)),
            pltpu.SemaphoreType.DMA((3, 3, 2)),
        ],
        compiler_params=pltpu.CompilerParams(
            collective_id=1, has_side_effects=True, vmem_limit_bytes=62 * 1024 * 1024
        ),
        name="close",
    )(got, hidden, gz, q, k, noisy, grad, scale1, w3)


def on_device(
    noisy, clean, actions, levels, starts, w_qkv, w_out, noise_table, action_table, temps, out_grad
):
    tokens, model = noisy.shape[3:]
    rows = 2 * tokens
    w3 = w_qkv.transpose(1, 0, 2)
    noisy_rows = noisy.reshape(rows, model)
    grad_rows = out_grad.reshape(rows, model)
    got, hidden, grad_z, q, k, scale1 = open_up(
        levels.reshape(2),
        actions.reshape(1),
        starts.reshape(1),
        noisy_rows,
        clean.reshape(tokens, model),
        grad_rows,
        noise_table.transpose(1, 0, 2),
        action_table,
        w3,
        w_out,
        temps,
    )
    grad_noisy, total_g, total_o = close(
        got, hidden, grad_z, q, k, noisy_rows, grad_rows, scale1, w3
    )
    return (grad_noisy.reshape(noisy.shape), total_g.transpose(1, 0, 2), total_o)


def solution(mesh):
    in_specs = (
        P("dp", "tm", None, None, None),
        P("dp", "tm", None, None),
        P("dp", "tm"),
        P("dp", "tm", None),
        P("dp", "tm"),
        P(),
        P(),
        P(),
        P(),
        P(),
        P("dp", "tm", None, None, None),
    )
    out_specs = (P("dp", "tm", None, None, None), P("tm", None, "dp"), P("tm", "dp"))
    return jax.shard_map(
        on_device, mesh=mesh, in_specs=in_specs, out_specs=out_specs, check_vma=False
    )
```

```python
import functools
import math

import jax
import jax.numpy as jnp
from jax import lax
from jax.experimental import pallas as pl
from jax.experimental.pallas import tpu as pltpu
from jax.sharding import PartitionSpec as P

EPS = 1e-06
NEG = -1e30
MESH = pl.DeviceIdType.MESH
HEADS = 8
HD = 128
BF = jnp.bfloat16
F32 = jnp.float32
ANY = pl.BlockSpec(memory_space=pl.ANY)
LOG2E = 1.4426950408889634


def dot(left, right, left_dim, right_dim):
    return lax.dot_general(
        left, right, (((left_dim,), (right_dim,)), ((), ())), preferred_element_type=F32
    )


def lanes(start, size):
    return pl.ds(pl.multiple_of(start, 128), size)


def rows_of(start, size):
    return pl.ds(pl.multiple_of(start, size), size)


def wait_bytes(ref, sem):
    pltpu.make_async_copy(ref, ref, sem).wait()


def place(t):
    return t // 8, (t // 2) % 4, t % 2


def head_home(h, x):
    return ((h // 2) * 4 + x) * 2 + h % 2


def open_kernel(
    level, action, start, noisy, clean, grad, noise, acts, w3, w_out,
    temps, got, hidden, gz, q, k, scale1, ph, pz,
    kv, own, stretch, clean_hidden, ckv, out, tile, w, wo, s_scr, res,
    w_sems, kv_sems, x_sems, own_sems, start_sems, local_sems, back_sems, swap_sems,
):
    t = lax.axis_index("tm")
    d = lax.axis_index("dp")
    y, x, zh = place(t)
    slot = y * 2 + zh
    loads = [
        pltpu.make_async_copy(w3.at[1], w.at[1], w_sems.at[1]),
        pltpu.make_async_copy(w3.at[2], w.at[2], w_sems.at[2]),
        pltpu.make_async_copy(w3.at[0], w.at[0], w_sems.at[0]),
        pltpu.make_async_copy(w_out, wo, w_sems.at[3]),
    ]
    for load in loads:
        load.start()

    def peer(h):
        return {"dp": d, "tm": head_home(h, x)}

    def beside(step):
        return {"dp": d, "tm": (y * 4 + (x + step) % 4) * 2 + zh}

    barrier = pltpu.get_barrier_semaphore()

    def greet(s, carry):
        pl.semaphore_signal(
            barrier, inc=1, device_id=peer((slot + s) % 8), device_id_type=MESH
        )
        return carry

    lax.fori_loop(1, 8, greet, 0)
    core = d % 2
    partner = {"dp": d + 1 - 2 * core, "tm": t}
    for device in (beside(1), beside(3), partner):
        pl.semaphore_signal(barrier, inc=1, device_id=device, device_id_type=MESH)

    def remote(src, dst, sems, device, arrived=1):
        return pltpu.make_async_remote_copy(
            src_ref=src,
            dst_ref=dst,
            send_sem=sems.at[0],
            recv_sem=sems.at[arrived],
            device_id=device,
            device_id_type=MESH,
        )

    def modulated(values, shift, scale):
        center = values - jnp.mean(values, axis=1, keepdims=True)
        factor = lax.rsqrt(jnp.mean(center * center, axis=1, keepdims=True) + EPS)
        return (center * factor * scale + shift).astype(BF)

    act = acts[action[0]]
    clean_shift = noise[0, 0:1, :] + act[0:1]
    clean_scale = 1.0 + (noise[1, 0:1, :] + act[1:2])

    def clean_rows(n, carry):
        cut = rows_of(n * 16, 16)
        clean_hidden[cut, :] = modulated(clean[cut, :].astype(F32), clean_shift, clean_scale)
        return carry

    lax.fori_loop(0, 8, clean_rows, 0, unroll=2)

    def normed(u):
        factor = lax.rsqrt(jnp.mean(u * u, axis=1, keepdims=True) + EPS)
        return (u * factor).astype(BF)

    def clean_keys(m, carry):
        u = dot(clean_hidden[...], w[1, :, lanes(m * 256, 256)], 1, 0)
        for i in range(2):
            ckv[2 * m + i, 0] = normed(u[:, i * HD : (i + 1) * HD])
        return carry

    def clean_vals(m, carry):
        u = dot(clean_hidden[...], w[2, :, lanes(m * 256, 256)], 1, 0).astype(BF)
        for i in range(2):
            ckv[2 * m + i, 1] = u[:, i * HD : (i + 1) * HD]
        return carry

    tile[...] = jnp.full((8, 128), start[0], jnp.int32)
    loads[0].wait()
    lax.fori_loop(0, 4, clean_keys, 0)
    loads[1].wait()
    lax.fori_loop(0, 4, clean_vals, 0)

    pl.semaphore_wait(barrier, 10)

    def send_kv(s, carry):
        h = (slot + s) % 8
        remote(ckv.at[h], kv.at[y, x, zh], kv_sems, peer(h)).start()
        remote(tile, stretch.at[slot], start_sems, peer(h)).start()
        return carry

    lax.fori_loop(1, 8, send_kv, 0)
    mine = [
        pltpu.make_async_copy(ckv.at[slot], kv.at[y, x, zh], local_sems.at[0]),
        pltpu.make_async_copy(tile, stretch.at[slot], local_sems.at[1]),
    ]
    for copy in mine:
        copy.start()

    for j in range(2):
        row = pl.ds(level[j], 1)
        shift = noise[0, row, :] + act[0:1]
        scale = 1.0 + (noise[1, row, :] + act[1:2])
        gate = noise[2, row, :] + act[2:3]
        scale1[j : j + 1, :] = scale

        def noisy_rows(n, carry):
            cut = rows_of((j * 8 + n) * 16, 16)
            hidden[cut, :] = modulated(noisy[cut, :].astype(F32), shift, scale)
            gz[cut, :] = (gate * grad[cut, :].astype(F32)).astype(BF)
            return carry

        lax.fori_loop(0, 8, noisy_rows, 0, unroll=2)

    swaps = [remote(hidden, ph, swap_sems.at[0], partner)]
    for l in range(2):
        cut = lanes(l * 1024 + (1 - core) * 512, 512)
        swaps.append(
            remote(gz.at[:, cut], pz.at[:, pl.ds(l * 512, 512)], swap_sems.at[1 + l], partner)
        )
    for copy in swaps:
        copy.start()
    loads[2].wait()
    loads[3].wait()

    def project(i, carry):
        m = (slot // 2 + 1 + i) % 4
        cut = lanes(m * 256, 256)
        uk = dot(hidden[...], w[1, :, cut], 1, 0)
        uv = dot(hidden[...], w[2, :, cut], 1, 0).astype(BF)
        uq = dot(hidden[...], w[0, :, cut], 1, 0)
        um = dot(gz[...], wo[rows_of(m * 256, 256), :], 1, 1).astype(BF)
        k[:, cut] = uk
        q[:, cut] = uq
        for a in range(2):
            part = slice(a * HD, (a + 1) * HD)
            out[2 * m + a, 0] = normed(uq[:, part])
            out[2 * m + a, 1] = normed(uk[:, part])
            out[2 * m + a, 2] = uv[:, part]
            out[2 * m + a, 3] = um[:, part]
        return carry

    def send_own(h, i):
        remote(out.at[h], own.at[slot], own_sems, peer(h), 1 + i).start()

    def send_pair(i):
        m = (slot // 2 + 1 + i) % 4
        send_own(2 * m, i)
        send_own(2 * m + 1, i)

    project(0, 0)
    send_pair(0)
    for copy in mine:
        copy.wait()
    wait_bytes(ckv.at[pl.ds(0, 7)], kv_sems.at[1])
    half = (pl.ds(0, 2), pl.ds(2, 2))

    def along_x(n):
        cut = half[(0, 1, 1, 0, 0, 1)[n]]
        whose = x if n < 4 else (x + (3 if n == 4 else 1)) % 4
        step = (1, 1, 3, 3, 1, 3)[n]
        return remote(kv.at[cut, whose], kv.at[cut, whose], x_sems.at[n], beside(step))

    for n in (0, 2, 1, 3):
        along_x(n).start()

    def project_send(i, carry):
        project(i, carry)
        send_pair(i)
        return carry

    lax.fori_loop(1, 3, project_send, 0)
    project(3, 0)
    sibling = slot + 1 - 2 * zh
    send_own(sibling, 3)
    last = pltpu.make_async_copy(out.at[slot], own.at[slot], local_sems.at[2])
    last.start()
    last.wait()
    for n in (0, 2):
        along_x(n).wait_recv()
        along_x(4 + n // 2).start()
    wait_bytes(stretch.at[pl.ds(0, 7)], start_sems.at[1])
    for n in (1, 3, 4, 5):
        along_x(n).wait_recv()

    scale = temps[slot] * (1.0 / math.sqrt(HD))
    c2 = scale * LOG2E
    h = HD
    pair = (0, 1)

    def keys(c, part):
        return kv[c, :, :, part].reshape(8 * h, h)

    def both(left, right, left_dim, right_dim):
        return jnp.concatenate(
            [
                dot(left[:h], right[:h], left_dim, right_dim),
                dot(left[h:], right[h:], left_dim, right_dim),
            ],
            0,
        )

    def attend(row):
        at = [row * 2 + n for n in pair]
        g = [row * 8 + x * 2 + n for n in pair]
        st = [stretch[i, 0:1, :] for i in at]
        qs = [own[i, 0] for i in at]
        ks = [own[i, 1] for i in at]
        vs = [own[i, 2] for i in at]
        ds = [own[i, 3] for i in at]
        s_own = [both(qs[n], ks[n], 1, 1) for n in pair]
        top = list(s_own)
        for c in range(row + 1):
            for n in pair:
                s = dot(qs[n], keys(c, 0), 1, 1)
                for b in range(8):
                    f = c * 8 + b
                    seen = (st[n] <= f) & (f < g[n])
                    sb = s[:, b * h : (b + 1) * h] + jnp.where(seen, 0.0, NEG)
                    s_scr[n, c, :, b * h : (b + 1) * h] = sb
                    top[n] = jnp.maximum(top[n], sb)
        m2 = [jnp.max(top[n], axis=1, keepdims=True) * c2 for n in pair]
        p_own = [jnp.exp2(s_own[n] * c2 - m2[n]) for n in pair]
        acc = [both(p_own[n].astype(BF), vs[n], 1, 0) for n in pair]
        total = list(p_own)
        for c in range(row + 1):
            for n in pair:
                p = jnp.exp2(s_scr[n, c] * c2 - m2[n])
                s_scr[n, c] = p
                for b in range(8):
                    total[n] = total[n] + p[:, b * h : (b + 1) * h]
                acc[n] = acc[n] + dot(p.astype(BF), keys(c, 1), 1, 0)
        inv = [1.0 / jnp.sum(total[n], axis=1, keepdims=True) for n in pair]
        mixed = [acc[n] * inv[n] for n in pair]
        delta = [jnp.sum(mixed[n] * ds[n].astype(F32), axis=1, keepdims=True) for n in pair]
        ds_own = [p_own[n] * (both(ds[n], vs[n], 1, 1) - delta[n]) for n in pair]
        dq = [both(ds_own[n].astype(BF), ks[n], 1, 0) for n in pair]
        for c in range(row + 1):
            for n in pair:
                pull = s_scr[n, c] * (dot(ds[n], keys(c, 1), 1, 1) - delta[n])
                dq[n] = dq[n] + dot(pull.astype(BF), keys(c, 0), 1, 0)
        for n in pair:
            i = at[n]
            res[i, 0] = mixed[n].astype(BF)
            res[i, 1] = (dq[n] * (inv[n] * scale)).astype(BF)
            dsn = (ds_own[n] * (inv[n] * scale)).astype(BF)
            pn = (p_own[n] * inv[n]).astype(BF)
            for j in range(2):
                cut = slice(j * h, (j + 1) * h)
                res[i, 2, cut] = dot(dsn[cut], qs[n][cut], 0, 0).astype(BF)
                res[i, 3, cut] = dot(pn[cut], ds[n][cut], 0, 0).astype(BF)

    def send_back(i):
        remote(res.at[i], got.at[slot], back_sems, peer(i)).start()

    def attend_row(s, carry):
        row = (y + 3 - s) % 4

        @pl.when(s < 3)
        def _():
            wait_bytes(own.at[pl.ds(0, 2)], own_sems.at[1 + s])

        @pl.when(s == 3)
        def _():
            wait_bytes(own.at[0], own_sems.at[4])

        for r in range(4):

            @pl.when(row == r)
            def _():
                attend(r)

        @pl.when(s < 3)
        def _():
            send_back(2 * row)
            send_back(2 * row + 1)

        return carry

    lax.fori_loop(0, 4, attend_row, 0)
    send_back(sibling)
    keep = pltpu.make_async_copy(res.at[slot], got.at[slot], local_sems.at[2])
    keep.start()
    keep.wait()
    wait_bytes(stretch.at[pl.ds(0, 7)], start_sems.at[0])
    for n in range(6):
        along_x(n).wait_send()
    for copy in swaps:
        copy.wait()
    wait_bytes(own.at[pl.ds(0, 7)], own_sems.at[0])
    wait_bytes(ckv.at[pl.ds(0, 7)], kv_sems.at[0])
    for way in (0, 1):
        wait_bytes(res.at[pl.ds(0, 7)], back_sems.at[way])


def open_up(level, action, start, noisy, clean, grad, noise, acts, w3, w_out, temps):
    rows, model = noisy.shape
    tokens = clean.shape[0]
    width = w_out.shape[0]
    vmem = pl.BlockSpec(memory_space=pltpu.VMEM)
    smem = pl.BlockSpec(memory_space=pltpu.SMEM)
    return pl.pallas_call(
        open_kernel,
        out_shape=(
            jax.ShapeDtypeStruct((8, 4, rows, HD), BF),
            jax.ShapeDtypeStruct((rows, model), BF),
            jax.ShapeDtypeStruct((rows, model), BF),
            jax.ShapeDtypeStruct((rows, width), F32),
            jax.ShapeDtypeStruct((rows, width), F32),
            jax.ShapeDtypeStruct((2, model), F32),
            jax.ShapeDtypeStruct((rows, model), BF),
            jax.ShapeDtypeStruct((rows, model // 2), BF),
        ),
        in_specs=[smem] * 3 + [vmem] * 5 + [ANY] * 2 + [smem],
        out_specs=(ANY,) + (vmem,) * 5 + (ANY, ANY),
        scratch_shapes=[
            pltpu.VMEM((4, 4, 2, 2, tokens, HD), BF),
            pltpu.VMEM((8, 4, rows, HD), BF),
            pltpu.VMEM((8, 8, 128), jnp.int32),
            pltpu.VMEM((tokens, model), BF),
            pltpu.VMEM((8, 2, tokens, HD), BF),
            pltpu.VMEM((8, 4, rows, HD), BF),
            pltpu.VMEM((8, 128), jnp.int32),
            pltpu.VMEM(w3.shape, BF),
            pltpu.VMEM(w_out.shape, BF),
            pltpu.VMEM((2, 4, rows, 8 * HD), F32),
            pltpu.VMEM((8, 4, rows, HD), BF),
            pltpu.SemaphoreType.DMA((4,)),
            pltpu.SemaphoreType.DMA((2,)),
            pltpu.SemaphoreType.DMA((6, 2)),
            pltpu.SemaphoreType.DMA((5,)),
            pltpu.SemaphoreType.DMA((2,)),
            pltpu.SemaphoreType.DMA((3,)),
            pltpu.SemaphoreType.DMA((2,)),
            pltpu.SemaphoreType.DMA((3, 2)),
        ],
        compiler_params=pltpu.CompilerParams(
            collective_id=0, has_side_effects=True, vmem_limit_bytes=60 * 1024 * 1024
        ),
        name="open",
    )(level, action, start, noisy, clean, grad, noise, acts, w3, w_out, temps)


ORDERS = (("x", "y", "z"), ("y", "z", "x"), ("z", "x", "y"))
UNITS = (11, 11, 10)
FIRST_UNIT = (0, 11, 22)


def stream_of(unit):
    k = unit // 11
    return k, unit - FIRST_UNIT[k]


def close_kernel(
    got, hidden, gz, q, k, scale1, ph, pz, noisy_all, grad_all, w3,
    out_n, out_g, out_o,
    noisy, grad, proj, pm, pp, w, gh,
    t0a, t0b, t0c, t1a, t1b, t1c, t2a, t2b, t2c, b0a, b0b, b0c, b1a, b1b, b1c, b2a, b2b, b2c,
    swap_sems, w_sem, ring_sems, last_sems,
):
    t = lax.axis_index("tm")
    d = lax.axis_index("dp")
    y, x, zh = place(t)
    zl, core = d // 2, d % 2
    z = zh * 2 + zl
    partner = {"dp": d + 1 - 2 * core, "tm": t}
    at = {"x": x, "y": y, "z": z}
    rows = hidden.shape[0]
    terms = ((t0a, t0b, t0c), (t1a, t1b, t1c), (t2a, t2b, t2c))
    boxes = ((b0a, b0b, b0c), (b1a, b1b, b1c), (b2a, b2b, b2c))

    def along(axis, step):
        c = dict(at)
        c[axis] = (c[axis] + step) % 4
        return {
            "dp": (c["z"] % 2) * 2 + core,
            "tm": (c["y"] * 4 + c["x"]) * 2 + c["z"] // 2,
        }

    loads = [
        pltpu.make_async_copy(w3, w, w_sem.at[0]),
        pltpu.make_async_copy(noisy_all, noisy, w_sem.at[1]),
        pltpu.make_async_copy(grad_all, grad, w_sem.at[2]),
    ]
    for load in loads:
        load.start()
    barrier = pltpu.get_barrier_semaphore()

    for axis in "xyz":
        for step in (1, 2, 3):
            pl.semaphore_signal(
                barrier, inc=1, device_id=along(axis, step), device_id_type=MESH
            )
    pl.semaphore_signal(barrier, inc=1, device_id=partner, device_id_type=MESH)
    def remote(src, dst, send_sem, recv_sem, device):
        return pltpu.make_async_remote_copy(
            src_ref=src,
            dst_ref=dst,
            send_sem=send_sem,
            recv_sem=recv_sem,
            device_id=device,
            device_id_type=MESH,
        )

    def swap(src, dst, part):
        copy = remote(src, dst, swap_sems.at[0, part], swap_sems.at[1, part], partner)
        copy.start()
        return copy

    def norm_back(h, carry):
        for part, u_ref in ((0, q), (1, k)):
            u = u_ref[:, lanes(h * HD, HD)]
            factor = lax.rsqrt(jnp.mean(u * u, axis=1, keepdims=True) + EPS)
            hat = u * factor
            g = got[h, 1 + part].astype(F32)
            du = factor * (g - hat * jnp.mean(hat * g, axis=1, keepdims=True))
            proj[:, lanes(part * 1024 + h * HD, HD)] = du.astype(BF)
        proj[:, lanes(2048 + h * HD, HD)] = got[h, 3]
        return carry

    lax.fori_loop(0, 8, norm_back, 0)
    pl.semaphore_wait(barrier, 10)
    other = 1 - core
    swaps = [swap(got.at[:, 0], pm, 0)]
    for l in range(2):
        for j in range(3):
            swaps.append(
                swap(
                    proj.at[:, lanes(j * 1024 + l * 512 + other * 256, 256)],
                    pp.at[:, pl.ds(l * 768 + j * 256, 256)],
                    1 + l * 3 + j,
                )
            )
    for copy in swaps:
        copy.wait_recv()

    def put(yb, xb, zb, unit, value):
        s, u = stream_of(unit)
        spot = {"x": xb, "y": yb, "z": zb}
        terms[0][s][spot[ORDERS[s][0]], spot[ORDERS[s][1]], spot[ORDERS[s][2]], u] = value

    def terms_of(n, carry):
        yb = ((y // 2 + 1 + n // 2) % 2) * 2 + (y + n % 2 + n // 2) % 2
        cut = lanes(yb * 512, 512)
        left = jnp.concatenate([hidden[:, cut], ph[:, cut]], 0).T
        for l in range(2):
            for j in range(3):
                mine = proj[:, lanes(j * 1024 + l * 512 + core * 256, 256)]
                theirs = pp[:, l * 768 + j * 256 : l * 768 + (j + 1) * 256]
                right = jnp.concatenate([mine, theirs], 0)
                term = dot(left, right, 1, 0).astype(BF)
                for xb in range(4):
                    for hb in range(2):
                        for rg in range(4):
                            r = (xb * 2 + hb) * 64 + rg * 16
                            for ch in range(2):
                                put(
                                    yb, xb, hb * 2 + l, (j * 4 + rg) * 2 + ch,
                                    term[r : r + 16, ch * 128 : (ch + 1) * 128],
                                )
        left = jnp.concatenate(
            [
                jnp.concatenate([got[2 * yb, 0], got[2 * yb + 1, 0]], 1),
                jnp.concatenate([pm[2 * yb], pm[2 * yb + 1]], 1),
            ],
            0,
        ).T
        for l in range(2):
            mine = gz[:, lanes(l * 1024 + core * 512, 512)]
            right = jnp.concatenate([mine, pz[:, l * 512 : (l + 1) * 512]], 0)
            term = dot(left, right, 1, 0).astype(BF)
            for xb in range(4):
                for hb in range(2):
                    for rg in range(2):
                        for ch in range(4):
                            r = (xb * 2 + hb) * 32 + rg * 16
                            put(
                                yb, xb, hb * 2 + l, 24 + rg * 4 + ch,
                                term[r : r + 16, ch * 128 : (ch + 1) * 128],
                            )

        @pl.when(n == 0)
        def _():
            ring(1, 0, 0, 0).start()
            ring(1, 0, 1, 0).start()

        @pl.when(n == 1)
        def _():
            for s in (0, 2):
                ring(s, 0, 0, 0).start()
                ring(s, 0, 1, 1).start()

        @pl.when((n == 1) & (y % 2 == 0) | (n == 2) & (y % 2 == 1))
        def _():
            ring(1, 0, 1, 1).start()

        @pl.when((n == 1) & (y % 2 == 1) | (n == 2) & (y % 2 == 0))
        def _():
            ring(1, 0, 0, 1).start()

        @pl.when(n == 3)
        def _():
            for s in (0, 2):
                ring(s, 0, 1, 0).start()
                ring(s, 0, 0, 1).start()

        return carry

    far_pair, near_pair = pl.ds((1 - y // 2) * 2, 2), pl.ds((y // 2) * 2, 2)

    def half(s, level, way):
        if level == 1 or s == 1:
            return (pl.ds(2 * way, 2),)
        cut = near_pair if way else far_pair
        return (cut,) if s == 0 else (slice(None), cut)

    def ring(s, level, way, part):
        axis = ORDERS[s][level]
        step = 1 if way == 0 else 3
        near, far = (at[axis] + step) % 4, (at[axis] + 2) % 4
        src = (
            terms[level][s].at[(far, *half(s, level, way))],
            terms[level][s].at[(near, *half(s, level, 1 - way))],
            terms[level][s].at[(near, *half(s, level, way))],
        )[part]
        sems = ring_sems.at[s, level, way, part]
        return remote(
            src, boxes[level][s].at[way, part], sems.at[0], sems.at[1], along(axis, step)
        )

    def ring_open(level, s):
        for part in range(2):
            for way in range(2):
                ring(s, level, way, part).start()

    def ring_middle(level, s):
        axis = ORDERS[s][level]
        for way in range(2):
            ring(s, level, way, 0).wait_recv()
            near = (at[axis] + (1 if way == 0 else 3)) % 4
            spot = terms[level][s].at[(near, *half(s, level, way))]
            spot[...] = (
                spot[...].astype(F32) + boxes[level][s][way, 0].astype(F32)
            ).astype(BF)
            ring(s, level, way, 2).start()

    def ring_close(level, s):
        for way in range(2):
            ring(s, level, way, 1).wait_recv()
            ring(s, level, way, 2).wait_recv()
        mine = at[ORDERS[s][level]]
        box = boxes[level][s]
        for way in range(2):
            cut = half(s, level, way)
            terms[level + 1][s][cut] = (
                terms[level][s][(mine, *cut)].astype(F32)
                + box[way, 2].astype(F32)
                + box[1 - way, 1].astype(F32)
            ).astype(BF)

    lax.fori_loop(0, 4, terms_of, 0)
    for load in loads:
        load.wait()

    def pull_hidden(n, carry):
        cut = lanes(n * 512, 512)
        total = dot(proj[:, :1024], w[0, cut, :], 1, 1)
        total = total + dot(proj[:, 1024:2048], w[1, cut, :], 1, 1)
        total = total + dot(proj[:, 2048:], w[2, cut, :], 1, 1)
        gh[:, cut] = total.astype(BF)
        return carry

    lax.fori_loop(0, 4, pull_hidden, 0)
    for s in range(3):
        ring_middle(0, s)

    def norm_rows(n, carry):
        cut = rows_of(n * 16, 16)
        level = n // 8
        v = noisy[cut, :].astype(F32)
        center = v - jnp.mean(v, axis=1, keepdims=True)
        factor = lax.rsqrt(jnp.mean(center * center, axis=1, keepdims=True) + EPS)
        hat = center * factor
        g = gh[cut, :].astype(F32) * scale1[pl.ds(level, 1), :]
        dv = factor * (
            g
            - jnp.mean(g, axis=1, keepdims=True)
            - hat * jnp.mean(g * hat, axis=1, keepdims=True)
        )
        out_n[cut, :] = (dv + grad[cut, :].astype(F32)).astype(BF)
        return carry

    lax.fori_loop(0, rows // 16, norm_rows, 0)

    for s in range(3):
        ring_close(0, s)
        ring_open(1, s)
    for s in range(3):
        ring_middle(1, s)

    def last(s, step):
        axis = ORDERS[s][2]
        there = (at[axis] + step) % 4
        sems = last_sems.at[s, step - 1]
        return remote(
            terms[2][s].at[there], boxes[2][s].at[step - 1], sems.at[0], sems.at[1],
            along(axis, step),
        )

    for s in range(3):
        ring_close(1, s)
        for step in (1, 2, 3):
            last(s, step).start()
    for s in range(3):
        for step in (1, 2, 3):
            last(s, step).wait_recv()
        mine = at[ORDERS[s][2]]
        sums = terms[2][s][mine].astype(F32)
        for step in (1, 2, 3):
            sums = sums + boxes[2][s][step - 1].astype(F32)
        sums = sums.astype(BF)
        for u in range(UNITS[s]):
            unit = FIRST_UNIT[s] + u
            if unit < 24:
                j, rg, ch = unit // 8, (unit // 2) % 4, unit % 2
                out_g[j, rg * 16 : (rg + 1) * 16, ch * 128 : (ch + 1) * 128] = sums[u]
            else:
                rg, ch = (unit - 24) // 4, unit % 4
                out_o[rg * 16 : (rg + 1) * 16, ch * 128 : (ch + 1) * 128] = sums[u]

    for copy in swaps:
        copy.wait_send()
    for s in range(3):
        for level in range(2):
            for way in range(2):
                for part in range(3):
                    ring(s, level, way, part).wait_send()
        for step in (1, 2, 3):
            last(s, step).wait_send()


def close(got, hidden, gz, q, k, scale1, ph, pz, noisy, grad, w3):
    rows, model = hidden.shape
    vmem = pl.BlockSpec(memory_space=pltpu.VMEM)

    def box(*shape):
        return [pltpu.VMEM(shape + (u, 16, 128), BF) for u in UNITS]

    return pl.pallas_call(
        close_kernel,
        out_shape=(
            jax.ShapeDtypeStruct((rows, model), BF),
            jax.ShapeDtypeStruct((3, 64, 256), BF),
            jax.ShapeDtypeStruct((32, 512), BF),
        ),
        in_specs=[vmem] * 8 + [ANY] * 3,
        out_specs=(vmem,) * 3,
        scratch_shapes=[
            pltpu.VMEM((rows, model), BF),
            pltpu.VMEM((rows, model), BF),
            pltpu.VMEM((rows, 3072), BF),
            pltpu.VMEM((8, rows, HD), BF),
            pltpu.VMEM((rows, 1536), BF),
            pltpu.VMEM(w3.shape, BF),
            pltpu.VMEM((rows, model), BF),
            *box(4, 4, 4),
            *box(4, 4),
            *box(4),
            *box(2, 3, 2, 4)[:2],
            box(2, 3, 4, 2)[2],
            *box(2, 3, 2),
            *box(3),
            pltpu.SemaphoreType.DMA((2, 7)),
            pltpu.SemaphoreType.DMA((3,)),
            pltpu.SemaphoreType.DMA((3, 2, 2, 3, 2)),
            pltpu.SemaphoreType.DMA((3, 3, 2)),
        ],
        compiler_params=pltpu.CompilerParams(
            collective_id=1, has_side_effects=True, vmem_limit_bytes=62 * 1024 * 1024
        ),
        name="close",
    )(got, hidden, gz, q, k, scale1, ph, pz, noisy, grad, w3)


def on_device(
    noisy, clean, actions, levels, starts, w_qkv, w_out, noise_table, action_table, temps, out_grad
):
    tokens, model = noisy.shape[3:]
    rows = 2 * tokens
    w3 = w_qkv.transpose(1, 0, 2)
    noisy_rows = noisy.reshape(rows, model)
    grad_rows = out_grad.reshape(rows, model)
    got, hidden, grad_z, q, k, scale1, ph, pz = open_up(
        levels.reshape(2),
        actions.reshape(1),
        starts.reshape(1),
        noisy_rows,
        clean.reshape(tokens, model),
        grad_rows,
        noise_table.transpose(1, 0, 2),
        action_table,
        w3,
        w_out,
        temps,
    )
    grad_noisy, total_g, total_o = close(
        got, hidden, grad_z, q, k, scale1, ph, pz, noisy_rows, grad_rows, w3
    )
    return (grad_noisy.reshape(noisy.shape), total_g.transpose(1, 0, 2), total_o)


def solution(mesh):
    in_specs = (
        P("dp", "tm", None, None, None),
        P("dp", "tm", None, None),
        P("dp", "tm"),
        P("dp", "tm", None),
        P("dp", "tm"),
        P(),
        P(),
        P(),
        P(),
        P(),
        P("dp", "tm", None, None, None),
    )
    out_specs = (P("dp", "tm", None, None, None), P("tm", None, "dp"), P("tm", "dp"))
    return jax.shard_map(
        on_device, mesh=mesh, in_specs=in_specs, out_specs=out_specs, check_vma=False
    )
```

```python
import functools
import math

import jax
import jax.numpy as jnp
from jax import lax
from jax.experimental import pallas as pl
from jax.experimental.pallas import tpu as pltpu
from jax.sharding import PartitionSpec as P

EPS = 1e-06
NEG = -1e30
MESH = pl.DeviceIdType.MESH
HEADS = 8
HD = 128
BF = jnp.bfloat16
F32 = jnp.float32
ANY = pl.BlockSpec(memory_space=pl.ANY)
LOG2E = 1.4426950408889634


def dot(left, right, left_dim, right_dim):
    return lax.dot_general(
        left, right, (((left_dim,), (right_dim,)), ((), ())), preferred_element_type=F32
    )


def lanes(start, size):
    return pl.ds(pl.multiple_of(start, 128), size)


def rows_of(start, size):
    return pl.ds(pl.multiple_of(start, size), size)


def wait_bytes(ref, sem):
    pltpu.make_async_copy(ref, ref, sem).wait()


def place(t):
    return t // 8, (t // 2) % 4, t % 2


def head_home(h, x):
    return ((h // 2) * 4 + x) * 2 + h % 2


def open_kernel(
    level, action, start, noisy_all, clean_all, grad_all, noise_all, acts_all, w3, w_out,
    temps, got, hidden_out, gz_out, q_out, k_out, scale_out, ph, pz,
    noisy, clean, grad, noise, acts, hidden, gz, q, k, scale1, kv, own, stretch, clean_hidden, ckv, out, tile, w, wo, s_scr, res,
    w_sems, kv_sems, x_sems, own_sems, start_sems, local_sems, back_sems, swap_sems, in_sems, out_sems,
):
    t = lax.axis_index("tm")
    d = lax.axis_index("dp")
    y, x, zh = place(t)
    slot = y * 2 + zh
    first = [
        pltpu.make_async_copy(clean_all, clean, in_sems.at[0]),
        pltpu.make_async_copy(noise_all, noise, in_sems.at[1]),
        pltpu.make_async_copy(acts_all, acts, in_sems.at[2]),
    ]
    loads = [
        pltpu.make_async_copy(w3.at[1], w.at[1], w_sems.at[1]),
        pltpu.make_async_copy(w3.at[2], w.at[2], w_sems.at[2]),
        pltpu.make_async_copy(w3.at[0], w.at[0], w_sems.at[0]),
        pltpu.make_async_copy(w_out, wo, w_sems.at[3]),
    ]
    second = [
        pltpu.make_async_copy(noisy_all, noisy, in_sems.at[3]),
        pltpu.make_async_copy(grad_all, grad, in_sems.at[4]),
    ]
    for load in first + loads[:2] + second + loads[2:]:
        load.start()

    def peer(h):
        return {"dp": d, "tm": head_home(h, x)}

    def beside(step):
        return {"dp": d, "tm": (y * 4 + (x + step) % 4) * 2 + zh}

    barrier = pltpu.get_barrier_semaphore()

    def greet(s, carry):
        pl.semaphore_signal(
            barrier, inc=1, device_id=peer((slot + s) % 8), device_id_type=MESH
        )
        return carry

    lax.fori_loop(1, 8, greet, 0)
    core = d % 2
    partner = {"dp": d + 1 - 2 * core, "tm": t}
    for device in (beside(1), beside(3), partner):
        pl.semaphore_signal(barrier, inc=1, device_id=device, device_id_type=MESH)

    def remote(src, dst, sems, device, arrived=1):
        return pltpu.make_async_remote_copy(
            src_ref=src,
            dst_ref=dst,
            send_sem=sems.at[0],
            recv_sem=sems.at[arrived],
            device_id=device,
            device_id_type=MESH,
        )

    def modulated(values, shift, scale):
        center = values - jnp.mean(values, axis=1, keepdims=True)
        factor = lax.rsqrt(jnp.mean(center * center, axis=1, keepdims=True) + EPS)
        return (center * factor * scale + shift).astype(BF)

    for load in first:
        load.wait()
    act = acts[action[0]]
    clean_shift = noise[0, 0:1, :] + act[0:1]
    clean_scale = 1.0 + (noise[1, 0:1, :] + act[1:2])

    def clean_rows(n, carry):
        cut = rows_of(n * 16, 16)
        clean_hidden[cut, :] = modulated(clean[cut, :].astype(F32), clean_shift, clean_scale)
        return carry

    lax.fori_loop(0, 8, clean_rows, 0, unroll=2)

    def normed(u):
        factor = lax.rsqrt(jnp.mean(u * u, axis=1, keepdims=True) + EPS)
        return (u * factor).astype(BF)

    def clean_keys(m, carry):
        u = dot(clean_hidden[...], w[1, :, lanes(m * 256, 256)], 1, 0)
        for i in range(2):
            ckv[2 * m + i, 0] = normed(u[:, i * HD : (i + 1) * HD])
        return carry

    def clean_vals(m, carry):
        u = dot(clean_hidden[...], w[2, :, lanes(m * 256, 256)], 1, 0).astype(BF)
        for i in range(2):
            ckv[2 * m + i, 1] = u[:, i * HD : (i + 1) * HD]
        return carry

    tile[...] = jnp.full((8, 128), start[0], jnp.int32)
    loads[0].wait()
    lax.fori_loop(0, 4, clean_keys, 0)
    loads[1].wait()
    lax.fori_loop(0, 4, clean_vals, 0)

    pl.semaphore_wait(barrier, 10)

    def send_kv(s, carry):
        h = (slot + s) % 8
        remote(ckv.at[h], kv.at[y, x, zh], kv_sems, peer(h)).start()
        remote(tile, stretch.at[slot], start_sems, peer(h)).start()
        return carry

    lax.fori_loop(1, 8, send_kv, 0)
    mine = [
        pltpu.make_async_copy(ckv.at[slot], kv.at[y, x, zh], local_sems.at[0]),
        pltpu.make_async_copy(tile, stretch.at[slot], local_sems.at[1]),
    ]
    for copy in mine:
        copy.start()

    for load in second:
        load.wait()
    for j in range(2):
        row = pl.ds(level[j], 1)
        shift = noise[0, row, :] + act[0:1]
        scale = 1.0 + (noise[1, row, :] + act[1:2])
        gate = noise[2, row, :] + act[2:3]
        scale1[j : j + 1, :] = scale

        def noisy_rows(n, carry):
            cut = rows_of((j * 8 + n) * 16, 16)
            hidden[cut, :] = modulated(noisy[cut, :].astype(F32), shift, scale)
            gz[cut, :] = (gate * grad[cut, :].astype(F32)).astype(BF)
            return carry

        lax.fori_loop(0, 8, noisy_rows, 0, unroll=2)

    swaps = [remote(hidden, ph, swap_sems.at[0], partner)]
    for l in range(2):
        cut = lanes(l * 1024 + (1 - core) * 512, 512)
        swaps.append(
            remote(gz.at[:, cut], pz.at[:, pl.ds(l * 512, 512)], swap_sems.at[1 + l], partner)
        )
    for copy in swaps:
        copy.start()
    results = [
        pltpu.make_async_copy(hidden, hidden_out, out_sems.at[0]),
        pltpu.make_async_copy(gz, gz_out, out_sems.at[1]),
        pltpu.make_async_copy(scale1, scale_out, out_sems.at[2]),
        pltpu.make_async_copy(q, q_out, out_sems.at[3]),
        pltpu.make_async_copy(k, k_out, out_sems.at[4]),
    ]
    for copy in results[:3]:
        copy.start()
    loads[2].wait()
    loads[3].wait()

    def project(i, carry):
        m = (slot // 2 + 1 + i) % 4
        cut = lanes(m * 256, 256)
        uk = dot(hidden[...], w[1, :, cut], 1, 0)
        uv = dot(hidden[...], w[2, :, cut], 1, 0).astype(BF)
        uq = dot(hidden[...], w[0, :, cut], 1, 0)
        um = dot(gz[...], wo[rows_of(m * 256, 256), :], 1, 1).astype(BF)
        k[:, cut] = uk
        q[:, cut] = uq
        for a in range(2):
            part = slice(a * HD, (a + 1) * HD)
            out[2 * m + a, 0] = normed(uq[:, part])
            out[2 * m + a, 1] = normed(uk[:, part])
            out[2 * m + a, 2] = uv[:, part]
            out[2 * m + a, 3] = um[:, part]
        return carry

    def send_own(h, i):
        remote(out.at[h], own.at[slot], own_sems, peer(h), 1 + i).start()

    def send_pair(i):
        m = (slot // 2 + 1 + i) % 4
        send_own(2 * m, i)
        send_own(2 * m + 1, i)

    project(0, 0)
    send_pair(0)
    for copy in mine:
        copy.wait()
    wait_bytes(ckv.at[pl.ds(0, 7)], kv_sems.at[1])
    half = (pl.ds(0, 2), pl.ds(2, 2))

    def along_x(n):
        cut = half[(0, 1, 1, 0, 0, 1)[n]]
        whose = x if n < 4 else (x + (3 if n == 4 else 1)) % 4
        step = (1, 1, 3, 3, 1, 3)[n]
        return remote(kv.at[cut, whose], kv.at[cut, whose], x_sems.at[n], beside(step))

    for n in (0, 2, 1, 3):
        along_x(n).start()

    def project_send(i, carry):
        project(i, carry)
        send_pair(i)
        return carry

    lax.fori_loop(1, 3, project_send, 0)
    project(3, 0)
    sibling = slot + 1 - 2 * zh
    send_own(sibling, 3)
    last = pltpu.make_async_copy(out.at[slot], own.at[slot], local_sems.at[2])
    last.start()
    for copy in results[3:]:
        copy.start()
    last.wait()
    for n in (0, 2):
        along_x(n).wait_recv()
        along_x(4 + n // 2).start()
    wait_bytes(stretch.at[pl.ds(0, 7)], start_sems.at[1])
    for n in (1, 3, 4, 5):
        along_x(n).wait_recv()

    scale = temps[slot] * (1.0 / math.sqrt(HD))
    c2 = scale * LOG2E
    h = HD
    pair = (0, 1)

    def keys(c, part):
        return kv[c, :, :, part].reshape(8 * h, h)

    def both(left, right, left_dim, right_dim):
        return jnp.concatenate(
            [
                dot(left[:h], right[:h], left_dim, right_dim),
                dot(left[h:], right[h:], left_dim, right_dim),
            ],
            0,
        )

    def attend(row):
        at = [row * 2 + n for n in pair]
        g = [row * 8 + x * 2 + n for n in pair]
        st = [stretch[i, 0:1, :] for i in at]
        qs = [own[i, 0] for i in at]
        ks = [own[i, 1] for i in at]
        vs = [own[i, 2] for i in at]
        ds = [own[i, 3] for i in at]
        s_own = [both(qs[n], ks[n], 1, 1) for n in pair]
        top = list(s_own)
        for c in range(row + 1):
            for n in pair:
                s = dot(qs[n], keys(c, 0), 1, 1)
                for b in range(8):
                    f = c * 8 + b
                    seen = (st[n] <= f) & (f < g[n])
                    sb = s[:, b * h : (b + 1) * h] + jnp.where(seen, 0.0, NEG)
                    s_scr[n, c, :, b * h : (b + 1) * h] = sb
                    top[n] = jnp.maximum(top[n], sb)
        m2 = [jnp.max(top[n], axis=1, keepdims=True) * c2 for n in pair]
        p_own = [jnp.exp2(s_own[n] * c2 - m2[n]) for n in pair]
        acc = [both(p_own[n].astype(BF), vs[n], 1, 0) for n in pair]
        total = list(p_own)
        for c in range(row + 1):
            for n in pair:
                p = jnp.exp2(s_scr[n, c] * c2 - m2[n])
                s_scr[n, c] = p
                for b in range(8):
                    total[n] = total[n] + p[:, b * h : (b + 1) * h]
                acc[n] = acc[n] + dot(p.astype(BF), keys(c, 1), 1, 0)
        inv = [1.0 / jnp.sum(total[n], axis=1, keepdims=True) for n in pair]
        mixed = [acc[n] * inv[n] for n in pair]
        delta = [jnp.sum(mixed[n] * ds[n].astype(F32), axis=1, keepdims=True) for n in pair]
        ds_own = [p_own[n] * (both(ds[n], vs[n], 1, 1) - delta[n]) for n in pair]
        dq = [both(ds_own[n].astype(BF), ks[n], 1, 0) for n in pair]
        for c in range(row + 1):
            for n in pair:
                pull = s_scr[n, c] * (dot(ds[n], keys(c, 1), 1, 1) - delta[n])
                dq[n] = dq[n] + dot(pull.astype(BF), keys(c, 0), 1, 0)
        for n in pair:
            i = at[n]
            res[i, 0] = mixed[n].astype(BF)
            res[i, 1] = (dq[n] * (inv[n] * scale)).astype(BF)
            dsn = (ds_own[n] * (inv[n] * scale)).astype(BF)
            pn = (p_own[n] * inv[n]).astype(BF)
            for j in range(2):
                cut = slice(j * h, (j + 1) * h)
                res[i, 2, cut] = dot(dsn[cut], qs[n][cut], 0, 0).astype(BF)
                res[i, 3, cut] = dot(pn[cut], ds[n][cut], 0, 0).astype(BF)

    def send_back(i):
        remote(res.at[i], got.at[slot], back_sems, peer(i)).start()

    def attend_row(s, carry):
        row = (y + 3 - s) % 4

        @pl.when(s < 3)
        def _():
            wait_bytes(own.at[pl.ds(0, 2)], own_sems.at[1 + s])

        @pl.when(s == 3)
        def _():
            wait_bytes(own.at[0], own_sems.at[4])

        for r in range(4):

            @pl.when(row == r)
            def _():
                attend(r)

        @pl.when(s < 3)
        def _():
            send_back(2 * row)
            send_back(2 * row + 1)

        return carry

    lax.fori_loop(0, 4, attend_row, 0)
    send_back(sibling)
    keep = pltpu.make_async_copy(res.at[slot], got.at[slot], local_sems.at[2])
    keep.start()
    keep.wait()
    wait_bytes(stretch.at[pl.ds(0, 7)], start_sems.at[0])
    for n in range(6):
        along_x(n).wait_send()
    for copy in swaps + results:
        copy.wait()
    wait_bytes(own.at[pl.ds(0, 7)], own_sems.at[0])
    wait_bytes(ckv.at[pl.ds(0, 7)], kv_sems.at[0])
    for way in (0, 1):
        wait_bytes(res.at[pl.ds(0, 7)], back_sems.at[way])


def open_up(level, action, start, noisy, clean, grad, noise, acts, w3, w_out, temps):
    rows, model = noisy.shape
    tokens = clean.shape[0]
    width = w_out.shape[0]
    smem = pl.BlockSpec(memory_space=pltpu.SMEM)
    return pl.pallas_call(
        open_kernel,
        out_shape=(
            jax.ShapeDtypeStruct((8, 4, rows, HD), BF),
            jax.ShapeDtypeStruct((rows, model), BF),
            jax.ShapeDtypeStruct((rows, model), BF),
            jax.ShapeDtypeStruct((rows, width), F32),
            jax.ShapeDtypeStruct((rows, width), F32),
            jax.ShapeDtypeStruct((2, model), F32),
            jax.ShapeDtypeStruct((rows, model), BF),
            jax.ShapeDtypeStruct((rows, model // 2), BF),
        ),
        in_specs=[smem] * 3 + [ANY] * 7 + [smem],
        out_specs=(ANY,) * 8,
        scratch_shapes=[
            pltpu.VMEM(noisy.shape, BF),
            pltpu.VMEM(clean.shape, BF),
            pltpu.VMEM(grad.shape, BF),
            pltpu.VMEM(noise.shape, F32),
            pltpu.VMEM(acts.shape, F32),
            pltpu.VMEM((rows, model), BF),
            pltpu.VMEM((rows, model), BF),
            pltpu.VMEM((rows, width), F32),
            pltpu.VMEM((rows, width), F32),
            pltpu.VMEM((2, model), F32),
            pltpu.VMEM((4, 4, 2, 2, tokens, HD), BF),
            pltpu.VMEM((8, 4, rows, HD), BF),
            pltpu.VMEM((8, 8, 128), jnp.int32),
            pltpu.VMEM((tokens, model), BF),
            pltpu.VMEM((8, 2, tokens, HD), BF),
            pltpu.VMEM((8, 4, rows, HD), BF),
            pltpu.VMEM((8, 128), jnp.int32),
            pltpu.VMEM(w3.shape, BF),
            pltpu.VMEM(w_out.shape, BF),
            pltpu.VMEM((2, 4, rows, 8 * HD), F32),
            pltpu.VMEM((8, 4, rows, HD), BF),
            pltpu.SemaphoreType.DMA((4,)),
            pltpu.SemaphoreType.DMA((2,)),
            pltpu.SemaphoreType.DMA((6, 2)),
            pltpu.SemaphoreType.DMA((5,)),
            pltpu.SemaphoreType.DMA((2,)),
            pltpu.SemaphoreType.DMA((3,)),
            pltpu.SemaphoreType.DMA((2,)),
            pltpu.SemaphoreType.DMA((3, 2)),
            pltpu.SemaphoreType.DMA((5,)),
            pltpu.SemaphoreType.DMA((5,)),
        ],
        compiler_params=pltpu.CompilerParams(
            collective_id=0, has_side_effects=True, vmem_limit_bytes=60 * 1024 * 1024
        ),
        name="open",
    )(level, action, start, noisy, clean, grad, noise, acts, w3, w_out, temps)


ORDERS = (("x", "y", "z"), ("y", "z", "x"), ("z", "x", "y"))
UNITS = (11, 11, 10)
FIRST_UNIT = (0, 11, 22)


def stream_of(unit):
    k = unit // 11
    return k, unit - FIRST_UNIT[k]


def close_kernel(
    got_all, q_all, k_all, hidden_all, gz_all, ph_all, pz_all, scale_all, noisy_all, grad_all, w3,
    out_n, out_g, out_o,
    got, q, k, hidden, gz, ph, pz, scale1, noisy, grad, proj, pm, pp, w, gh,
    t0a, t0b, t0c, t1a, t1b, t1c, t2a, t2b, t2c, b0a, b0b, b0c, b1a, b1b, b1c, b2a, b2b, b2c,
    swap_sems, w_sem, ring_sems, last_sems,
):
    t = lax.axis_index("tm")
    d = lax.axis_index("dp")
    y, x, zh = place(t)
    zl, core = d // 2, d % 2
    z = zh * 2 + zl
    partner = {"dp": d + 1 - 2 * core, "tm": t}
    at = {"x": x, "y": y, "z": z}
    rows = hidden.shape[0]
    terms = ((t0a, t0b, t0c), (t1a, t1b, t1c), (t2a, t2b, t2c))
    boxes = ((b0a, b0b, b0c), (b1a, b1b, b1c), (b2a, b2b, b2c))

    def along(axis, step):
        c = dict(at)
        c[axis] = (c[axis] + step) % 4
        return {
            "dp": (c["z"] % 2) * 2 + core,
            "tm": (c["y"] * 4 + c["x"]) * 2 + c["z"] // 2,
        }

    sources = (
        got_all, q_all, k_all, hidden_all, gz_all, ph_all, pz_all, scale_all, noisy_all, grad_all, w3,
    )
    places = (got, q, k, hidden, gz, ph, pz, scale1, noisy, grad, w)
    loads = [
        pltpu.make_async_copy(source, spot, w_sem.at[n])
        for n, (source, spot) in enumerate(zip(sources, places, strict=True))
    ]
    for load in loads:
        load.start()
    barrier = pltpu.get_barrier_semaphore()

    for axis in "xyz":
        for step in (1, 2, 3):
            pl.semaphore_signal(
                barrier, inc=1, device_id=along(axis, step), device_id_type=MESH
            )
    pl.semaphore_signal(barrier, inc=1, device_id=partner, device_id_type=MESH)
    def remote(src, dst, send_sem, recv_sem, device):
        return pltpu.make_async_remote_copy(
            src_ref=src,
            dst_ref=dst,
            send_sem=send_sem,
            recv_sem=recv_sem,
            device_id=device,
            device_id_type=MESH,
        )

    def swap(src, dst, part):
        copy = remote(src, dst, swap_sems.at[0, part], swap_sems.at[1, part], partner)
        copy.start()
        return copy

    def norm_back(h, carry):
        for part, u_ref in ((0, q), (1, k)):
            u = u_ref[:, lanes(h * HD, HD)]
            factor = lax.rsqrt(jnp.mean(u * u, axis=1, keepdims=True) + EPS)
            hat = u * factor
            g = got[h, 1 + part].astype(F32)
            du = factor * (g - hat * jnp.mean(hat * g, axis=1, keepdims=True))
            proj[:, lanes(part * 1024 + h * HD, HD)] = du.astype(BF)
        proj[:, lanes(2048 + h * HD, HD)] = got[h, 3]
        return carry

    for load in loads[:3]:
        load.wait()
    other = 1 - core
    swaps = []
    for l in range(2):
        lax.fori_loop(0, 2, lambda i, c: norm_back(l * 4 + other * 2 + i, c), 0)
        if l == 0:
            pl.semaphore_wait(barrier, 10)
            swaps.append(swap(got.at[:, 0], pm, 0))
        for j in range(3):
            swaps.append(
                swap(
                    proj.at[:, lanes(j * 1024 + l * 512 + other * 256, 256)],
                    pp.at[:, pl.ds(l * 768 + j * 256, 256)],
                    1 + l * 3 + j,
                )
            )
    for l in range(2):
        lax.fori_loop(0, 2, lambda i, c: norm_back(l * 4 + core * 2 + i, c), 0)
    for load in loads[3:7]:
        load.wait()
    for copy in swaps:
        copy.wait_recv()

    def put(yb, xb, zb, unit, value):
        s, u = stream_of(unit)
        spot = {"x": xb, "y": yb, "z": zb}
        terms[0][s][spot[ORDERS[s][0]], spot[ORDERS[s][1]], spot[ORDERS[s][2]], u] = value

    def terms_of(n, carry):
        yb = ((y // 2 + 1 + n // 2) % 2) * 2 + (y + n % 2 + n // 2) % 2
        cut = lanes(yb * 512, 512)
        left = jnp.concatenate([hidden[:, cut], ph[:, cut]], 0).T
        for l in range(2):
            for j in range(3):
                mine = proj[:, lanes(j * 1024 + l * 512 + core * 256, 256)]
                theirs = pp[:, l * 768 + j * 256 : l * 768 + (j + 1) * 256]
                right = jnp.concatenate([mine, theirs], 0)
                term = dot(left, right, 1, 0).astype(BF)
                for xb in range(4):
                    for hb in range(2):
                        for rg in range(4):
                            r = (xb * 2 + hb) * 64 + rg * 16
                            for ch in range(2):
                                put(
                                    yb, xb, hb * 2 + l, (j * 4 + rg) * 2 + ch,
                                    term[r : r + 16, ch * 128 : (ch + 1) * 128],
                                )
        left = jnp.concatenate(
            [
                jnp.concatenate([got[2 * yb, 0], got[2 * yb + 1, 0]], 1),
                jnp.concatenate([pm[2 * yb], pm[2 * yb + 1]], 1),
            ],
            0,
        ).T
        for l in range(2):
            mine = gz[:, lanes(l * 1024 + core * 512, 512)]
            right = jnp.concatenate([mine, pz[:, l * 512 : (l + 1) * 512]], 0)
            term = dot(left, right, 1, 0).astype(BF)
            for xb in range(4):
                for hb in range(2):
                    for rg in range(2):
                        for ch in range(4):
                            r = (xb * 2 + hb) * 32 + rg * 16
                            put(
                                yb, xb, hb * 2 + l, 24 + rg * 4 + ch,
                                term[r : r + 16, ch * 128 : (ch + 1) * 128],
                            )

        @pl.when(n == 0)
        def _():
            ring(1, 0, 0, 0).start()
            ring(1, 0, 1, 0).start()

        @pl.when(n == 1)
        def _():
            for s in (0, 2):
                ring(s, 0, 0, 0).start()
                ring(s, 0, 1, 1).start()

        @pl.when((n == 1) & (y % 2 == 0) | (n == 2) & (y % 2 == 1))
        def _():
            ring(1, 0, 1, 1).start()

        @pl.when((n == 1) & (y % 2 == 1) | (n == 2) & (y % 2 == 0))
        def _():
            ring(1, 0, 0, 1).start()

        @pl.when(n == 3)
        def _():
            for s in (0, 2):
                ring(s, 0, 1, 0).start()
                ring(s, 0, 0, 1).start()

        return carry

    far_pair, near_pair = pl.ds((1 - y // 2) * 2, 2), pl.ds((y // 2) * 2, 2)

    def half(s, level, way):
        if level == 1 or s == 1:
            return (pl.ds(2 * way, 2),)
        cut = near_pair if way else far_pair
        return (cut,) if s == 0 else (slice(None), cut)

    def ring(s, level, way, part):
        axis = ORDERS[s][level]
        step = 1 if way == 0 else 3
        near, far = (at[axis] + step) % 4, (at[axis] + 2) % 4
        src = (
            terms[level][s].at[(far, *half(s, level, way))],
            terms[level][s].at[(near, *half(s, level, 1 - way))],
            terms[level][s].at[(near, *half(s, level, way))],
        )[part]
        sems = ring_sems.at[s, level, way, part]
        return remote(
            src, boxes[level][s].at[way, part], sems.at[0], sems.at[1], along(axis, step)
        )

    def ring_open(level, s):
        for part in range(2):
            for way in range(2):
                ring(s, level, way, part).start()

    def ring_middle(level, s):
        axis = ORDERS[s][level]
        for way in range(2):
            ring(s, level, way, 0).wait_recv()
            near = (at[axis] + (1 if way == 0 else 3)) % 4
            spot = terms[level][s].at[(near, *half(s, level, way))]
            spot[...] = (
                spot[...].astype(F32) + boxes[level][s][way, 0].astype(F32)
            ).astype(BF)
            ring(s, level, way, 2).start()

    def ring_close(level, s):
        for way in range(2):
            ring(s, level, way, 1).wait_recv()
            ring(s, level, way, 2).wait_recv()
        mine = at[ORDERS[s][level]]
        box = boxes[level][s]
        for way in range(2):
            cut = half(s, level, way)
            terms[level + 1][s][cut] = (
                terms[level][s][(mine, *cut)].astype(F32)
                + box[way, 2].astype(F32)
                + box[1 - way, 1].astype(F32)
            ).astype(BF)

    lax.fori_loop(0, 4, terms_of, 0)
    for load in loads[7:]:
        load.wait()

    def pull_hidden(n, carry):
        cut = lanes(n * 512, 512)
        total = dot(proj[:, :1024], w[0, cut, :], 1, 1)
        total = total + dot(proj[:, 1024:2048], w[1, cut, :], 1, 1)
        total = total + dot(proj[:, 2048:], w[2, cut, :], 1, 1)
        gh[:, cut] = total.astype(BF)
        return carry

    lax.fori_loop(0, 4, pull_hidden, 0)
    for s in range(3):
        ring_middle(0, s)

    def norm_rows(n, carry):
        cut = rows_of(n * 16, 16)
        level = n // 8
        v = noisy[cut, :].astype(F32)
        center = v - jnp.mean(v, axis=1, keepdims=True)
        factor = lax.rsqrt(jnp.mean(center * center, axis=1, keepdims=True) + EPS)
        hat = center * factor
        g = gh[cut, :].astype(F32) * scale1[pl.ds(level, 1), :]
        dv = factor * (
            g
            - jnp.mean(g, axis=1, keepdims=True)
            - hat * jnp.mean(g * hat, axis=1, keepdims=True)
        )
        out_n[cut, :] = (dv + grad[cut, :].astype(F32)).astype(BF)
        return carry

    lax.fori_loop(0, rows // 16, norm_rows, 0)

    for s in range(3):
        ring_close(0, s)
        ring_open(1, s)
    for s in range(3):
        ring_middle(1, s)

    def last(s, step):
        axis = ORDERS[s][2]
        there = (at[axis] + step) % 4
        sems = last_sems.at[s, step - 1]
        return remote(
            terms[2][s].at[there], boxes[2][s].at[step - 1], sems.at[0], sems.at[1],
            along(axis, step),
        )

    for s in range(3):
        ring_close(1, s)
        for step in (1, 2, 3):
            last(s, step).start()
    for s in range(3):
        for step in (1, 2, 3):
            last(s, step).wait_recv()
        mine = at[ORDERS[s][2]]
        sums = terms[2][s][mine].astype(F32)
        for step in (1, 2, 3):
            sums = sums + boxes[2][s][step - 1].astype(F32)
        sums = sums.astype(BF)
        for u in range(UNITS[s]):
            unit = FIRST_UNIT[s] + u
            if unit < 24:
                j, rg, ch = unit // 8, (unit // 2) % 4, unit % 2
                out_g[j, rg * 16 : (rg + 1) * 16, ch * 128 : (ch + 1) * 128] = sums[u]
            else:
                rg, ch = (unit - 24) // 4, unit % 4
                out_o[rg * 16 : (rg + 1) * 16, ch * 128 : (ch + 1) * 128] = sums[u]

    for copy in swaps:
        copy.wait_send()
    for s in range(3):
        for level in range(2):
            for way in range(2):
                for part in range(3):
                    ring(s, level, way, part).wait_send()
        for step in (1, 2, 3):
            last(s, step).wait_send()


def close(got, q, k, hidden, gz, ph, pz, scale1, noisy, grad, w3):
    rows, model = hidden.shape
    vmem = pl.BlockSpec(memory_space=pltpu.VMEM)

    def box(*shape):
        return [pltpu.VMEM(shape + (u, 16, 128), BF) for u in UNITS]

    return pl.pallas_call(
        close_kernel,
        out_shape=(
            jax.ShapeDtypeStruct((rows, model), BF),
            jax.ShapeDtypeStruct((3, 64, 256), BF),
            jax.ShapeDtypeStruct((32, 512), BF),
        ),
        in_specs=[ANY] * 11,
        out_specs=(vmem,) * 3,
        scratch_shapes=[
            *[
                pltpu.VMEM(array.shape, array.dtype)
                for array in (got, q, k, hidden, gz, ph, pz, scale1, noisy, grad)
            ],
            pltpu.VMEM((rows, 3072), BF),
            pltpu.VMEM((8, rows, HD), BF),
            pltpu.VMEM((rows, 1536), BF),
            pltpu.VMEM(w3.shape, BF),
            pltpu.VMEM((rows, model), BF),
            *box(4, 4, 4),
            *box(4, 4),
            *box(4),
            *box(2, 3, 2, 4)[:2],
            box(2, 3, 4, 2)[2],
            *box(2, 3, 2),
            *box(3),
            pltpu.SemaphoreType.DMA((2, 7)),
            pltpu.SemaphoreType.DMA((11,)),
            pltpu.SemaphoreType.DMA((3, 2, 2, 3, 2)),
            pltpu.SemaphoreType.DMA((3, 3, 2)),
        ],
        compiler_params=pltpu.CompilerParams(
            collective_id=1, has_side_effects=True, vmem_limit_bytes=62 * 1024 * 1024
        ),
        name="close",
    )(got, q, k, hidden, gz, ph, pz, scale1, noisy, grad, w3)


def on_device(
    noisy, clean, actions, levels, starts, w_qkv, w_out, noise_table, action_table, temps, out_grad
):
    tokens, model = noisy.shape[3:]
    rows = 2 * tokens
    w3 = w_qkv.transpose(1, 0, 2)
    noisy_rows = noisy.reshape(rows, model)
    grad_rows = out_grad.reshape(rows, model)
    got, hidden, grad_z, q, k, scale1, ph, pz = open_up(
        levels.reshape(2),
        actions.reshape(1),
        starts.reshape(1),
        noisy_rows,
        clean.reshape(tokens, model),
        grad_rows,
        noise_table.transpose(1, 0, 2),
        action_table,
        w3,
        w_out,
        temps,
    )
    grad_noisy, total_g, total_o = close(
        got, q, k, hidden, grad_z, ph, pz, scale1, noisy_rows, grad_rows, w3
    )
    return (grad_noisy.reshape(noisy.shape), total_g.transpose(1, 0, 2), total_o)


def solution(mesh):
    in_specs = (
        P("dp", "tm", None, None, None),
        P("dp", "tm", None, None),
        P("dp", "tm"),
        P("dp", "tm", None),
        P("dp", "tm"),
        P(),
        P(),
        P(),
        P(),
        P(),
        P("dp", "tm", None, None, None),
    )
    out_specs = (P("dp", "tm", None, None, None), P("tm", None, "dp"), P("tm", "dp"))
    return jax.shard_map(
        on_device, mesh=mesh, in_specs=in_specs, out_specs=out_specs, check_vma=False
    )
```

```python
import functools
import math

import jax
import jax.numpy as jnp
from jax import lax
from jax.experimental import pallas as pl
from jax.experimental.pallas import tpu as pltpu
from jax.sharding import PartitionSpec as P

EPS = 1e-06
NEG = -1e30
MESH = pl.DeviceIdType.MESH
HEADS = 8
HD = 128
BF = jnp.bfloat16
F32 = jnp.float32
ANY = pl.BlockSpec(memory_space=pl.ANY)
LOG2E = 1.4426950408889634


def dot(left, right, left_dim, right_dim):
    return lax.dot_general(
        left, right, (((left_dim,), (right_dim,)), ((), ())), preferred_element_type=F32
    )


def lanes(start, size):
    return pl.ds(pl.multiple_of(start, 128), size)


def rows_of(start, size):
    return pl.ds(pl.multiple_of(start, size), size)


def wait_bytes(ref, sem):
    pltpu.make_async_copy(ref, ref, sem).wait()


def place(t):
    return t // 8, (t // 2) % 4, t % 2


def head_home(h, x):
    return ((h // 2) * 4 + x) * 2 + h % 2


def open_kernel(
    level, action, start, noisy_all, clean_all, grad_all, noise_all, acts_all, w3, w_out,
    temps, got, hidden_out, gz_out, q_out, k_out, scale_out, ph, pz,
    noisy, clean, grad, noise, acts, hidden, gz, q, k, scale1, kv, own, stretch, clean_hidden, ckv, out, tile, w, wo, s_scr, res,
    w_sems, kv_sems, x_sems, own_sems, start_sems, local_sems, back_sems, swap_sems, in_sems, out_sems,
):
    t = lax.axis_index("tm")
    d = lax.axis_index("dp")
    y, x, zh = place(t)
    slot = y * 2 + zh
    first = [
        pltpu.make_async_copy(clean_all, clean, in_sems.at[0]),
        pltpu.make_async_copy(noise_all, noise, in_sems.at[1]),
        pltpu.make_async_copy(acts_all, acts, in_sems.at[2]),
    ]
    loads = [
        pltpu.make_async_copy(w3.at[1], w.at[1], w_sems.at[1]),
        pltpu.make_async_copy(w3.at[2], w.at[2], w_sems.at[2]),
        pltpu.make_async_copy(w3.at[0], w.at[0], w_sems.at[0]),
        pltpu.make_async_copy(w_out, wo, w_sems.at[3]),
    ]
    second = [
        pltpu.make_async_copy(noisy_all, noisy, in_sems.at[3]),
        pltpu.make_async_copy(grad_all, grad, in_sems.at[4]),
    ]
    for load in first + loads[:2] + second + loads[2:]:
        load.start()

    def peer(h):
        return {"dp": d, "tm": head_home(h, x)}

    def beside(step):
        return {"dp": d, "tm": (y * 4 + (x + step) % 4) * 2 + zh}

    barrier = pltpu.get_barrier_semaphore()

    def greet(s, carry):
        pl.semaphore_signal(
            barrier, inc=1, device_id=peer((slot + s) % 8), device_id_type=MESH
        )
        return carry

    lax.fori_loop(1, 8, greet, 0)
    core = d % 2
    partner = {"dp": d + 1 - 2 * core, "tm": t}
    for device in (beside(1), beside(3), partner):
        pl.semaphore_signal(barrier, inc=1, device_id=device, device_id_type=MESH)

    def remote(src, dst, sems, device, arrived=1):
        return pltpu.make_async_remote_copy(
            src_ref=src,
            dst_ref=dst,
            send_sem=sems.at[0],
            recv_sem=sems.at[arrived],
            device_id=device,
            device_id_type=MESH,
        )

    def modulated(values, shift, scale):
        center = values - jnp.mean(values, axis=1, keepdims=True)
        factor = lax.rsqrt(jnp.mean(center * center, axis=1, keepdims=True) + EPS)
        return (center * factor * scale + shift).astype(BF)

    for load in first:
        load.wait()
    act = acts[action[0]]
    clean_shift = noise[0, 0:1, :] + act[0:1]
    clean_scale = 1.0 + (noise[1, 0:1, :] + act[1:2])

    def clean_rows(n, carry):
        cut = rows_of(n * 16, 16)
        clean_hidden[cut, :] = modulated(clean[cut, :].astype(F32), clean_shift, clean_scale)
        return carry

    lax.fori_loop(0, 8, clean_rows, 0, unroll=2)

    def normed(u):
        factor = lax.rsqrt(jnp.mean(u * u, axis=1, keepdims=True) + EPS)
        return (u * factor).astype(BF)

    def clean_keys(m, carry):
        u = dot(clean_hidden[...], w[1, :, lanes(m * 256, 256)], 1, 0)
        for i in range(2):
            ckv[2 * m + i, 0] = normed(u[:, i * HD : (i + 1) * HD])
        return carry

    def clean_vals(m, carry):
        u = dot(clean_hidden[...], w[2, :, lanes(m * 256, 256)], 1, 0).astype(BF)
        for i in range(2):
            ckv[2 * m + i, 1] = u[:, i * HD : (i + 1) * HD]
        return carry

    tile[...] = jnp.full((8, 128), start[0], jnp.int32)
    loads[0].wait()
    lax.fori_loop(0, 4, clean_keys, 0)
    loads[1].wait()
    lax.fori_loop(0, 4, clean_vals, 0)

    pl.semaphore_wait(barrier, 10)

    def send_kv(s, carry):
        h = (slot + s) % 8
        remote(ckv.at[h], kv.at[y, x, zh], kv_sems, peer(h)).start()
        remote(tile, stretch.at[slot], start_sems, peer(h)).start()
        return carry

    lax.fori_loop(1, 8, send_kv, 0)
    mine = [
        pltpu.make_async_copy(ckv.at[slot], kv.at[y, x, zh], local_sems.at[0]),
        pltpu.make_async_copy(tile, stretch.at[slot], local_sems.at[1]),
    ]
    for copy in mine:
        copy.start()

    for load in second:
        load.wait()
    for j in range(2):
        row = pl.ds(level[j], 1)
        shift = noise[0, row, :] + act[0:1]
        scale = 1.0 + (noise[1, row, :] + act[1:2])
        gate = noise[2, row, :] + act[2:3]
        scale1[j : j + 1, :] = scale

        def noisy_rows(n, carry):
            cut = rows_of((j * 8 + n) * 16, 16)
            hidden[cut, :] = modulated(noisy[cut, :].astype(F32), shift, scale)
            gz[cut, :] = (gate * grad[cut, :].astype(F32)).astype(BF)
            return carry

        lax.fori_loop(0, 8, noisy_rows, 0, unroll=2)

    swaps = [remote(hidden, ph, swap_sems.at[0], partner)]
    for l in range(2):
        cut = lanes(l * 1024 + (1 - core) * 512, 512)
        swaps.append(
            remote(gz.at[:, cut], pz.at[:, pl.ds(l * 512, 512)], swap_sems.at[1 + l], partner)
        )
    for copy in swaps:
        copy.start()
    results = [
        pltpu.make_async_copy(hidden, hidden_out, out_sems.at[0]),
        pltpu.make_async_copy(gz, gz_out, out_sems.at[1]),
        pltpu.make_async_copy(scale1, scale_out, out_sems.at[2]),
        pltpu.make_async_copy(q, q_out, out_sems.at[3]),
        pltpu.make_async_copy(k, k_out, out_sems.at[4]),
    ]
    for copy in results[:3]:
        copy.start()
    loads[2].wait()
    loads[3].wait()

    def project(i, carry):
        m = (slot // 2 + 1 + i) % 4
        cut = lanes(m * 256, 256)
        uk = dot(hidden[...], w[1, :, cut], 1, 0)
        uv = dot(hidden[...], w[2, :, cut], 1, 0).astype(BF)
        uq = dot(hidden[...], w[0, :, cut], 1, 0)
        um = dot(gz[...], wo[rows_of(m * 256, 256), :], 1, 1).astype(BF)
        k[:, cut] = uk
        q[:, cut] = uq
        for a in range(2):
            part = slice(a * HD, (a + 1) * HD)
            out[2 * m + a, 0] = normed(uq[:, part])
            out[2 * m + a, 1] = normed(uk[:, part])
            out[2 * m + a, 2] = uv[:, part]
            out[2 * m + a, 3] = um[:, part]
        return carry

    def send_own(h, i):
        remote(out.at[h], own.at[slot], own_sems, peer(h), 1 + i).start()

    def send_pair(i):
        m = (slot // 2 + 1 + i) % 4
        send_own(2 * m, i)
        send_own(2 * m + 1, i)

    project(0, 0)
    send_pair(0)
    for copy in mine:
        copy.wait()
    wait_bytes(ckv.at[pl.ds(0, 7)], kv_sems.at[1])
    half = (pl.ds(0, 2), pl.ds(2, 2))

    def along_x(n):
        cut = half[(0, 1, 1, 0, 0, 1)[n]]
        whose = x if n < 4 else (x + (3 if n == 4 else 1)) % 4
        step = (1, 1, 3, 3, 1, 3)[n]
        return remote(kv.at[cut, whose], kv.at[cut, whose], x_sems.at[n], beside(step))

    for n in (0, 2, 1, 3):
        along_x(n).start()

    def project_send(i, carry):
        project(i, carry)
        send_pair(i)
        return carry

    lax.fori_loop(1, 3, project_send, 0)
    project(3, 0)
    sibling = slot + 1 - 2 * zh
    send_own(sibling, 3)
    last = pltpu.make_async_copy(out.at[slot], own.at[slot], local_sems.at[2])
    last.start()
    for copy in results[3:]:
        copy.start()
    last.wait()
    for n in (0, 2):
        along_x(n).wait_recv()
        along_x(4 + n // 2).start()
    wait_bytes(stretch.at[pl.ds(0, 7)], start_sems.at[1])
    for n in (1, 3, 4, 5):
        along_x(n).wait_recv()

    scale = temps[slot] * (1.0 / math.sqrt(HD))
    c2 = scale * LOG2E
    h = HD
    pair = (0, 1)

    def keys(c, part):
        return kv[c, :, :, part].reshape(8 * h, h)

    def both(left, right, left_dim, right_dim):
        return jnp.concatenate(
            [
                dot(left[:h], right[:h], left_dim, right_dim),
                dot(left[h:], right[h:], left_dim, right_dim),
            ],
            0,
        )

    def attend(row):
        at = [row * 2 + n for n in pair]
        g = [row * 8 + x * 2 + n for n in pair]
        st = [stretch[i, 0:1, :] for i in at]
        qs = [own[i, 0] for i in at]
        ks = [own[i, 1] for i in at]
        vs = [own[i, 2] for i in at]
        ds = [own[i, 3] for i in at]
        s_own = [both(qs[n], ks[n], 1, 1) for n in pair]
        top = list(s_own)
        for c in range(row + 1):
            for n in pair:
                s = dot(qs[n], keys(c, 0), 1, 1)
                for b in range(8):
                    f = c * 8 + b
                    seen = (st[n] <= f) & (f < g[n])
                    sb = s[:, b * h : (b + 1) * h] + jnp.where(seen, 0.0, NEG)
                    s_scr[n, c, :, b * h : (b + 1) * h] = sb
                    top[n] = jnp.maximum(top[n], sb)
        m2 = [jnp.max(top[n], axis=1, keepdims=True) * c2 for n in pair]
        p_own = [jnp.exp2(s_own[n] * c2 - m2[n]) for n in pair]
        acc = [both(p_own[n].astype(BF), vs[n], 1, 0) for n in pair]
        total = list(p_own)
        for c in range(row + 1):
            for n in pair:
                p = jnp.exp2(s_scr[n, c] * c2 - m2[n])
                s_scr[n, c] = p
                for b in range(8):
                    total[n] = total[n] + p[:, b * h : (b + 1) * h]
                acc[n] = acc[n] + dot(p.astype(BF), keys(c, 1), 1, 0)
        inv = [1.0 / jnp.sum(total[n], axis=1, keepdims=True) for n in pair]
        mixed = [acc[n] * inv[n] for n in pair]
        delta = [jnp.sum(mixed[n] * ds[n].astype(F32), axis=1, keepdims=True) for n in pair]
        ds_own = [p_own[n] * (both(ds[n], vs[n], 1, 1) - delta[n]) for n in pair]
        dq = [both(ds_own[n].astype(BF), ks[n], 1, 0) for n in pair]
        for c in range(row + 1):
            for n in pair:
                pull = s_scr[n, c] * (dot(ds[n], keys(c, 1), 1, 1) - delta[n])
                dq[n] = dq[n] + dot(pull.astype(BF), keys(c, 0), 1, 0)
        for n in pair:
            i = at[n]
            res[i, 0] = mixed[n].astype(BF)
            res[i, 1] = (dq[n] * (inv[n] * scale)).astype(BF)
            dsn = (ds_own[n] * (inv[n] * scale)).astype(BF)
            pn = (p_own[n] * inv[n]).astype(BF)
            for j in range(2):
                cut = slice(j * h, (j + 1) * h)
                res[i, 2, cut] = dot(dsn[cut], qs[n][cut], 0, 0).astype(BF)
                res[i, 3, cut] = dot(pn[cut], ds[n][cut], 0, 0).astype(BF)

    def send_back(i):
        remote(res.at[i], got.at[slot], back_sems, peer(i)).start()

    def attend_row(s, carry):
        row = (y + 3 - s) % 4

        @pl.when(s < 3)
        def _():
            wait_bytes(own.at[pl.ds(0, 2)], own_sems.at[1 + s])

        @pl.when(s == 3)
        def _():
            wait_bytes(own.at[0], own_sems.at[4])

        for r in range(4):

            @pl.when(row == r)
            def _():
                attend(r)

        @pl.when(s < 3)
        def _():
            send_back(2 * row)
            send_back(2 * row + 1)

        return carry

    lax.fori_loop(0, 4, attend_row, 0)
    send_back(sibling)
    keep = pltpu.make_async_copy(res.at[slot], got.at[slot], local_sems.at[2])
    keep.start()
    keep.wait()
    wait_bytes(stretch.at[pl.ds(0, 7)], start_sems.at[0])
    for n in range(6):
        along_x(n).wait_send()
    for copy in swaps + results:
        copy.wait()
    wait_bytes(own.at[pl.ds(0, 7)], own_sems.at[0])
    wait_bytes(ckv.at[pl.ds(0, 7)], kv_sems.at[0])
    for way in (0, 1):
        wait_bytes(res.at[pl.ds(0, 7)], back_sems.at[way])


def open_up(level, action, start, noisy, clean, grad, noise, acts, w3, w_out, temps):
    rows, model = noisy.shape
    tokens = clean.shape[0]
    width = w_out.shape[0]
    smem = pl.BlockSpec(memory_space=pltpu.SMEM)
    return pl.pallas_call(
        open_kernel,
        out_shape=(
            jax.ShapeDtypeStruct((8, 4, rows, HD), BF),
            jax.ShapeDtypeStruct((rows, model), BF),
            jax.ShapeDtypeStruct((rows, model), BF),
            jax.ShapeDtypeStruct((rows, width), F32),
            jax.ShapeDtypeStruct((rows, width), F32),
            jax.ShapeDtypeStruct((2, model), F32),
            jax.ShapeDtypeStruct((rows, model), BF),
            jax.ShapeDtypeStruct((rows, model // 2), BF),
        ),
        in_specs=[smem] * 3 + [ANY] * 7 + [smem],
        out_specs=(ANY,) * 8,
        scratch_shapes=[
            pltpu.VMEM(noisy.shape, BF),
            pltpu.VMEM(clean.shape, BF),
            pltpu.VMEM(grad.shape, BF),
            pltpu.VMEM(noise.shape, F32),
            pltpu.VMEM(acts.shape, F32),
            pltpu.VMEM((rows, model), BF),
            pltpu.VMEM((rows, model), BF),
            pltpu.VMEM((rows, width), F32),
            pltpu.VMEM((rows, width), F32),
            pltpu.VMEM((2, model), F32),
            pltpu.VMEM((4, 4, 2, 2, tokens, HD), BF),
            pltpu.VMEM((8, 4, rows, HD), BF),
            pltpu.VMEM((8, 8, 128), jnp.int32),
            pltpu.VMEM((tokens, model), BF),
            pltpu.VMEM((8, 2, tokens, HD), BF),
            pltpu.VMEM((8, 4, rows, HD), BF),
            pltpu.VMEM((8, 128), jnp.int32),
            pltpu.VMEM(w3.shape, BF),
            pltpu.VMEM(w_out.shape, BF),
            pltpu.VMEM((2, 4, rows, 8 * HD), F32),
            pltpu.VMEM((8, 4, rows, HD), BF),
            pltpu.SemaphoreType.DMA((4,)),
            pltpu.SemaphoreType.DMA((2,)),
            pltpu.SemaphoreType.DMA((6, 2)),
            pltpu.SemaphoreType.DMA((5,)),
            pltpu.SemaphoreType.DMA((2,)),
            pltpu.SemaphoreType.DMA((3,)),
            pltpu.SemaphoreType.DMA((2,)),
            pltpu.SemaphoreType.DMA((3, 2)),
            pltpu.SemaphoreType.DMA((5,)),
            pltpu.SemaphoreType.DMA((5,)),
        ],
        compiler_params=pltpu.CompilerParams(
            collective_id=0, has_side_effects=True, vmem_limit_bytes=60 * 1024 * 1024
        ),
        name="open",
    )(level, action, start, noisy, clean, grad, noise, acts, w3, w_out, temps)


ORDERS = (("x", "y", "z"), ("y", "z", "x"), ("z", "x", "y"))
UNITS = (11, 11, 10)
FIRST_UNIT = (0, 11, 22)


def stream_of(unit):
    k = unit // 11
    return k, unit - FIRST_UNIT[k]


def close_kernel(
    got_all, q_all, k_all, hidden_all, gz_all, ph_all, pz_all, scale_all, noisy_all, grad_all, w3,
    all_n, out_g, out_o,
    out_n, got, q, k, hidden, gz, ph, pz, scale1, noisy, grad, proj, pm, pp, w, gh,
    t0a, t0b, t0c, t1a, t1b, t1c, t2a, t2b, t2c, b0a, b0b, b0c, b1a, b1b, b1c, b2a, b2b, b2c,
    swap_sems, w_sem, ring_sems, last_sems,
):
    t = lax.axis_index("tm")
    d = lax.axis_index("dp")
    y, x, zh = place(t)
    zl, core = d // 2, d % 2
    z = zh * 2 + zl
    partner = {"dp": d + 1 - 2 * core, "tm": t}
    at = {"x": x, "y": y, "z": z}
    rows = hidden.shape[0]
    terms = ((t0a, t0b, t0c), (t1a, t1b, t1c), (t2a, t2b, t2c))
    boxes = ((b0a, b0b, b0c), (b1a, b1b, b1c), (b2a, b2b, b2c))

    def along(axis, step):
        c = dict(at)
        c[axis] = (c[axis] + step) % 4
        return {
            "dp": (c["z"] % 2) * 2 + core,
            "tm": (c["y"] * 4 + c["x"]) * 2 + c["z"] // 2,
        }

    sources = (
        got_all, q_all, k_all, hidden_all, gz_all, ph_all, pz_all, scale_all, noisy_all, grad_all, w3,
    )
    places = (got, q, k, hidden, gz, ph, pz, scale1, noisy, grad, w)
    loads = [
        pltpu.make_async_copy(source, spot, w_sem.at[n])
        for n, (source, spot) in enumerate(zip(sources, places, strict=True))
    ]
    for load in loads:
        load.start()
    barrier = pltpu.get_barrier_semaphore()

    for axis in "xyz":
        for step in (1, 2, 3):
            pl.semaphore_signal(
                barrier, inc=1, device_id=along(axis, step), device_id_type=MESH
            )
    pl.semaphore_signal(barrier, inc=1, device_id=partner, device_id_type=MESH)
    def remote(src, dst, send_sem, recv_sem, device):
        return pltpu.make_async_remote_copy(
            src_ref=src,
            dst_ref=dst,
            send_sem=send_sem,
            recv_sem=recv_sem,
            device_id=device,
            device_id_type=MESH,
        )

    def swap(src, dst, part):
        copy = remote(src, dst, swap_sems.at[0, part], swap_sems.at[1, part], partner)
        copy.start()
        return copy

    def norm_back(h, carry):
        for part, u_ref in ((0, q), (1, k)):
            u = u_ref[:, lanes(h * HD, HD)]
            factor = lax.rsqrt(jnp.mean(u * u, axis=1, keepdims=True) + EPS)
            hat = u * factor
            g = got[h, 1 + part].astype(F32)
            du = factor * (g - hat * jnp.mean(hat * g, axis=1, keepdims=True))
            proj[:, lanes(part * 1024 + h * HD, HD)] = du.astype(BF)
        proj[:, lanes(2048 + h * HD, HD)] = got[h, 3]
        return carry

    for load in loads[:3]:
        load.wait()
    other = 1 - core
    swaps = []
    for l in range(2):
        lax.fori_loop(0, 2, lambda i, c: norm_back(l * 4 + other * 2 + i, c), 0)
        if l == 0:
            pl.semaphore_wait(barrier, 10)
            swaps.append(swap(got.at[:, 0], pm, 0))
        for j in range(3):
            swaps.append(
                swap(
                    proj.at[:, lanes(j * 1024 + l * 512 + other * 256, 256)],
                    pp.at[:, pl.ds(l * 768 + j * 256, 256)],
                    1 + l * 3 + j,
                )
            )
    for l in range(2):
        lax.fori_loop(0, 2, lambda i, c: norm_back(l * 4 + core * 2 + i, c), 0)
    for load in loads[3:7]:
        load.wait()
    for copy in swaps:
        copy.wait_recv()

    def put(yb, xb, zb, unit, value):
        s, u = stream_of(unit)
        spot = {"x": xb, "y": yb, "z": zb}
        terms[0][s][spot[ORDERS[s][0]], spot[ORDERS[s][1]], spot[ORDERS[s][2]], u] = value

    def terms_of(n, carry):
        yb = ((y // 2 + 1 + n // 2) % 2) * 2 + (y + n % 2 + n // 2) % 2
        cut = lanes(yb * 512, 512)
        left = jnp.concatenate([hidden[:, cut], ph[:, cut]], 0).T
        for l in range(2):
            for j in range(3):
                mine = proj[:, lanes(j * 1024 + l * 512 + core * 256, 256)]
                theirs = pp[:, l * 768 + j * 256 : l * 768 + (j + 1) * 256]
                right = jnp.concatenate([mine, theirs], 0)
                term = dot(left, right, 1, 0).astype(BF)
                for xb in range(4):
                    for hb in range(2):
                        for rg in range(4):
                            r = (xb * 2 + hb) * 64 + rg * 16
                            for ch in range(2):
                                put(
                                    yb, xb, hb * 2 + l, (j * 4 + rg) * 2 + ch,
                                    term[r : r + 16, ch * 128 : (ch + 1) * 128],
                                )
        left = jnp.concatenate(
            [
                jnp.concatenate([got[2 * yb, 0], got[2 * yb + 1, 0]], 1),
                jnp.concatenate([pm[2 * yb], pm[2 * yb + 1]], 1),
            ],
            0,
        ).T
        for l in range(2):
            mine = gz[:, lanes(l * 1024 + core * 512, 512)]
            right = jnp.concatenate([mine, pz[:, l * 512 : (l + 1) * 512]], 0)
            term = dot(left, right, 1, 0).astype(BF)
            for xb in range(4):
                for hb in range(2):
                    for rg in range(2):
                        for ch in range(4):
                            r = (xb * 2 + hb) * 32 + rg * 16
                            put(
                                yb, xb, hb * 2 + l, 24 + rg * 4 + ch,
                                term[r : r + 16, ch * 128 : (ch + 1) * 128],
                            )

        @pl.when(n == 0)
        def _():
            ring(1, 0, 0, 0).start()
            ring(1, 0, 1, 0).start()

        @pl.when(n == 1)
        def _():
            for s in (0, 2):
                ring(s, 0, 0, 0).start()
                ring(s, 0, 1, 1).start()

        @pl.when((n == 1) & (y % 2 == 0) | (n == 2) & (y % 2 == 1))
        def _():
            ring(1, 0, 1, 1).start()

        @pl.when((n == 1) & (y % 2 == 1) | (n == 2) & (y % 2 == 0))
        def _():
            ring(1, 0, 0, 1).start()

        @pl.when(n == 3)
        def _():
            for s in (0, 2):
                ring(s, 0, 1, 0).start()
                ring(s, 0, 0, 1).start()

        return carry

    far_pair, near_pair = pl.ds((1 - y // 2) * 2, 2), pl.ds((y // 2) * 2, 2)

    def half(s, level, way):
        if level == 1 or s == 1:
            return (pl.ds(2 * way, 2),)
        cut = near_pair if way else far_pair
        return (cut,) if s == 0 else (slice(None), cut)

    def ring(s, level, way, part):
        axis = ORDERS[s][level]
        step = 1 if way == 0 else 3
        near, far = (at[axis] + step) % 4, (at[axis] + 2) % 4
        src = (
            terms[level][s].at[(far, *half(s, level, way))],
            terms[level][s].at[(near, *half(s, level, 1 - way))],
            terms[level][s].at[(near, *half(s, level, way))],
        )[part]
        sems = ring_sems.at[s, level, way, part]
        return remote(
            src, boxes[level][s].at[way, part], sems.at[0], sems.at[1], along(axis, step)
        )

    def ring_open(level, s):
        for part in range(2):
            for way in range(2):
                ring(s, level, way, part).start()

    def ring_middle(level, s):
        axis = ORDERS[s][level]
        for way in range(2):
            ring(s, level, way, 0).wait_recv()
            near = (at[axis] + (1 if way == 0 else 3)) % 4
            spot = terms[level][s].at[(near, *half(s, level, way))]
            spot[...] = (
                spot[...].astype(F32) + boxes[level][s][way, 0].astype(F32)
            ).astype(BF)
            ring(s, level, way, 2).start()

    def ring_close(level, s):
        for way in range(2):
            ring(s, level, way, 1).wait_recv()
            ring(s, level, way, 2).wait_recv()
        mine = at[ORDERS[s][level]]
        box = boxes[level][s]
        for way in range(2):
            cut = half(s, level, way)
            terms[level + 1][s][cut] = (
                terms[level][s][(mine, *cut)].astype(F32)
                + box[way, 2].astype(F32)
                + box[1 - way, 1].astype(F32)
            ).astype(BF)

    lax.fori_loop(0, 4, terms_of, 0)
    for load in loads[7:]:
        load.wait()

    def pull_hidden(n, carry):
        cut = lanes(n * 512, 512)
        total = dot(proj[:, :1024], w[0, cut, :], 1, 1)
        total = total + dot(proj[:, 1024:2048], w[1, cut, :], 1, 1)
        total = total + dot(proj[:, 2048:], w[2, cut, :], 1, 1)
        gh[:, cut] = total.astype(BF)
        return carry

    lax.fori_loop(0, 4, pull_hidden, 0)
    for s in range(3):
        ring_middle(0, s)

    def norm_rows(n, carry):
        cut = rows_of(n * 16, 16)
        level = n // 8
        v = noisy[cut, :].astype(F32)
        center = v - jnp.mean(v, axis=1, keepdims=True)
        factor = lax.rsqrt(jnp.mean(center * center, axis=1, keepdims=True) + EPS)
        hat = center * factor
        g = gh[cut, :].astype(F32) * scale1[pl.ds(level, 1), :]
        dv = factor * (
            g
            - jnp.mean(g, axis=1, keepdims=True)
            - hat * jnp.mean(g * hat, axis=1, keepdims=True)
        )
        out_n[cut, :] = (dv + grad[cut, :].astype(F32)).astype(BF)
        return carry

    lax.fori_loop(0, rows // 16, norm_rows, 0)
    leave = pltpu.make_async_copy(out_n, all_n, w_sem.at[11])
    leave.start()

    for s in range(3):
        ring_close(0, s)
        ring_open(1, s)
    for s in range(3):
        ring_middle(1, s)

    def last(s, step):
        axis = ORDERS[s][2]
        there = (at[axis] + step) % 4
        sems = last_sems.at[s, step - 1]
        return remote(
            terms[2][s].at[there], boxes[2][s].at[step - 1], sems.at[0], sems.at[1],
            along(axis, step),
        )

    for s in range(3):
        ring_close(1, s)
        for step in (1, 2, 3):
            last(s, step).start()
    for s in range(3):
        for step in (1, 2, 3):
            last(s, step).wait_recv()
        mine = at[ORDERS[s][2]]
        sums = terms[2][s][mine].astype(F32)
        for step in (1, 2, 3):
            sums = sums + boxes[2][s][step - 1].astype(F32)
        sums = sums.astype(BF)
        for u in range(UNITS[s]):
            unit = FIRST_UNIT[s] + u
            if unit < 24:
                j, rg, ch = unit // 8, (unit // 2) % 4, unit % 2
                out_g[j, rg * 16 : (rg + 1) * 16, ch * 128 : (ch + 1) * 128] = sums[u]
            else:
                rg, ch = (unit - 24) // 4, unit % 4
                out_o[rg * 16 : (rg + 1) * 16, ch * 128 : (ch + 1) * 128] = sums[u]

    leave.wait()
    for copy in swaps:
        copy.wait_send()
    for s in range(3):
        for level in range(2):
            for way in range(2):
                for part in range(3):
                    ring(s, level, way, part).wait_send()
        for step in (1, 2, 3):
            last(s, step).wait_send()


def close(got, q, k, hidden, gz, ph, pz, scale1, noisy, grad, w3):
    rows, model = hidden.shape
    vmem = pl.BlockSpec(memory_space=pltpu.VMEM)

    def box(*shape):
        return [pltpu.VMEM(shape + (u, 16, 128), BF) for u in UNITS]

    return pl.pallas_call(
        close_kernel,
        out_shape=(
            jax.ShapeDtypeStruct((rows, model), BF),
            jax.ShapeDtypeStruct((3, 64, 256), BF),
            jax.ShapeDtypeStruct((32, 512), BF),
        ),
        in_specs=[ANY] * 11,
        out_specs=(ANY, vmem, vmem),
        scratch_shapes=[
            pltpu.VMEM((rows, model), BF),
            *[
                pltpu.VMEM(array.shape, array.dtype)
                for array in (got, q, k, hidden, gz, ph, pz, scale1, noisy, grad)
            ],
            pltpu.VMEM((rows, 3072), BF),
            pltpu.VMEM((8, rows, HD), BF),
            pltpu.VMEM((rows, 1536), BF),
            pltpu.VMEM(w3.shape, BF),
            pltpu.VMEM((rows, model), BF),
            *box(4, 4, 4),
            *box(4, 4),
            *box(4),
            *box(2, 3, 2, 4)[:2],
            box(2, 3, 4, 2)[2],
            *box(2, 3, 2),
            *box(3),
            pltpu.SemaphoreType.DMA((2, 7)),
            pltpu.SemaphoreType.DMA((12,)),
            pltpu.SemaphoreType.DMA((3, 2, 2, 3, 2)),
            pltpu.SemaphoreType.DMA((3, 3, 2)),
        ],
        compiler_params=pltpu.CompilerParams(
            collective_id=1, has_side_effects=True, vmem_limit_bytes=62 * 1024 * 1024
        ),
        name="close",
    )(got, q, k, hidden, gz, ph, pz, scale1, noisy, grad, w3)


def finish_kernel(*refs):
    sources, targets, places, sems = refs[:3], refs[3:6], refs[6:9], refs[9]
    inward = [pltpu.make_async_copy(sources[n], places[n], sems.at[0, n]) for n in range(3)]
    outward = [pltpu.make_async_copy(places[n], targets[n], sems.at[1, n]) for n in range(3)]
    for copy in inward:
        copy.start()
    for n in range(3):
        inward[n].wait()
        outward[n].start()
    for copy in outward:
        copy.wait()


def finish(*arrays):
    return pl.pallas_call(
        finish_kernel,
        out_shape=tuple(jax.ShapeDtypeStruct(array.shape, array.dtype) for array in arrays),
        in_specs=[ANY] * 3,
        out_specs=(ANY,) * 3,
        scratch_shapes=[
            *[pltpu.VMEM(array.shape, array.dtype) for array in arrays],
            pltpu.SemaphoreType.DMA((2, 3)),
        ],
        compiler_params=pltpu.CompilerParams(vmem_limit_bytes=62 * 1024 * 1024),
        name="finish",
    )(*arrays)


def on_device(
    noisy, clean, actions, levels, starts, w_qkv, w_out, noise_table, action_table, temps, out_grad
):
    tokens, model = noisy.shape[3:]
    rows = 2 * tokens
    w3 = w_qkv.transpose(1, 0, 2)
    noisy_rows = noisy.reshape(rows, model)
    grad_rows = out_grad.reshape(rows, model)
    got, hidden, grad_z, q, k, scale1, ph, pz = open_up(
        levels.reshape(2),
        actions.reshape(1),
        starts.reshape(1),
        noisy_rows,
        clean.reshape(tokens, model),
        grad_rows,
        noise_table.transpose(1, 0, 2),
        action_table,
        w3,
        w_out,
        temps,
    )
    grad_noisy, total_g, total_o = finish(
        *close(got, q, k, hidden, grad_z, ph, pz, scale1, noisy_rows, grad_rows, w3)
    )
    return (grad_noisy.reshape(noisy.shape), total_g.transpose(1, 0, 2), total_o)


def solution(mesh):
    in_specs = (
        P("dp", "tm", None, None, None),
        P("dp", "tm", None, None),
        P("dp", "tm"),
        P("dp", "tm", None),
        P("dp", "tm"),
        P(),
        P(),
        P(),
        P(),
        P(),
        P("dp", "tm", None, None, None),
    )
    out_specs = (P("dp", "tm", None, None, None), P("tm", None, "dp"), P("tm", "dp"))
    return jax.shard_map(
        on_device, mesh=mesh, in_specs=in_specs, out_specs=out_specs, check_vma=False
    )
```

```python
import functools
import math

import jax
import jax.numpy as jnp
from jax import lax
from jax.experimental import pallas as pl
from jax.experimental.pallas import tpu as pltpu
from jax.sharding import PartitionSpec as P

EPS = 1e-06
NEG = -1e30
MESH = pl.DeviceIdType.MESH
HEADS = 8
HD = 128
BF = jnp.bfloat16
F32 = jnp.float32
ANY = pl.BlockSpec(memory_space=pl.ANY)
LOG2E = 1.4426950408889634


def dot(left, right, left_dim, right_dim):
    return lax.dot_general(
        left, right, (((left_dim,), (right_dim,)), ((), ())), preferred_element_type=F32
    )


def lanes(start, size):
    return pl.ds(pl.multiple_of(start, 128), size)


def rows_of(start, size):
    return pl.ds(pl.multiple_of(start, size), size)


def wait_bytes(ref, sem):
    pltpu.make_async_copy(ref, ref, sem).wait()


def place(t):
    return t // 8, (t // 2) % 4, t % 2


def head_home(h, x):
    return ((h // 2) * 4 + x) * 2 + h % 2


def open_kernel(
    level, action, start, noisy_all, clean_all, grad_all, noise_all, acts_all, w3, w_out,
    temps, got, hidden_out, gz_out, q_out, k_out, scale_out, ph, pz,
    noisy, clean, grad, noise, acts, hidden, gz, q, k, scale1, kv, own, stretch, clean_hidden, ckv, out, tile, w, wo, s_scr, res,
    w_sems, kv_sems, x_sems, own_sems, start_sems, local_sems, back_sems, swap_sems, in_sems, out_sems,
):
    t = lax.axis_index("tm")
    d = lax.axis_index("dp")
    y, x, zh = place(t)
    slot = y * 2 + zh
    first = [
        pltpu.make_async_copy(clean_all, clean, in_sems.at[0]),
        pltpu.make_async_copy(noise_all, noise, in_sems.at[1]),
        pltpu.make_async_copy(acts_all, acts, in_sems.at[2]),
    ]
    loads = [
        pltpu.make_async_copy(w3.at[1], w.at[1], w_sems.at[1]),
        pltpu.make_async_copy(w3.at[2], w.at[2], w_sems.at[2]),
        pltpu.make_async_copy(w3.at[0], w.at[0], w_sems.at[0]),
        pltpu.make_async_copy(w_out, wo, w_sems.at[3]),
    ]
    second = [
        pltpu.make_async_copy(noisy_all, noisy, in_sems.at[3]),
        pltpu.make_async_copy(grad_all, grad, in_sems.at[4]),
    ]
    for load in first + loads[:2] + second + loads[2:]:
        load.start()

    def peer(h):
        return {"dp": d, "tm": head_home(h, x)}

    def beside(step):
        return {"dp": d, "tm": (y * 4 + (x + step) % 4) * 2 + zh}

    barrier = pltpu.get_barrier_semaphore()

    def greet(s, carry):
        pl.semaphore_signal(
            barrier, inc=1, device_id=peer((slot + s) % 8), device_id_type=MESH
        )
        return carry

    lax.fori_loop(1, 8, greet, 0)
    core = d % 2
    partner = {"dp": d + 1 - 2 * core, "tm": t}
    for device in (beside(1), beside(3), partner):
        pl.semaphore_signal(barrier, inc=1, device_id=device, device_id_type=MESH)

    def remote(src, dst, sems, device, arrived=1):
        return pltpu.make_async_remote_copy(
            src_ref=src,
            dst_ref=dst,
            send_sem=sems.at[0],
            recv_sem=sems.at[arrived],
            device_id=device,
            device_id_type=MESH,
        )

    def modulated(values, shift, scale):
        center = values - jnp.mean(values, axis=1, keepdims=True)
        factor = lax.rsqrt(jnp.mean(center * center, axis=1, keepdims=True) + EPS)
        return (center * factor * scale + shift).astype(BF)

    for load in first:
        load.wait()
    act = acts[action[0]]
    clean_shift = noise[0, 0:1, :] + act[0:1]
    clean_scale = 1.0 + (noise[1, 0:1, :] + act[1:2])

    def clean_rows(n, carry):
        cut = rows_of(n * 16, 16)
        clean_hidden[cut, :] = modulated(clean[cut, :].astype(F32), clean_shift, clean_scale)
        return carry

    lax.fori_loop(0, 8, clean_rows, 0, unroll=2)

    def normed(u):
        factor = lax.rsqrt(jnp.mean(u * u, axis=1, keepdims=True) + EPS)
        return (u * factor).astype(BF)

    def clean_keys(m, carry):
        u = dot(clean_hidden[...], w[1, :, lanes(m * 256, 256)], 1, 0)
        for i in range(2):
            ckv[2 * m + i, 0] = normed(u[:, i * HD : (i + 1) * HD])
        return carry

    def clean_vals(m, carry):
        u = dot(clean_hidden[...], w[2, :, lanes(m * 256, 256)], 1, 0).astype(BF)
        for i in range(2):
            ckv[2 * m + i, 1] = u[:, i * HD : (i + 1) * HD]
        return carry

    tile[...] = jnp.full((8, 128), start[0], jnp.int32)
    loads[0].wait()
    lax.fori_loop(0, 4, clean_keys, 0)
    loads[1].wait()
    lax.fori_loop(0, 4, clean_vals, 0)

    pl.semaphore_wait(barrier, 10)

    def send_kv(s, carry):
        h = (slot + s) % 8
        remote(ckv.at[h], kv.at[y, x, zh], kv_sems, peer(h)).start()
        remote(tile, stretch.at[slot], start_sems, peer(h)).start()
        return carry

    lax.fori_loop(1, 8, send_kv, 0)
    mine = [
        pltpu.make_async_copy(ckv.at[slot], kv.at[y, x, zh], local_sems.at[0]),
        pltpu.make_async_copy(tile, stretch.at[slot], local_sems.at[1]),
    ]
    for copy in mine:
        copy.start()

    for load in second:
        load.wait()
    for j in range(2):
        row = pl.ds(level[j], 1)
        shift = noise[0, row, :] + act[0:1]
        scale = 1.0 + (noise[1, row, :] + act[1:2])
        gate = noise[2, row, :] + act[2:3]
        scale1[j : j + 1, :] = scale

        def noisy_rows(n, carry):
            cut = rows_of((j * 8 + n) * 16, 16)
            hidden[cut, :] = modulated(noisy[cut, :].astype(F32), shift, scale)
            gz[cut, :] = (gate * grad[cut, :].astype(F32)).astype(BF)
            return carry

        lax.fori_loop(0, 8, noisy_rows, 0, unroll=2)

    swaps = [remote(hidden, ph, swap_sems.at[0], partner)]
    for l in range(2):
        cut = lanes(l * 1024 + (1 - core) * 512, 512)
        swaps.append(
            remote(gz.at[:, cut], pz.at[:, pl.ds(l * 512, 512)], swap_sems.at[1 + l], partner)
        )
    for copy in swaps:
        copy.start()
    results = [
        pltpu.make_async_copy(hidden, hidden_out, out_sems.at[0]),
        pltpu.make_async_copy(gz, gz_out, out_sems.at[1]),
        pltpu.make_async_copy(scale1, scale_out, out_sems.at[2]),
        pltpu.make_async_copy(q, q_out, out_sems.at[3]),
        pltpu.make_async_copy(k, k_out, out_sems.at[4]),
    ]
    for copy in results[:3]:
        copy.start()
    loads[2].wait()
    loads[3].wait()

    def project(i, carry):
        m = (slot // 2 + 1 + i) % 4
        cut = lanes(m * 256, 256)
        uk = dot(hidden[...], w[1, :, cut], 1, 0)
        uv = dot(hidden[...], w[2, :, cut], 1, 0).astype(BF)
        uq = dot(hidden[...], w[0, :, cut], 1, 0)
        um = dot(gz[...], wo[rows_of(m * 256, 256), :], 1, 1).astype(BF)
        k[:, cut] = uk
        q[:, cut] = uq
        for a in range(2):
            part = slice(a * HD, (a + 1) * HD)
            out[2 * m + a, 0] = normed(uq[:, part])
            out[2 * m + a, 1] = normed(uk[:, part])
            out[2 * m + a, 2] = uv[:, part]
            out[2 * m + a, 3] = um[:, part]
        return carry

    def send_own(h, i):
        remote(out.at[h], own.at[slot], own_sems, peer(h), 1 + i).start()

    def send_pair(i):
        m = (slot // 2 + 1 + i) % 4
        send_own(2 * m, i)
        send_own(2 * m + 1, i)

    project(0, 0)
    send_pair(0)
    for copy in mine:
        copy.wait()
    wait_bytes(ckv.at[pl.ds(0, 7)], kv_sems.at[1])
    half = (pl.ds(0, 2), pl.ds(2, 2))

    def along_x(n):
        cut = half[(0, 1, 1, 0, 0, 1)[n]]
        whose = x if n < 4 else (x + (3 if n == 4 else 1)) % 4
        step = (1, 1, 3, 3, 1, 3)[n]
        return remote(kv.at[cut, whose], kv.at[cut, whose], x_sems.at[n], beside(step))

    for n in (0, 2, 1, 3):
        along_x(n).start()

    def project_send(i, carry):
        project(i, carry)
        send_pair(i)
        return carry

    lax.fori_loop(1, 3, project_send, 0)
    project(3, 0)
    sibling = slot + 1 - 2 * zh
    send_own(sibling, 3)
    last = pltpu.make_async_copy(out.at[slot], own.at[slot], local_sems.at[2])
    last.start()
    for copy in results[3:]:
        copy.start()
    last.wait()
    for n in (0, 2):
        along_x(n).wait_recv()
        along_x(4 + n // 2).start()
    wait_bytes(stretch.at[pl.ds(0, 7)], start_sems.at[1])
    for n in (1, 3, 4, 5):
        along_x(n).wait_recv()

    scale = temps[slot] * (1.0 / math.sqrt(HD))
    c2 = scale * LOG2E
    h = HD
    pair = (0, 1)

    def keys(c, part):
        return kv[c, :, :, part].reshape(8 * h, h)

    def both(left, right, left_dim, right_dim):
        return jnp.concatenate(
            [
                dot(left[:h], right[:h], left_dim, right_dim),
                dot(left[h:], right[h:], left_dim, right_dim),
            ],
            0,
        )

    def attend(row):
        at = [row * 2 + n for n in pair]
        g = [row * 8 + x * 2 + n for n in pair]
        st = [stretch[i, 0:1, :] for i in at]
        qs = [own[i, 0] for i in at]
        ks = [own[i, 1] for i in at]
        vs = [own[i, 2] for i in at]
        ds = [own[i, 3] for i in at]
        s_own = [both(qs[n], ks[n], 1, 1) for n in pair]
        top = list(s_own)
        for c in range(row + 1):
            for n in pair:
                s = dot(qs[n], keys(c, 0), 1, 1)
                for b in range(8):
                    f = c * 8 + b
                    seen = (st[n] <= f) & (f < g[n])
                    sb = s[:, b * h : (b + 1) * h] + jnp.where(seen, 0.0, NEG)
                    s_scr[n, c, :, b * h : (b + 1) * h] = sb
                    top[n] = jnp.maximum(top[n], sb)
        m2 = [jnp.max(top[n], axis=1, keepdims=True) * c2 for n in pair]
        p_own = [jnp.exp2(s_own[n] * c2 - m2[n]) for n in pair]
        acc = [both(p_own[n].astype(BF), vs[n], 1, 0) for n in pair]
        total = list(p_own)
        for c in range(row + 1):
            for n in pair:
                p = jnp.exp2(s_scr[n, c] * c2 - m2[n])
                s_scr[n, c] = p
                for b in range(8):
                    total[n] = total[n] + p[:, b * h : (b + 1) * h]
                acc[n] = acc[n] + dot(p.astype(BF), keys(c, 1), 1, 0)
        inv = [1.0 / jnp.sum(total[n], axis=1, keepdims=True) for n in pair]
        mixed = [acc[n] * inv[n] for n in pair]
        delta = [jnp.sum(mixed[n] * ds[n].astype(F32), axis=1, keepdims=True) for n in pair]
        ds_own = [p_own[n] * (both(ds[n], vs[n], 1, 1) - delta[n]) for n in pair]
        dq = [both(ds_own[n].astype(BF), ks[n], 1, 0) for n in pair]
        for c in range(row + 1):
            for n in pair:
                pull = s_scr[n, c] * (dot(ds[n], keys(c, 1), 1, 1) - delta[n])
                dq[n] = dq[n] + dot(pull.astype(BF), keys(c, 0), 1, 0)
        for n in pair:
            i = at[n]
            res[i, 0] = mixed[n].astype(BF)
            res[i, 1] = (dq[n] * (inv[n] * scale)).astype(BF)
            dsn = (ds_own[n] * (inv[n] * scale)).astype(BF)
            pn = (p_own[n] * inv[n]).astype(BF)
            for j in range(2):
                cut = slice(j * h, (j + 1) * h)
                res[i, 2, cut] = dot(dsn[cut], qs[n][cut], 0, 0).astype(BF)
                res[i, 3, cut] = dot(pn[cut], ds[n][cut], 0, 0).astype(BF)

    def send_back(i):
        remote(res.at[i], got.at[slot], back_sems, peer(i)).start()

    def attend_row(s, carry):
        row = jnp.where(s < 3, s + jnp.where(s >= y, 1, 0), y)
        came = 1 + (y + 3 - row) % 4

        @pl.when(s < 3)
        def _():
            wait_bytes(own.at[pl.ds(0, 2)], own_sems.at[came])

        @pl.when(s == 3)
        def _():
            wait_bytes(own.at[0], own_sems.at[4])

        for r in range(4):

            @pl.when(row == r)
            def _():
                attend(r)

        @pl.when(s < 3)
        def _():
            send_back(2 * row)
            send_back(2 * row + 1)

        return carry

    lax.fori_loop(0, 4, attend_row, 0)
    send_back(sibling)
    keep = pltpu.make_async_copy(res.at[slot], got.at[slot], local_sems.at[2])
    keep.start()
    keep.wait()
    wait_bytes(stretch.at[pl.ds(0, 7)], start_sems.at[0])
    for n in range(6):
        along_x(n).wait_send()
    for copy in swaps + results:
        copy.wait()
    wait_bytes(own.at[pl.ds(0, 7)], own_sems.at[0])
    wait_bytes(ckv.at[pl.ds(0, 7)], kv_sems.at[0])
    for way in (0, 1):
        wait_bytes(res.at[pl.ds(0, 7)], back_sems.at[way])


def open_up(level, action, start, noisy, clean, grad, noise, acts, w3, w_out, temps):
    rows, model = noisy.shape
    tokens = clean.shape[0]
    width = w_out.shape[0]
    smem = pl.BlockSpec(memory_space=pltpu.SMEM)
    return pl.pallas_call(
        open_kernel,
        out_shape=(
            jax.ShapeDtypeStruct((8, 4, rows, HD), BF),
            jax.ShapeDtypeStruct((rows, model), BF),
            jax.ShapeDtypeStruct((rows, model), BF),
            jax.ShapeDtypeStruct((rows, width), F32),
            jax.ShapeDtypeStruct((rows, width), F32),
            jax.ShapeDtypeStruct((2, model), F32),
            jax.ShapeDtypeStruct((rows, model), BF),
            jax.ShapeDtypeStruct((rows, model // 2), BF),
        ),
        in_specs=[smem] * 3 + [ANY] * 7 + [smem],
        out_specs=(ANY,) * 8,
        scratch_shapes=[
            pltpu.VMEM(noisy.shape, BF),
            pltpu.VMEM(clean.shape, BF),
            pltpu.VMEM(grad.shape, BF),
            pltpu.VMEM(noise.shape, F32),
            pltpu.VMEM(acts.shape, F32),
            pltpu.VMEM((rows, model), BF),
            pltpu.VMEM((rows, model), BF),
            pltpu.VMEM((rows, width), F32),
            pltpu.VMEM((rows, width), F32),
            pltpu.VMEM((2, model), F32),
            pltpu.VMEM((4, 4, 2, 2, tokens, HD), BF),
            pltpu.VMEM((8, 4, rows, HD), BF),
            pltpu.VMEM((8, 8, 128), jnp.int32),
            pltpu.VMEM((tokens, model), BF),
            pltpu.VMEM((8, 2, tokens, HD), BF),
            pltpu.VMEM((8, 4, rows, HD), BF),
            pltpu.VMEM((8, 128), jnp.int32),
            pltpu.VMEM(w3.shape, BF),
            pltpu.VMEM(w_out.shape, BF),
            pltpu.VMEM((2, 4, rows, 8 * HD), F32),
            pltpu.VMEM((8, 4, rows, HD), BF),
            pltpu.SemaphoreType.DMA((4,)),
            pltpu.SemaphoreType.DMA((2,)),
            pltpu.SemaphoreType.DMA((6, 2)),
            pltpu.SemaphoreType.DMA((5,)),
            pltpu.SemaphoreType.DMA((2,)),
            pltpu.SemaphoreType.DMA((3,)),
            pltpu.SemaphoreType.DMA((2,)),
            pltpu.SemaphoreType.DMA((3, 2)),
            pltpu.SemaphoreType.DMA((5,)),
            pltpu.SemaphoreType.DMA((5,)),
        ],
        compiler_params=pltpu.CompilerParams(
            collective_id=0, has_side_effects=True, vmem_limit_bytes=60 * 1024 * 1024
        ),
        name="open",
    )(level, action, start, noisy, clean, grad, noise, acts, w3, w_out, temps)


ORDERS = (("x", "y", "z"), ("y", "z", "x"), ("z", "x", "y"))
UNITS = (11, 11, 10)
FIRST_UNIT = (0, 11, 22)


def stream_of(unit):
    k = unit // 11
    return k, unit - FIRST_UNIT[k]


def close_kernel(
    got_all, q_all, k_all, hidden_all, gz_all, ph_all, pz_all, scale_all, noisy_all, grad_all, w3,
    all_n, out_g, out_o,
    out_n, got, q, k, hidden, gz, ph, pz, scale1, noisy, grad, proj, pm, pp, w, gh,
    t0a, t0b, t0c, t1a, t1b, t1c, t2a, t2b, t2c, b0a, b0b, b0c, b1a, b1b, b1c, b2a, b2b, b2c,
    swap_sems, w_sem, ring_sems, last_sems,
):
    t = lax.axis_index("tm")
    d = lax.axis_index("dp")
    y, x, zh = place(t)
    zl, core = d // 2, d % 2
    z = zh * 2 + zl
    partner = {"dp": d + 1 - 2 * core, "tm": t}
    at = {"x": x, "y": y, "z": z}
    rows = hidden.shape[0]
    terms = ((t0a, t0b, t0c), (t1a, t1b, t1c), (t2a, t2b, t2c))
    boxes = ((b0a, b0b, b0c), (b1a, b1b, b1c), (b2a, b2b, b2c))

    def along(axis, step):
        c = dict(at)
        c[axis] = (c[axis] + step) % 4
        return {
            "dp": (c["z"] % 2) * 2 + core,
            "tm": (c["y"] * 4 + c["x"]) * 2 + c["z"] // 2,
        }

    sources = (
        got_all, q_all, k_all, hidden_all, gz_all, ph_all, pz_all, scale_all, noisy_all, grad_all, w3,
    )
    places = (got, q, k, hidden, gz, ph, pz, scale1, noisy, grad, w)
    loads = [
        pltpu.make_async_copy(source, spot, w_sem.at[n])
        for n, (source, spot) in enumerate(zip(sources, places, strict=True))
    ]
    for load in loads:
        load.start()
    barrier = pltpu.get_barrier_semaphore()

    for axis in "xyz":
        for step in (1, 2, 3):
            pl.semaphore_signal(
                barrier, inc=1, device_id=along(axis, step), device_id_type=MESH
            )
    pl.semaphore_signal(barrier, inc=1, device_id=partner, device_id_type=MESH)
    def remote(src, dst, send_sem, recv_sem, device):
        return pltpu.make_async_remote_copy(
            src_ref=src,
            dst_ref=dst,
            send_sem=send_sem,
            recv_sem=recv_sem,
            device_id=device,
            device_id_type=MESH,
        )

    def swap(src, dst, part):
        copy = remote(src, dst, swap_sems.at[0, part], swap_sems.at[1, part], partner)
        copy.start()
        return copy

    def norm_back(h, carry):
        for part, u_ref in ((0, q), (1, k)):
            u = u_ref[:, lanes(h * HD, HD)]
            factor = lax.rsqrt(jnp.mean(u * u, axis=1, keepdims=True) + EPS)
            hat = u * factor
            g = got[h, 1 + part].astype(F32)
            du = factor * (g - hat * jnp.mean(hat * g, axis=1, keepdims=True))
            proj[:, lanes(part * 1024 + h * HD, HD)] = du.astype(BF)
        proj[:, lanes(2048 + h * HD, HD)] = got[h, 3]
        return carry

    for load in loads[:3]:
        load.wait()
    other = 1 - core
    swaps = []
    for l in range(2):
        lax.fori_loop(0, 2, lambda i, c: norm_back(l * 4 + other * 2 + i, c), 0)
        if l == 0:
            pl.semaphore_wait(barrier, 10)
            swaps.append(swap(got.at[:, 0], pm, 0))
        for j in range(3):
            swaps.append(
                swap(
                    proj.at[:, lanes(j * 1024 + l * 512 + other * 256, 256)],
                    pp.at[:, pl.ds(l * 768 + j * 256, 256)],
                    1 + l * 3 + j,
                )
            )
    for l in range(2):
        lax.fori_loop(0, 2, lambda i, c: norm_back(l * 4 + core * 2 + i, c), 0)
    for load in loads[3:7]:
        load.wait()
    for copy in swaps:
        copy.wait_recv()

    def put(yb, xb, zb, unit, value):
        s, u = stream_of(unit)
        spot = {"x": xb, "y": yb, "z": zb}
        terms[0][s][spot[ORDERS[s][0]], spot[ORDERS[s][1]], spot[ORDERS[s][2]], u] = value

    def terms_of(n, carry):
        yb = ((y // 2 + 1 + n // 2) % 2) * 2 + (y + n % 2 + n // 2) % 2
        cut = lanes(yb * 512, 512)
        left = jnp.concatenate([hidden[:, cut], ph[:, cut]], 0).T
        for l in range(2):
            for j in range(3):
                mine = proj[:, lanes(j * 1024 + l * 512 + core * 256, 256)]
                theirs = pp[:, l * 768 + j * 256 : l * 768 + (j + 1) * 256]
                right = jnp.concatenate([mine, theirs], 0)
                term = dot(left, right, 1, 0).astype(BF)
                for xb in range(4):
                    for hb in range(2):
                        for rg in range(4):
                            r = (xb * 2 + hb) * 64 + rg * 16
                            for ch in range(2):
                                put(
                                    yb, xb, hb * 2 + l, (j * 4 + rg) * 2 + ch,
                                    term[r : r + 16, ch * 128 : (ch + 1) * 128],
                                )
        left = jnp.concatenate(
            [
                jnp.concatenate([got[2 * yb, 0], got[2 * yb + 1, 0]], 1),
                jnp.concatenate([pm[2 * yb], pm[2 * yb + 1]], 1),
            ],
            0,
        ).T
        for l in range(2):
            mine = gz[:, lanes(l * 1024 + core * 512, 512)]
            right = jnp.concatenate([mine, pz[:, l * 512 : (l + 1) * 512]], 0)
            term = dot(left, right, 1, 0).astype(BF)
            for xb in range(4):
                for hb in range(2):
                    for rg in range(2):
                        for ch in range(4):
                            r = (xb * 2 + hb) * 32 + rg * 16
                            put(
                                yb, xb, hb * 2 + l, 24 + rg * 4 + ch,
                                term[r : r + 16, ch * 128 : (ch + 1) * 128],
                            )

        @pl.when(n == 0)
        def _():
            ring(1, 0, 0, 0).start()
            ring(1, 0, 1, 0).start()

        @pl.when(n == 1)
        def _():
            for s in (0, 2):
                ring(s, 0, 0, 0).start()
                ring(s, 0, 1, 1).start()

        @pl.when((n == 1) & (y % 2 == 0) | (n == 2) & (y % 2 == 1))
        def _():
            ring(1, 0, 1, 1).start()

        @pl.when((n == 1) & (y % 2 == 1) | (n == 2) & (y % 2 == 0))
        def _():
            ring(1, 0, 0, 1).start()

        @pl.when(n == 3)
        def _():
            for s in (0, 2):
                ring(s, 0, 1, 0).start()
                ring(s, 0, 0, 1).start()

        return carry

    far_pair, near_pair = pl.ds((1 - y // 2) * 2, 2), pl.ds((y // 2) * 2, 2)

    def half(s, level, way):
        if level == 1 or s == 1:
            return (pl.ds(2 * way, 2),)
        cut = near_pair if way else far_pair
        return (cut,) if s == 0 else (slice(None), cut)

    def ring(s, level, way, part):
        axis = ORDERS[s][level]
        step = 1 if way == 0 else 3
        near, far = (at[axis] + step) % 4, (at[axis] + 2) % 4
        src = (
            terms[level][s].at[(far, *half(s, level, way))],
            terms[level][s].at[(near, *half(s, level, 1 - way))],
            terms[level][s].at[(near, *half(s, level, way))],
        )[part]
        sems = ring_sems.at[s, level, way, part]
        return remote(
            src, boxes[level][s].at[way, part], sems.at[0], sems.at[1], along(axis, step)
        )

    def ring_open(level, s):
        for part in range(2):
            for way in range(2):
                ring(s, level, way, part).start()

    def ring_middle(level, s):
        axis = ORDERS[s][level]
        for way in range(2):
            ring(s, level, way, 0).wait_recv()
            near = (at[axis] + (1 if way == 0 else 3)) % 4
            spot = terms[level][s].at[(near, *half(s, level, way))]
            spot[...] = (
                spot[...].astype(F32) + boxes[level][s][way, 0].astype(F32)
            ).astype(BF)
            ring(s, level, way, 2).start()

    def ring_close(level, s):
        for way in range(2):
            ring(s, level, way, 1).wait_recv()
            ring(s, level, way, 2).wait_recv()
        mine = at[ORDERS[s][level]]
        box = boxes[level][s]
        for way in range(2):
            cut = half(s, level, way)
            terms[level + 1][s][cut] = (
                terms[level][s][(mine, *cut)].astype(F32)
                + box[way, 2].astype(F32)
                + box[1 - way, 1].astype(F32)
            ).astype(BF)

    lax.fori_loop(0, 4, terms_of, 0)
    for load in loads[7:]:
        load.wait()

    def pull_hidden(n, carry):
        cut = lanes(n * 512, 512)
        total = dot(proj[:, :1024], w[0, cut, :], 1, 1)
        total = total + dot(proj[:, 1024:2048], w[1, cut, :], 1, 1)
        total = total + dot(proj[:, 2048:], w[2, cut, :], 1, 1)
        gh[:, cut] = total.astype(BF)
        return carry

    lax.fori_loop(0, 4, pull_hidden, 0)
    for s in range(3):
        ring_middle(0, s)

    def norm_rows(n, carry):
        cut = rows_of(n * 16, 16)
        level = n // 8
        v = noisy[cut, :].astype(F32)
        center = v - jnp.mean(v, axis=1, keepdims=True)
        factor = lax.rsqrt(jnp.mean(center * center, axis=1, keepdims=True) + EPS)
        hat = center * factor
        g = gh[cut, :].astype(F32) * scale1[pl.ds(level, 1), :]
        dv = factor * (
            g
            - jnp.mean(g, axis=1, keepdims=True)
            - hat * jnp.mean(g * hat, axis=1, keepdims=True)
        )
        out_n[cut, :] = (dv + grad[cut, :].astype(F32)).astype(BF)
        return carry

    lax.fori_loop(0, rows // 16, norm_rows, 0)
    leave = pltpu.make_async_copy(out_n, all_n, w_sem.at[11])
    leave.start()

    for s in range(3):
        ring_close(0, s)
        ring_open(1, s)
    for s in range(3):
        ring_middle(1, s)

    def last(s, step):
        axis = ORDERS[s][2]
        there = (at[axis] + step) % 4
        sems = last_sems.at[s, step - 1]
        return remote(
            terms[2][s].at[there], boxes[2][s].at[step - 1], sems.at[0], sems.at[1],
            along(axis, step),
        )

    for s in range(3):
        ring_close(1, s)
        for step in (1, 2, 3):
            last(s, step).start()
    for s in range(3):
        for step in (1, 2, 3):
            last(s, step).wait_recv()
        mine = at[ORDERS[s][2]]
        sums = terms[2][s][mine].astype(F32)
        for step in (1, 2, 3):
            sums = sums + boxes[2][s][step - 1].astype(F32)
        sums = sums.astype(BF)
        for u in range(UNITS[s]):
            unit = FIRST_UNIT[s] + u
            if unit < 24:
                j, rg, ch = unit // 8, (unit // 2) % 4, unit % 2
                out_g[j, rg * 16 : (rg + 1) * 16, ch * 128 : (ch + 1) * 128] = sums[u]
            else:
                rg, ch = (unit - 24) // 4, unit % 4
                out_o[rg * 16 : (rg + 1) * 16, ch * 128 : (ch + 1) * 128] = sums[u]

    leave.wait()
    for copy in swaps:
        copy.wait_send()
    for s in range(3):
        for level in range(2):
            for way in range(2):
                for part in range(3):
                    ring(s, level, way, part).wait_send()
        for step in (1, 2, 3):
            last(s, step).wait_send()


def close(got, q, k, hidden, gz, ph, pz, scale1, noisy, grad, w3):
    rows, model = hidden.shape
    vmem = pl.BlockSpec(memory_space=pltpu.VMEM)

    def box(*shape):
        return [pltpu.VMEM(shape + (u, 16, 128), BF) for u in UNITS]

    return pl.pallas_call(
        close_kernel,
        out_shape=(
            jax.ShapeDtypeStruct((rows, model), BF),
            jax.ShapeDtypeStruct((3, 64, 256), BF),
            jax.ShapeDtypeStruct((32, 512), BF),
        ),
        in_specs=[ANY] * 11,
        out_specs=(ANY, vmem, vmem),
        scratch_shapes=[
            pltpu.VMEM((rows, model), BF),
            *[
                pltpu.VMEM(array.shape, array.dtype)
                for array in (got, q, k, hidden, gz, ph, pz, scale1, noisy, grad)
            ],
            pltpu.VMEM((rows, 3072), BF),
            pltpu.VMEM((8, rows, HD), BF),
            pltpu.VMEM((rows, 1536), BF),
            pltpu.VMEM(w3.shape, BF),
            pltpu.VMEM((rows, model), BF),
            *box(4, 4, 4),
            *box(4, 4),
            *box(4),
            *box(2, 3, 2, 4)[:2],
            box(2, 3, 4, 2)[2],
            *box(2, 3, 2),
            *box(3),
            pltpu.SemaphoreType.DMA((2, 7)),
            pltpu.SemaphoreType.DMA((12,)),
            pltpu.SemaphoreType.DMA((3, 2, 2, 3, 2)),
            pltpu.SemaphoreType.DMA((3, 3, 2)),
        ],
        compiler_params=pltpu.CompilerParams(
            collective_id=1, has_side_effects=True, vmem_limit_bytes=62 * 1024 * 1024
        ),
        name="close",
    )(got, q, k, hidden, gz, ph, pz, scale1, noisy, grad, w3)


def finish_kernel(*refs):
    sources, targets, places, sems = refs[:3], refs[3:6], refs[6:9], refs[9]
    inward = [pltpu.make_async_copy(sources[n], places[n], sems.at[0, n]) for n in range(3)]
    outward = [pltpu.make_async_copy(places[n], targets[n], sems.at[1, n]) for n in range(3)]
    for copy in inward:
        copy.start()
    for n in range(3):
        inward[n].wait()
        outward[n].start()
    for copy in outward:
        copy.wait()


def finish(*arrays):
    return pl.pallas_call(
        finish_kernel,
        out_shape=tuple(jax.ShapeDtypeStruct(array.shape, array.dtype) for array in arrays),
        in_specs=[ANY] * 3,
        out_specs=(ANY,) * 3,
        scratch_shapes=[
            *[pltpu.VMEM(array.shape, array.dtype) for array in arrays],
            pltpu.SemaphoreType.DMA((2, 3)),
        ],
        compiler_params=pltpu.CompilerParams(vmem_limit_bytes=62 * 1024 * 1024),
        name="finish",
    )(*arrays)


def on_device(
    noisy, clean, actions, levels, starts, w_qkv, w_out, noise_table, action_table, temps, out_grad
):
    tokens, model = noisy.shape[3:]
    rows = 2 * tokens
    w3 = w_qkv.transpose(1, 0, 2)
    noisy_rows = noisy.reshape(rows, model)
    grad_rows = out_grad.reshape(rows, model)
    got, hidden, grad_z, q, k, scale1, ph, pz = open_up(
        levels.reshape(2),
        actions.reshape(1),
        starts.reshape(1),
        noisy_rows,
        clean.reshape(tokens, model),
        grad_rows,
        noise_table.transpose(1, 0, 2),
        action_table,
        w3,
        w_out,
        temps,
    )
    grad_noisy, total_g, total_o = finish(
        *close(got, q, k, hidden, grad_z, ph, pz, scale1, noisy_rows, grad_rows, w3)
    )
    return (grad_noisy.reshape(noisy.shape), total_g.transpose(1, 0, 2), total_o)


def solution(mesh):
    in_specs = (
        P("dp", "tm", None, None, None),
        P("dp", "tm", None, None),
        P("dp", "tm"),
        P("dp", "tm", None),
        P("dp", "tm"),
        P(),
        P(),
        P(),
        P(),
        P(),
        P("dp", "tm", None, None, None),
    )
    out_specs = (P("dp", "tm", None, None, None), P("tm", None, "dp"), P("tm", "dp"))
    return jax.shard_map(
        on_device, mesh=mesh, in_specs=in_specs, out_specs=out_specs, check_vma=False
    )
```
